256 devices in a mesh: dp: 32 (over y_lo, z, core), tensor: 8 (over y_hi, x).
Axes of the slice: x: 4, y: 4 (y_hi: 2, y_lo: 2; y = y_hi * 2 + y_lo), z: 8, core: 2. Of those that a mesh axis runs over, the one named last changes fastest.
Arguments:
- image_features: bfloat16 [8192, 1408], P('dp', 'tensor'), may hold values from -6 to 6
- text_features: bfloat16 [8192, 1152], P('dp', 'tensor'), may hold values from -6 to 6
- image_weight: bfloat16 [1408, 1152], P('tensor'), may hold values from -0.15625 to 0.15625
- text_weight: bfloat16 [1152, 1152], P('tensor'), may hold values from -0.1875 to 0.1875
- image_pair: int32 [8192], P('dp'), may hold values from 0 to 8191, each once
- temp_index: int32 [], replicated, may hold values from 0 to 8
- bias_index: int32 [], replicated, may hold values from 2 to 7
Outputs:
- grad_image_weight: float32 [1408, 1152], P('tensor', 'dp')
- grad_text_weight: float32 [1152, 1152], P('tensor', 'dp')
The draws below stay inside these ranges and needn't reach their ends.
Inputs may be any that keep to these rules, and one draw needn't show every extreme that they name: image_pair holds each text row index exactly once.
All inputs are finite; a program needn't handle non-finite values.
Results may differ from the reference program's by a relative error of at most 0.0034.
Values may be sent and summed in bfloat16 or wider, within the bound.
A program may use at most 64 MiB of HBM per device.

```python
import jax
import jax.numpy as jnp
from jax import lax

DI = 1408
DT = 1152
E = 1152
TOKENS = 8192


def levels(stream_key, shape, shards, least, top_value):
    gain, own = 1.0, jax.random.fold_in(stream_key, 6)
    for dim, blocks in shards:
        draws = jnp.exp(jax.random.uniform(jax.random.fold_in(own, dim), (blocks,), jnp.float32, least / len(shards), top_value / len(shards)))
        gain = gain * jnp.repeat(draws, shape[dim] // blocks).reshape([-1 if axis == dim else 1 for axis in range(len(shape))])
    return gain


def centred(key, dims, spread, bound, split=(), kind=jnp.bfloat16):
    level = levels(key, dims, split, -0.22, 0.18) if split else 1.0
    entries = jax.random.normal(key, dims, jnp.float32) * spread * level
    return jnp.minimum(jnp.maximum(entries, -bound), bound).astype(kind)


def setup_inputs(seed: int = 0) -> dict:
    key_of = jax.random.split(jax.random.key(seed), 8)
    return {
        "image_features": centred(key_of[0], (TOKENS, DI), 1.0, 6.0, ((0, 32), (1, 8))),
        "text_features": centred(key_of[1], (TOKENS, DT), 1.0, 6.0, ((0, 32), (1, 8))),
        "image_weight": centred(key_of[2], (DI, E), DI ** -0.5, 0.15625, ((0, 8),)),
        "text_weight": centred(key_of[3], (DT, E), DT ** -0.5, 0.1875, ((0, 8),)),
        "image_pair": jax.random.permutation(key_of[4], TOKENS).astype(jnp.int32),
        "temp_index": jax.random.randint(key_of[5], (), 0, 9).astype(jnp.int32),
        "bias_index": jax.random.randint(key_of[6], (), 2, 8).astype(jnp.int32),
    }


def unit_rows(values):
    norm = jnp.sqrt(lax.optimization_barrier(jnp.sum(values * values, axis=1, keepdims=True)) + 1e-06)
    direct = values / norm
    return (norm, direct)

def back_rows(direct, norm, grad):
    inner = lax.optimization_barrier(jnp.sum(direct * grad, axis=1, keepdims=True))
    return ((grad - direct * inner) / norm).astype(jnp.bfloat16)

def reference(image_features, text_features, image_weight, text_weight, image_pair, temp_index, bias_index):
    scale = 4.0 + temp_index.astype(jnp.float32)
    shift = -0.5 * bias_index.astype(jnp.float32)
    img = jnp.dot(image_features, image_weight, preferred_element_type=jnp.float32)
    txt = jnp.dot(text_features, text_weight, preferred_element_type=jnp.float32)
    img_norm, img_dir = unit_rows(img)
    txt_norm, txt_dir = unit_rows(txt)
    img_unit = img_dir.astype(jnp.bfloat16)
    txt_unit = txt_dir.astype(jnp.bfloat16)
    block = 512 if TOKENS % 512 == 0 else TOKENS
    count = TOKENS // block
    columns = jnp.arange(TOKENS, dtype=jnp.int32)

    def step(carry, inputs):
        rows_unit, targets = inputs
        logits = scale * jnp.dot(rows_unit, txt_unit.T, preferred_element_type=jnp.float32) + shift
        sign = jnp.where(columns[None, :] == targets[:, None], jnp.float32(1.0), jnp.float32(-1.0))
        weights = (-scale * sign * jax.nn.sigmoid(-sign * logits)).astype(jnp.bfloat16)
        img_part = jnp.dot(weights, txt_unit, preferred_element_type=jnp.float32)
        carry = carry + lax.dot_general(weights, rows_unit, (((0,), (0,)), ((), ())), preferred_element_type=jnp.float32)
        return (carry, img_part)
    txt_grad_unit, img_grad_unit = lax.scan(step, jnp.zeros((TOKENS, E), jnp.float32), (img_unit.reshape(count, block, E), image_pair.astype(jnp.int32).reshape(count, block)))
    img_grad_unit = img_grad_unit.reshape(TOKENS, E)
    img_grad = back_rows(img_dir, img_norm, img_grad_unit)
    txt_grad = back_rows(txt_dir, txt_norm, txt_grad_unit)
    contract = (((0,), (0,)), ((), ()))
    grad_image_weight = lax.dot_general(image_features, img_grad, contract, preferred_element_type=jnp.float32)
    grad_text_weight = lax.dot_general(text_features, txt_grad, contract, preferred_element_type=jnp.float32)
    return (grad_image_weight, grad_text_weight)
```

```python
import functools

import jax
import jax.numpy as jnp
from jax import lax
from jax.experimental import pallas as pl
from jax.experimental.pallas import tpu as pltpu
from jax.sharding import PartitionSpec as P

MESH = pl.DeviceIdType.MESH
E = 1152
DI = 176
DT = 144
R = 32
TS = 8
ZS = 8
PS = 16
OUT = 36
OUT_ROWS = 48
OUT_LANES = 384
LEVELS = 32000.0
WIRE = E + 128
f32 = jnp.float32
bf16 = jnp.bfloat16


def encode(x, wire, k):
    m = jnp.max(jnp.abs(x), axis=1, keepdims=True)
    hi = jnp.floor(m)
    lo = jnp.floor((m - hi) * LEVELS) + 1.0
    top = hi + lo * (1.0 / LEVELS)
    wire[k, :, 0:E] = jnp.round(x * (LEVELS / top)).astype(jnp.int32).astype(jnp.int16)
    lane = lax.broadcasted_iota(jnp.int32, (R, 128), 1)
    wire[k, :, E:WIRE] = jnp.where(lane < 64, hi, lo).astype(jnp.int32).astype(jnp.int16)


def decode(wire, k):
    code = wire[k, :, E:WIRE].astype(jnp.int32).astype(f32)
    lane = lax.broadcasted_iota(jnp.int32, (R, 128), 1)
    top = jnp.sum(jnp.where(lane < 64, code, code * (1.0 / LEVELS)), axis=1, keepdims=True) * (1.0 / 64)
    return wire[k, :, 0:E].astype(jnp.int32).astype(f32) * (top * (1.0 / LEVELS))


def unit_rows(values):
    norm = jnp.sqrt(jnp.sum(values * values, axis=1, keepdims=True) + 1e-06)
    return norm, values / norm


def back_rows(direct, norm, grad):
    inner = jnp.sum(direct * grad, axis=1, keepdims=True)
    return ((grad - direct * inner) / norm).astype(bf16)


def kernel(
    temp_ref, bias_ref, pair_ref, fi_ref, ft_ref, wi_ref, wt_ref, out_ref,
    part_i, part_t, a_i_out, a_i_in, a_t_out, a_t_in,
    dir_i, dir_t, norm_i, norm_t, all_i, all_t, pair_out, pair_in,
    w_ref, gi, gt, gt_sib, gt_own, c_i_out, c_i_in, c_t_out, c_t_in,
    grad_i, grad_t, g_ref, g_sib, e_own, e_out, e_in,
    a_i_ss, a_i_rs, a_t_ss, a_t_rs, b_i_ss, b_i_rs, b_t_ss, b_t_rs, relay_ss, relay_rs,
    c_i_ss, c_i_rs, c_t_ss, c_t_rs, d_i_ss, d_i_rs, d_t_ss, d_t_rs, e_ss, e_rs, one_ss, one_rs,
):
    dp = lax.axis_index("dp")
    t = lax.axis_index("tensor")
    ylo = lax.div(dp, 16)
    z = lax.rem(lax.div(dp, 2), 8)
    c = lax.rem(dp, 2)
    oc = 1 - c
    p = ylo * TS + t
    q = ylo * ZS + z

    def device(ylo_, z_, c_, t_):
        return ((ylo_ * ZS + z_) * 2 + c_, t_)

    sibling = device(ylo, z, oc, t)
    across = device(1 - ylo, z, c, t)

    def plane(k):
        return device(lax.div(k, TS), z, c, lax.rem(k, TS))

    def column(k):
        return device(lax.div(k, ZS), lax.rem(k, ZS), c, t)

    def copy(src, dst, ssem, rsem, dev):
        return pltpu.make_async_remote_copy(
            src_ref=src, dst_ref=dst, send_sem=ssem, recv_sem=rsem, device_id=dev, device_id_type=MESH
        )

    barrier = pltpu.get_barrier_semaphore()

    def greet_plane(k, _):
        pl.semaphore_signal(barrier, inc=1, device_id=plane(lax.rem(p + k, PS)), device_id_type=MESH)
        return 0

    def greet_column(k, _):
        zz = lax.rem(z + k, ZS)
        pl.semaphore_signal(barrier, inc=1, device_id=device(ylo, zz, c, t), device_id_type=MESH)
        pl.semaphore_signal(barrier, inc=1, device_id=device(1 - ylo, zz, c, t), device_id_type=MESH)
        return 0

    lax.fori_loop(1, PS, greet_plane, 0)
    lax.fori_loop(1, ZS, greet_column, 0)
    pl.semaphore_signal(barrier, inc=1, device_id=sibling, device_id_type=MESH)

    part_t[...] = jnp.dot(ft_ref[...], wt_ref[...], preferred_element_type=f32).reshape(TS, R, E)
    pair_out[...] = jnp.broadcast_to(pair_ref[...], (8, 256))
    g_ref[...] = jnp.zeros_like(g_ref)
    pl.semaphore_wait(barrier, (PS - 1) + 2 * (ZS - 1) + 1)
    pair_copy = copy(pair_out, pair_in, one_ss.at[0], one_rs.at[0], across)
    pair_copy.start()

    def a_copy(wire_out, wire_in, ss, rs, k, slot):
        return copy(wire_out.at[k], wire_in.at[slot], ss.at[k], rs.at[slot], (dp, k))

    def a_send(part, wire_out, wire_in, ss, rs):
        def step(j, _):
            k = lax.rem(t + j, TS)
            encode(part[k], wire_out, k)
            a_copy(wire_out, wire_in, ss, rs, k, t).start()
            return 0
        lax.fori_loop(1, TS, step, 0)

    def a_take(part, wire_out, wire_in, ss, rs):
        def step(j, total):
            k = lax.rem(t + j, TS)
            a_copy(wire_out, wire_in, ss, rs, k, k).wait_recv()
            return total + decode(wire_in, k)
        return lax.fori_loop(1, TS, step, part[t])

    a_send(part_t, a_t_out, a_t_in, a_t_ss, a_t_rs)
    part_i[...] = jnp.dot(fi_ref[...], wi_ref[...], preferred_element_type=f32).reshape(TS, R, E)
    a_send(part_i, a_i_out, a_i_in, a_i_ss, a_i_rs)

    def b_t_copy(zz, slot):
        s = c * ZS + slot
        return copy(all_t.at[s], all_t.at[s], b_t_ss.at[zz], b_t_rs.at[slot], device(ylo, zz, c, t))

    def relay(cc, zz):
        s = cc * ZS + zz
        return copy(all_t.at[s], all_t.at[s], relay_ss.at[zz], relay_rs.at[zz], sibling)

    norm, direct = unit_rows(a_take(part_t, a_t_out, a_t_in, a_t_ss, a_t_rs))
    norm_t[...] = norm
    dir_t[...] = direct
    all_t[c * ZS + z] = direct.astype(bf16)

    def b_t_send(j, _):
        b_t_copy(lax.rem(z + j, ZS), z).start()
        return 0

    lax.fori_loop(1, ZS, b_t_send, 0)
    relay(c, z).start()

    def b_i_copy(k, slot):
        return copy(all_i.at[slot], all_i.at[slot], b_i_ss.at[k], b_i_rs.at[slot], plane(k))

    norm, direct = unit_rows(a_take(part_i, a_i_out, a_i_in, a_i_ss, a_i_rs))
    norm_i[...] = norm
    dir_i[...] = direct
    all_i[p] = direct.astype(bf16)

    def b_i_send(j, _):
        b_i_copy(lax.rem(p + j, PS), p).start()
        return 0

    lax.fori_loop(1, PS, b_i_send, 0)

    def b_t_take(j, _):
        zz = lax.rem(z + j, ZS)
        b_t_copy(zz, zz).wait_recv()
        relay(c, zz).start()
        return 0

    lax.fori_loop(1, ZS, b_t_take, 0)

    def b_i_take(j, _):
        k = lax.rem(p + j, PS)
        b_i_copy(k, k).wait_recv()
        return 0

    lax.fori_loop(1, PS, b_i_take, 0)

    def relay_take(zz, _):
        relay(oc, zz).wait_recv()
        return 0

    lax.fori_loop(0, ZS, relay_take, 0)
    pair_copy.wait_recv()

    scale = 4.0 + temp_ref[0].astype(f32)
    shift = -0.5 * bias_ref[0].astype(f32)

    def local_target(pair):
        r = pair & 31
        tt = (pair >> 5) & 7
        cc = (pair >> 8) & 1
        zz = (pair >> 9) & 7
        yy = (pair >> 12) & 1
        here = jnp.logical_and(tt == t, yy == ylo)
        return jnp.where(here, (cc * ZS + zz) * R + r, -1)

    own = local_target(pair_out[0:1, :])
    other = local_target(pair_in[0:1, :])
    first = jnp.where(ylo == 0, own, other)
    second = jnp.where(ylo == 0, other, own)
    target = jnp.concatenate([first, second], axis=1)

    def tile(j, _):
        b = lax.rem(2 * oc + j, 4)
        rows = all_t[pl.ds(b * 4, 4)].reshape(4 * R, E)
        img = all_i[...].reshape(PS * R, E)
        logits = scale * lax.dot_general(rows, img, (((1,), (1,)), ((), ())), preferred_element_type=f32) + shift
        index = lax.broadcasted_iota(jnp.int32, (4 * R, PS * R), 0) + b * (4 * R)
        sign = jnp.where(index == target, f32(1.0), f32(-1.0))
        w = (-scale * sign * jax.nn.sigmoid(-sign * logits)).astype(bf16)
        w_ref[pl.ds(pl.multiple_of(b * (4 * R), 4 * R), 4 * R), :] = w
        gt[pl.ds(b * 4, 4)] = jnp.dot(w, img, preferred_element_type=f32).reshape(4, R, E)
        return 0

    lax.fori_loop(0, 2, tile, 0)
    sib_copy = copy(gt.at[pl.ds(oc * ZS, ZS)], gt_sib, one_ss.at[1], one_rs.at[1], sibling)
    sib_copy.start()
    lax.fori_loop(2, 4, tile, 0)
    sib_copy.wait_recv()

    def c_t_copy(zz, slot):
        return copy(c_t_out.at[zz], c_t_in.at[slot], c_t_ss.at[zz], c_t_rs.at[slot], device(ylo, zz, c, t))

    def c_t_send(j, _):
        zz = lax.rem(z + j, ZS)
        encode(gt[c * ZS + zz] + gt_sib[zz], c_t_out, zz)
        c_t_copy(zz, z).start()
        return 0

    lax.fori_loop(1, ZS, c_t_send, 0)

    def c_i_copy(k, slot):
        return copy(c_i_out.at[k], c_i_in.at[slot], c_i_ss.at[k], c_i_rs.at[slot], plane(k))

    for b in range(4):
        gi[4 * b:4 * b + 4] = lax.dot_general(
            w_ref[:, 4 * R * b:4 * R * (b + 1)], all_t[...].reshape(PS * R, E), (((0,), (0,)), ((), ())),
            preferred_element_type=f32,
        ).reshape(4, R, E)

    def c_i_send(j, _):
        k = lax.rem(p + j, PS)
        encode(gi[k], c_i_out, k)
        c_i_copy(k, p).start()
        return 0

    lax.fori_loop(1, PS, c_i_send, 0)

    def c_i_take(j, total):
        k = lax.rem(p + j, PS)
        c_i_copy(k, k).wait_recv()
        return total + decode(c_i_in, k)

    def c_t_take(j, total):
        zz = lax.rem(z + j, ZS)
        c_t_copy(zz, zz).wait_recv()
        return total + decode(c_t_in, zz)

    def d_copy(grad, ss, rs, k, slot):
        return copy(grad.at[slot], grad.at[slot], ss.at[k], rs.at[slot], (dp, k))

    def d_send(grad, ss, rs):
        def step(j, _):
            d_copy(grad, ss, rs, lax.rem(t + j, TS), t).start()
            return 0
        lax.fori_loop(1, TS, step, 0)

    def d_take(grad, ss, rs):
        def step(j, _):
            k = lax.rem(t + j, TS)
            d_copy(grad, ss, rs, k, k).wait_recv()
            return 0
        lax.fori_loop(1, TS, step, 0)

    total = lax.fori_loop(1, ZS, c_t_take, gt[c * ZS + z] + gt_sib[z])
    grad_t[t] = back_rows(dir_t[...], norm_t[...], total)
    d_send(grad_t, d_t_ss, d_t_rs)
    total = lax.fori_loop(1, PS, c_i_take, gi[p])
    grad_i[t] = back_rows(dir_i[...], norm_i[...], total)
    d_send(grad_i, d_i_ss, d_i_rs)

    def weight_grad(grad, feat_ref, lane, width):
        g = lax.dot_general(
            grad[...].reshape(TS * R, E), feat_ref[...], (((0,), (0,)), ((), ())), preferred_element_type=f32
        )
        for k in range(2 * PS):
            g_ref[k % 2, k // 2, 0:OUT, lane:lane + width] = g[k * OUT:(k + 1) * OUT, :]

    d_take(grad_t, d_t_ss, d_t_rs)
    weight_grad(grad_t, ft_ref, DI, DT)
    d_take(grad_i, d_i_ss, d_i_rs)
    weight_grad(grad_i, fi_ref, 0, DI)
    g_copy = copy(g_ref.at[oc], g_sib, one_ss.at[2], one_rs.at[2], sibling)
    g_copy.start()
    g_copy.wait_recv()

    def e_copy(k, slot):
        return copy(e_out.at[k], e_in.at[slot], e_ss.at[k], e_rs.at[slot], column(k))

    def e_send(j, _):
        k = lax.rem(q + j, PS)
        e_out[k] = (g_ref[c, k] + g_sib[k]).astype(bf16)
        e_copy(k, q).start()
        return 0

    lax.fori_loop(1, PS, e_send, 0)

    def e_take(j, total):
        k = lax.rem(q + j, PS)
        e_copy(k, k).wait_recv()
        return total + e_in[k].astype(f32)

    out_ref[...] = lax.fori_loop(1, PS, e_take, g_ref[c, q] + g_sib[q])

    def sent_tensor(j, _):
        k = lax.rem(t + j, TS)
        a_copy(a_t_out, a_t_in, a_t_ss, a_t_rs, k, t).wait_send()
        a_copy(a_i_out, a_i_in, a_i_ss, a_i_rs, k, t).wait_send()
        d_copy(grad_t, d_t_ss, d_t_rs, k, t).wait_send()
        d_copy(grad_i, d_i_ss, d_i_rs, k, t).wait_send()
        return 0

    def sent_z(j, _):
        zz = lax.rem(z + j, ZS)
        b_t_copy(zz, z).wait_send()
        c_t_copy(zz, z).wait_send()
        return 0

    def sent_plane(j, _):
        k = lax.rem(p + j, PS)
        b_i_copy(k, p).wait_send()
        c_i_copy(k, p).wait_send()
        return 0

    def sent_column(j, _):
        e_copy(lax.rem(q + j, PS), q).wait_send()
        return 0

    def sent_relay(zz, _):
        relay(c, zz).wait_send()
        return 0

    lax.fori_loop(1, TS, sent_tensor, 0)
    lax.fori_loop(1, ZS, sent_z, 0)
    lax.fori_loop(1, PS, sent_plane, 0)
    lax.fori_loop(1, PS, sent_column, 0)
    lax.fori_loop(0, ZS, sent_relay, 0)
    pair_copy.wait_send()
    sib_copy.wait_send()
    g_copy.wait_send()


def on_device(image_features, text_features, image_weight, text_weight, image_pair, temp_index, bias_index):
    vmem = pl.BlockSpec(memory_space=pltpu.VMEM)
    smem = pl.BlockSpec(memory_space=pltpu.SMEM)
    dma = pltpu.SemaphoreType.DMA
    i16 = jnp.int16
    V = pltpu.VMEM
    acc = pl.pallas_call(
        kernel,
        out_shape=jax.ShapeDtypeStruct((OUT_ROWS, OUT_LANES), f32),
        in_specs=[smem, smem] + [vmem] * 5,
        out_specs=vmem,
        scratch_shapes=[
            V((TS, R, E), f32), V((TS, R, E), f32),
            V((TS, R, WIRE), i16), V((TS, R, WIRE), i16), V((TS, R, WIRE), i16), V((TS, R, WIRE), i16),
            V((R, E), f32), V((R, E), f32), V((R, 1), f32), V((R, 1), f32),
            V((PS, R, E), bf16), V((PS, R, E), bf16), V((8, 256), jnp.int32), V((8, 256), jnp.int32),
            V((PS * R, PS * R), bf16), V((PS, R, E), f32), V((PS, R, E), f32), V((ZS, R, E), f32), V((8, 128), f32),
            V((PS, R, WIRE), i16), V((PS, R, WIRE), i16), V((ZS, R, WIRE), i16), V((ZS, R, WIRE), i16),
            V((TS, R, E), bf16), V((TS, R, E), bf16),
            V((2, PS, OUT_ROWS, OUT_LANES), f32), V((PS, OUT_ROWS, OUT_LANES), f32), V((8, 128), f32),
            V((PS, OUT_ROWS, OUT_LANES), bf16), V((PS, OUT_ROWS, OUT_LANES), bf16),
        ]
        + [dma((TS,))] * 4 + [dma((PS,))] * 2 + [dma((ZS,))] * 4
        + [dma((PS,))] * 2 + [dma((ZS,))] * 2 + [dma((TS,))] * 4 + [dma((PS,))] * 2 + [dma((3,))] * 2,
        compiler_params=pltpu.CompilerParams(
            collective_id=0, has_side_effects=True, vmem_limit_bytes=50 * 2**20
        ),
        name="pair_loss_grads",
    )(
        temp_index.reshape(1), bias_index.reshape(1), image_pair.reshape(1, 256),
        image_features, text_features, image_weight, text_weight,
    )
    return acc[0:OUT, 0:DI].T, acc[0:OUT, DI:DI + DT].T


def solution(mesh):
    return jax.shard_map(
        on_device,
        mesh=mesh,
        in_specs=(P("dp", "tensor"), P("dp", "tensor"), P("tensor", None), P("tensor", None), P("dp"), P(), P()),
        out_specs=(P("tensor", "dp"), P("tensor", "dp")),
        check_vma=False,
    )
```

```python
import jax
import jax.numpy as jnp
from jax import lax
from jax.experimental import pallas as pl
from jax.experimental.pallas import tpu as pltpu
from jax.sharding import PartitionSpec as P

MESH = pl.DeviceIdType.MESH
E = 1152
DI = 176
DT = 144
R = 32
TS = 8
ZS = 8
PS = 16
OUT = 36
XS = 4
H = 16
ROWS_I = 64
ROWS_T = 48
LEVELS = 32000.0
WIRE = E + 128
f32 = jnp.float32
bf16 = jnp.bfloat16


def encode(x):
    m = jnp.max(jnp.abs(x), axis=1, keepdims=True)
    hi = jnp.floor(m)
    lo = jnp.floor((m - hi) * LEVELS) + 1.0
    top = hi + lo * (1.0 / LEVELS)
    lane = lax.broadcasted_iota(jnp.int32, (x.shape[0], 128), 1)
    values = jnp.round(x * (LEVELS / top)).astype(jnp.int32).astype(jnp.int16)
    return values, jnp.where(lane < 64, hi, lo).astype(jnp.int32).astype(jnp.int16)


def put(wire, k, x):
    wire[k, :, 0:E], wire[k, :, E:WIRE] = encode(x)


def decode(wire, k):
    code = wire[k, :, E:WIRE].astype(jnp.int32).astype(f32)
    lane = lax.broadcasted_iota(jnp.int32, code.shape, 1)
    top = jnp.sum(jnp.where(lane < 64, code, code * (1.0 / LEVELS)), axis=1, keepdims=True) * (1.0 / 64)
    return wire[k, :, 0:E].astype(jnp.int32).astype(f32) * (top * (1.0 / LEVELS))


def unit_rows(values):
    norm = jnp.sqrt(jnp.sum(values * values, axis=1, keepdims=True) + 1e-06)
    return norm, values / norm


def back_rows(direct, norm, grad):
    inner = jnp.sum(direct * grad, axis=1, keepdims=True)
    return ((grad - direct * inner) / norm).astype(bf16)


def kernel(
    temp_ref, bias_ref, pair_hbm, fi_hbm, ft_hbm, wi_hbm, wt_hbm, out_ref,
    fi_ref, ft_ref, wi_ref, wt_ref,
    part_i, part_t, a_i_out, a_i_in, a_t_out, a_t_in,
    dir_i, dir_t, norm_i, norm_t, unit_0, unit_1, all_t, pair_out, pair_in, target_ref,
    w_ref, gi_0, gi_1, gt, gt_sib, ca_out_0, ca_in_0, ca_out_1, ca_in_1,
    half_0, half_1, cb_out_0, cb_in_0, cb_out_1, cb_in_1, c_t_out, c_t_in,
    grad_i, grad_t, g_i, g_t, sib_i, sib_t, e_i_out, e_i_in, e_t_out, e_t_in,
    load_s, a_i_ss, a_i_rs, a_t_ss, a_t_rs, ba_ss, ba_rs, bb_ss, bb_rs, b_t_ss, b_t_rs, relay_ss, relay_rs,
    ca_ss, ca_rs, cb_ss, cb_rs, c_t_ss, c_t_rs, d_i_ss, d_i_rs, d_t_ss, d_t_rs,
    e_i_ss, e_i_rs, e_t_ss, e_t_rs, one_ss, one_rs,
):
    loads = [
        pltpu.make_async_copy(src, dst, load_s.at[k])
        for k, (src, dst) in enumerate((
            (ft_hbm, ft_ref), (wt_hbm, wt_ref), (fi_hbm, fi_ref), (wi_hbm, wi_ref), (pair_hbm, pair_out.at[0:1])
        ))
    ]
    for load in loads:
        load.start()

    dp = lax.axis_index("dp")
    t = lax.axis_index("tensor")
    ylo = lax.div(dp, 16)
    z = lax.rem(lax.div(dp, 2), 8)
    c = lax.rem(dp, 2)
    oc = 1 - c
    yhi = lax.div(t, XS)
    x = lax.rem(t, XS)
    y = yhi * 2 + ylo
    q = ylo * ZS + z

    def device(ylo_, z_, c_, t_):
        return ((ylo_ * ZS + z_) * 2 + c_, t_)

    sibling = device(ylo, z, oc, t)
    across = device(1 - ylo, z, c, t)
    beyond = device(1 - ylo, z, c, (1 - yhi) * XS + x)

    def at_x(xx):
        return (dp, yhi * XS + xx)

    def at_y(yy):
        return device(lax.rem(yy, 2), z, c, lax.div(yy, 2) * XS + x)

    def column(k):
        return device(lax.div(k, ZS), lax.rem(k, ZS), c, t)

    def tensor_peer(j):
        j = lax.rem(j * 5, TS)
        return lax.rem(yhi + lax.div(j, XS), 2) * XS + lax.rem(x + lax.rem(j, XS), XS)

    def z_peer(j):
        return lax.rem(z + j * 3, ZS)

    def column_peer(j):
        j = lax.rem(j * 7, PS)
        return lax.rem(ylo + lax.div(j, ZS), 2) * ZS + lax.rem(z + lax.rem(j, ZS), ZS)

    def copy(src, dst, ssem, rsem, dev):
        return pltpu.make_async_remote_copy(
            src_ref=src, dst_ref=dst, send_sem=ssem, recv_sem=rsem, device_id=dev, device_id_type=MESH
        )

    barrier = pltpu.get_barrier_semaphore()

    def greet(dev):
        pl.semaphore_signal(barrier, inc=1, device_id=dev, device_id_type=MESH)

    def greet_tensor(j, _):
        greet((dp, tensor_peer(j)))
        return 0

    def greet_column(j, _):
        greet(column(column_peer(j)))
        return 0

    lax.fori_loop(1, TS, greet_tensor, 0)
    lax.fori_loop(1, PS, greet_column, 0)
    greet(beyond)
    greet(sibling)

    def product(feat, weight):
        return lax.dot_general(
            feat[...], weight[...], (((0,), (0,)), ((), ())), preferred_element_type=f32
        ).reshape(TS, R, E)

    g_i[...] = jnp.zeros_like(g_i)
    g_t[...] = jnp.zeros_like(g_t)
    loads[0].wait()
    loads[1].wait()
    part_t[...] = product(ft_ref, wt_ref)
    loads[4].wait()
    pair_out[...] = jnp.broadcast_to(pair_out[0:1, :], (8, 256))
    pl.semaphore_wait(barrier, (TS - 1) + (PS - 1) + 2)

    def a_copy(wire_out, wire_in, ss, rs, k, slot):
        return copy(wire_out.at[k], wire_in.at[slot], ss.at[k], rs.at[slot], (dp, k))

    def a_send(part, wire_out, wire_in, ss, rs):
        def step(j, _):
            k = tensor_peer(j)
            put(wire_out, k, part[k])
            a_copy(wire_out, wire_in, ss, rs, k, t).start()
            return 0
        lax.fori_loop(1, TS, step, 0)

    def a_take(part, wire_out, wire_in, ss, rs):
        def step(j, total):
            k = tensor_peer(TS - j)
            a_copy(wire_out, wire_in, ss, rs, k, k).wait_recv()
            return total + decode(wire_in, k)
        return lax.fori_loop(1, TS, step, part[t])

    a_send(part_t, a_t_out, a_t_in, a_t_ss, a_t_rs)
    pair_copy = copy(pair_out, pair_in, one_ss.at[0], one_rs.at[0], across)
    pair_copy.start()
    loads[2].wait()
    loads[3].wait()
    part_i[...] = product(fi_ref, wi_ref)
    a_send(part_i, a_i_out, a_i_in, a_i_ss, a_i_rs)

    def local_target(pair):
        r = pair & 31
        tt = (pair >> 5) & 7
        cc = (pair >> 8) & 1
        zz = (pair >> 9) & 7
        yy = (pair >> 12) & 1
        here = jnp.logical_and(tt == t, yy == ylo)
        return jnp.where(here, (cc * ZS + zz) * R + r, -1)

    pair_copy.wait_recv()
    own = local_target(pair_out[0:1, :])
    other = local_target(pair_in[0:1, :])
    by_ylo = (jnp.where(ylo == 0, own, other), jnp.where(ylo == 0, other, own))
    for yy in range(XS):
        for xx in range(XS):
            lane = ((yy // 2) * XS + xx) * R
            s0, s1 = (yy * XS + xx) * H, (xx * XS + yy) * H + PS * H
            target_ref[0:1, s0:s0 + H] = by_ylo[yy % 2][:, lane:lane + H]
            target_ref[0:1, s1:s1 + H] = by_ylo[yy % 2][:, lane + H:lane + R]

    def b_t_copy(zz, slot):
        s = c * ZS + slot
        return copy(all_t.at[s], all_t.at[s], b_t_ss.at[zz], b_t_rs.at[slot], device(ylo, zz, c, t))

    def relay(cc, zz):
        s = cc * ZS + zz
        return copy(all_t.at[s], all_t.at[s], relay_ss.at[zz], relay_rs.at[zz], sibling)

    norm, direct = unit_rows(a_take(part_t, a_t_out, a_t_in, a_t_ss, a_t_rs))
    norm_t[...] = norm
    dir_t[...] = direct
    all_t[c * ZS + z] = direct.astype(bf16)

    def b_t_send(j, _):
        b_t_copy(z_peer(j), z).start()
        return 0

    lax.fori_loop(1, ZS, b_t_send, 0)
    relay(c, z).start()

    halves = ((unit_0, at_x, x, at_y, y), (unit_1, at_y, y, at_x, x))

    def ba_copy(h, k, slot):
        unit, first, me, second, line = halves[h]
        s = line * XS + slot
        return copy(unit.at[s], unit.at[s], ba_ss.at[h * XS + k], ba_rs.at[h * XS + slot], first(k))

    def bb_copy(h, k, slot):
        unit, first, me, second, line = halves[h]
        s = pl.ds(slot * XS, XS)
        return copy(unit.at[s], unit.at[s], bb_ss.at[h * XS + k], bb_rs.at[h * XS + slot], second(k))

    norm, direct = unit_rows(a_take(part_i, a_i_out, a_i_in, a_i_ss, a_i_rs))
    norm_i[...] = norm
    dir_i[...] = direct
    unit = direct.astype(bf16)
    unit_0[y * XS + x] = unit[0:H]
    unit_1[x * XS + y] = unit[H:R]
    steps = [(d, h) for d in (2, 1, 3) for h in (0, 1)]
    for d, h in steps:
        me = halves[h][2]
        ba_copy(h, lax.rem(me + d, XS), me).start()
    for h in (0, 1):
        me, line = halves[h][2], halves[h][4]
        for d in (1, 3, 2):
            k = lax.rem(me + d, XS)
            ba_copy(h, k, k).wait_recv()
        for d in (2, 1, 3):
            bb_copy(h, lax.rem(line + d, XS), line).start()

    def b_t_take(j, _):
        zz = z_peer(ZS - j)
        b_t_copy(zz, zz).wait_recv()
        relay(c, zz).start()
        return 0

    lax.fori_loop(1, ZS, b_t_take, 0)

    def relay_take(zz, _):
        relay(oc, zz).wait_recv()
        return 0

    lax.fori_loop(0, ZS, relay_take, 0)
    for d, h in steps:
        k = lax.rem(halves[h][4] + d, XS)
        bb_copy(h, k, k).wait_recv()

    scale = 4.0 + temp_ref[0].astype(f32)
    shift = -0.5 * bias_ref[0].astype(f32)
    half = PS * H

    def tile(j, _):
        b = lax.rem(2 * oc + j, 4)
        rows = all_t[pl.ds(b * 4, 4)].reshape(4 * R, E)
        total = None
        for h, unit in ((0, unit_0), (1, unit_1)):
            img = unit[...].reshape(half, E)
            logits = scale * lax.dot_general(
                rows, img, (((1,), (1,)), ((), ())), preferred_element_type=f32
            ) + shift
            index = lax.broadcasted_iota(jnp.int32, (4 * R, half), 0) + b * (4 * R)
            sign = jnp.where(index == target_ref[0:1, h * half:(h + 1) * half], f32(1.0), f32(-1.0))
            w = (-scale * sign * jax.nn.sigmoid(-sign * logits)).astype(bf16)
            w_ref[pl.ds(pl.multiple_of(b * (4 * R), 4 * R), 4 * R), h * half:(h + 1) * half] = w
            part = jnp.dot(w, img, preferred_element_type=f32)
            total = part if total is None else total + part
        gt[pl.ds(b * 4, 4)] = total.reshape(4, R, E)
        return 0

    lax.fori_loop(0, 2, tile, 0)
    gt_copy = copy(gt.at[pl.ds(oc * ZS, ZS)], gt_sib, one_ss.at[1], one_rs.at[1], sibling)
    gt_copy.start()
    lax.fori_loop(2, 4, tile, 0)
    gt_copy.wait_recv()

    def c_t_copy(zz, slot):
        return copy(c_t_out.at[zz], c_t_in.at[slot], c_t_ss.at[zz], c_t_rs.at[slot], device(ylo, zz, c, t))

    def c_t_send(j, _):
        zz = z_peer(j)
        put(c_t_out, zz, gt[c * ZS + zz] + gt_sib[zz])
        c_t_copy(zz, z).start()
        return 0

    lax.fori_loop(1, ZS, c_t_send, 0)

    back = ((gi_0, ca_out_0, ca_in_0, half_0, cb_out_0, cb_in_0), (gi_1, ca_out_1, ca_in_1, half_1, cb_out_1, cb_in_1))

    def ca_copy(h, k, slot):
        out, into = back[h][1], back[h][2]
        return copy(out.at[k], into.at[slot], ca_ss.at[h * XS + k], ca_rs.at[h * XS + slot], halves[h][3](k))

    def cb_copy(h, k, slot):
        out, into = back[h][4], back[h][5]
        return copy(out.at[k], into.at[slot], cb_ss.at[h * XS + k], cb_rs.at[h * XS + slot], halves[h][1](k))

    for h in (0, 1):
        gi, out = back[h][0], back[h][1]
        for b in range(2):
            lane = h * half + b * 128
            gi[8 * b:8 * b + 8] = lax.dot_general(
                w_ref[:, lane:lane + 128], all_t[...].reshape(PS * R, E), (((0,), (0,)), ((), ())),
                preferred_element_type=f32,
            ).reshape(8, H, E)
        line = halves[h][4]
        for d in (2, 1, 3):
            k = lax.rem(line + d, XS)
            put(out, k, gi[pl.ds(k * XS, XS)].reshape(XS * H, E))
            ca_copy(h, k, line).start()

    for h in (0, 1):
        gi, into, part, out = back[h][0], back[h][2], back[h][3], back[h][4]
        me, line = halves[h][2], halves[h][4]
        total = gi[pl.ds(line * XS, XS)].reshape(XS * H, E)
        for d in (1, 3, 2):
            k = lax.rem(line + d, XS)
            ca_copy(h, k, k).wait_recv()
            total = total + decode(into, k)
        part[...] = total.reshape(XS, H, E)
        for d in (2, 1, 3):
            k = lax.rem(me + d, XS)
            put(out, k, part[k])
            cb_copy(h, k, me).start()

    def c_i_take(h):
        into, part, me = back[h][5], back[h][3], halves[h][2]
        total = part[me]
        for d in (1, 3, 2):
            k = lax.rem(me + d, XS)
            cb_copy(h, k, k).wait_recv()
            total = total + decode(into, k)
        return total

    def c_t_take(j, total):
        zz = z_peer(ZS - j)
        c_t_copy(zz, zz).wait_recv()
        return total + decode(c_t_in, zz)

    def d_copy(grad, ss, rs, k, slot):
        return copy(grad.at[slot], grad.at[slot], ss.at[k], rs.at[slot], (dp, k))

    def d_send(grad, ss, rs):
        def step(j, _):
            d_copy(grad, ss, rs, tensor_peer(j), t).start()
            return 0
        lax.fori_loop(1, TS, step, 0)

    def d_take(grad, ss, rs):
        def step(j, _):
            k = tensor_peer(TS - j)
            d_copy(grad, ss, rs, k, k).wait_recv()
            return 0
        lax.fori_loop(1, TS, step, 0)

    total = jnp.concatenate([c_i_take(0), c_i_take(1)], axis=0)
    grad_i[t] = back_rows(dir_i[...], norm_i[...], total)
    d_send(grad_i, d_i_ss, d_i_rs)
    total = lax.fori_loop(1, ZS, c_t_take, gt[c * ZS + z] + gt_sib[z])
    grad_t[t] = back_rows(dir_t[...], norm_t[...], total)
    d_send(grad_t, d_t_ss, d_t_rs)

    def weight_grad(grad, feat, packed, fold):
        g = lax.dot_general(
            grad[...].reshape(TS * R, E), feat[...], (((0,), (1,)), ((), ())), preferred_element_type=f32
        )
        rest, rows = g.shape[1] - 128, OUT // fold
        for k in range(2 * PS):
            packed[k % 2, k // 2, 0:OUT, :] = g[k * OUT:(k + 1) * OUT, 0:128]
            for n in range(fold):
                packed[k % 2, k // 2, OUT:OUT + rows, n * rest:(n + 1) * rest] = (
                    g[k * OUT + n * rows:k * OUT + (n + 1) * rows, 128:]
                )

    def e_copy(out, into, ss, rs, k, slot):
        return copy(out.at[k], into.at[slot], ss.at[k], rs.at[slot], column(k))

    def e_send(packed, sib, out, into, ss, rs):
        def step(j, _):
            k = column_peer(j)
            out[k] = (packed[c, k] + sib[k]).astype(bf16)
            e_copy(out, into, ss, rs, k, q).start()
            return 0
        lax.fori_loop(1, PS, step, 0)

    def e_take(packed, sib, out, into, ss, rs):
        def step(j, total):
            k = column_peer(PS - j)
            e_copy(out, into, ss, rs, k, k).wait_recv()
            return total + into[k].astype(f32)
        return lax.fori_loop(1, PS, step, packed[c, q] + sib[q])

    e_i = (g_i, sib_i, e_i_out, e_i_in, e_i_ss, e_i_rs)
    e_t = (g_t, sib_t, e_t_out, e_t_in, e_t_ss, e_t_rs)
    d_take(grad_i, d_i_ss, d_i_rs)
    weight_grad(grad_i, fi_ref, g_i, 2)
    g_i_copy = copy(g_i.at[oc], sib_i, one_ss.at[2], one_rs.at[2], sibling)
    g_i_copy.start()
    g_i_copy.wait_recv()
    e_send(*e_i)
    d_take(grad_t, d_t_ss, d_t_rs)
    weight_grad(grad_t, ft_ref, g_t, 3)
    g_t_copy = copy(g_t.at[oc], sib_t, one_ss.at[3], one_rs.at[3], sibling)
    g_t_copy.start()
    g_t_copy.wait_recv()
    e_send(*e_t)

    def unpack(total, lane, width, fold):
        rest, rows = width - 128, OUT // fold
        out_ref[0:OUT, lane:lane + 128] = total[0:OUT, :]
        for n in range(fold):
            out_ref[n * rows:(n + 1) * rows, lane + 128:lane + width] = (
                total[OUT:OUT + rows, n * rest:(n + 1) * rest]
            )

    unpack(e_take(*e_i), 0, DI, 2)
    unpack(e_take(*e_t), 256, DT, 3)

    def sent_tensor(j, _):
        k = tensor_peer(j)
        a_copy(a_t_out, a_t_in, a_t_ss, a_t_rs, k, t).wait_send()
        a_copy(a_i_out, a_i_in, a_i_ss, a_i_rs, k, t).wait_send()
        d_copy(grad_t, d_t_ss, d_t_rs, k, t).wait_send()
        d_copy(grad_i, d_i_ss, d_i_rs, k, t).wait_send()
        return 0

    def sent_z(j, _):
        zz = z_peer(j)
        b_t_copy(zz, z).wait_send()
        c_t_copy(zz, z).wait_send()
        return 0

    def sent_column(j, _):
        k = column_peer(j)
        e_copy(e_i_out, e_i_in, e_i_ss, e_i_rs, k, q).wait_send()
        e_copy(e_t_out, e_t_in, e_t_ss, e_t_rs, k, q).wait_send()
        return 0

    def sent_relay(zz, _):
        relay(c, zz).wait_send()
        return 0

    lax.fori_loop(1, TS, sent_tensor, 0)
    lax.fori_loop(1, ZS, sent_z, 0)
    lax.fori_loop(1, PS, sent_column, 0)
    lax.fori_loop(0, ZS, sent_relay, 0)
    for d, h in steps:
        me, line = halves[h][2], halves[h][4]
        ba_copy(h, lax.rem(me + d, XS), me).wait_send()
        bb_copy(h, lax.rem(line + d, XS), line).wait_send()
        ca_copy(h, lax.rem(line + d, XS), line).wait_send()
        cb_copy(h, lax.rem(me + d, XS), me).wait_send()
    for sent in (pair_copy, gt_copy, g_i_copy, g_t_copy):
        sent.wait_send()


def on_device(image_features, text_features, image_weight, text_weight, image_pair, temp_index, bias_index):
    vmem = pl.BlockSpec(memory_space=pltpu.VMEM)
    smem = pl.BlockSpec(memory_space=pltpu.SMEM)
    hbm = pl.BlockSpec(memory_space=pl.ANY)
    dma = pltpu.SemaphoreType.DMA
    i16 = jnp.int16
    V = pltpu.VMEM
    acc = pl.pallas_call(
        kernel,
        out_shape=jax.ShapeDtypeStruct((40, 512), f32),
        in_specs=[smem, smem] + [hbm] * 5,
        out_specs=vmem,
        scratch_shapes=[
            V((DI, 256), bf16), V((DT, 256), bf16), V((DI, E), bf16), V((DT, E), bf16),
            V((TS, R, E), f32), V((TS, R, E), f32),
            V((TS, R, WIRE), i16), V((TS, R, WIRE), i16), V((TS, R, WIRE), i16), V((TS, R, WIRE), i16),
            V((R, E), f32), V((R, E), f32), V((R, 1), f32), V((R, 1), f32),
            V((PS, H, E), bf16), V((PS, H, E), bf16), V((PS, R, E), bf16),
            V((8, 256), jnp.int32), V((8, 256), jnp.int32), V((8, PS * R), jnp.int32),
            V((PS * R, PS * R), bf16), V((PS, H, E), f32), V((PS, H, E), f32), V((PS, R, E), f32), V((ZS, R, E), f32),
        ]
        + [V((XS, XS * H, WIRE), i16)] * 4
        + [V((XS, H, E), f32)] * 2 + [V((XS, H, WIRE), i16)] * 4 + [V((ZS, R, WIRE), i16)] * 2
        + [
            V((TS, R, E), bf16), V((TS, R, E), bf16),
            V((2, PS, ROWS_I, 128), f32), V((2, PS, ROWS_T, 128), f32),
            V((PS, ROWS_I, 128), f32), V((PS, ROWS_T, 128), f32),
            V((PS, ROWS_I, 128), bf16), V((PS, ROWS_I, 128), bf16),
            V((PS, ROWS_T, 128), bf16), V((PS, ROWS_T, 128), bf16),
        ]
        + [dma((5,))] + [dma((TS,))] * 4 + [dma((2 * XS,))] * 4 + [dma((ZS,))] * 4
        + [dma((2 * XS,))] * 4 + [dma((ZS,))] * 2 + [dma((TS,))] * 4 + [dma((PS,))] * 4 + [dma((4,))] * 2,
        compiler_params=pltpu.CompilerParams(
            collective_id=0, has_side_effects=True, vmem_limit_bytes=56 * 2**20
        ),
        name="pair_loss_grads",
    )(
        temp_index.reshape(1), bias_index.reshape(1), image_pair.reshape(1, 256),
        image_features.T, text_features.T, image_weight, text_weight,
    )
    return acc[0:OUT, 0:DI].T, acc[0:OUT, 256:256 + DT].T


def solution(mesh):
    return jax.shard_map(
        on_device,
        mesh=mesh,
        in_specs=(P("dp", "tensor"), P("dp", "tensor"), P("tensor", None), P("tensor", None), P("dp"), P(), P()),
        out_specs=(P("tensor", "dp"), P("tensor", "dp")),
        check_vma=False,
    )
```

```python
import jax
import jax.numpy as jnp
from jax import lax
from jax.experimental import pallas as pl
from jax.experimental.pallas import tpu as pltpu
from jax.sharding import PartitionSpec as P

MESH = pl.DeviceIdType.MESH
E = 1152
DI = 176
DT = 144
R = 32
TS = 8
ZS = 8
PS = 16
OUT = 36
XS = 4
H = 16
ROWS_I = 64
ROWS_T = 48
LEVELS = 32000.0
G = E // 128
f32 = jnp.float32
bf16 = jnp.bfloat16


def put(wire, k, x):
    n = x.shape[0]
    m = jnp.max(jnp.abs(x), axis=1, keepdims=True)
    hi = jnp.floor(m)
    lo = jnp.floor((m - hi) * LEVELS) + 1.0
    q = jnp.round(x * (LEVELS / (hi + lo * (1.0 / LEVELS)))).astype(jnp.int32).astype(jnp.int16)
    for g in range(G):
        wire[k, g * n:(g + 1) * n, :] = q[:, g * 128:(g + 1) * 128]
    diagonal = lax.broadcasted_iota(jnp.int32, (n, 128), 0) == lax.broadcasted_iota(jnp.int32, (n, 128), 1)
    hi = jnp.sum(jnp.where(diagonal, hi, 0.0), axis=0, keepdims=True)
    lo = jnp.sum(jnp.where(diagonal, lo, 0.0), axis=0, keepdims=True)
    row = lax.broadcasted_iota(jnp.int32, (16, 128), 0)
    wire[k, G * n:G * n + 16, :] = (
        jnp.where(row == 0, hi, jnp.where(row == 1, lo, 0.0)).astype(jnp.int32).astype(jnp.int16)
    )


def take(wire, k, n):
    code = wire[k, G * n:G * n + 16, :].astype(jnp.int32).astype(f32)
    top = code[0:1, :] + code[1:2, :] * (1.0 / LEVELS)
    diagonal = lax.broadcasted_iota(jnp.int32, (n, 128), 0) == lax.broadcasted_iota(jnp.int32, (n, 128), 1)
    step = jnp.sum(jnp.where(diagonal, top, 0.0), axis=1, keepdims=True) * (1.0 / LEVELS)
    return jnp.concatenate(
        [wire[k, g * n:(g + 1) * n, :].astype(jnp.int32).astype(f32) * step for g in range(G)], axis=1
    )


def unit_rows(values):
    norm = jnp.sqrt(jnp.sum(values * values, axis=1, keepdims=True) + 1e-06)
    return norm, values / norm


def back_rows(direct, norm, grad):
    inner = jnp.sum(direct * grad, axis=1, keepdims=True)
    return ((grad - direct * inner) / norm).astype(bf16)


def kernel(
    temp_hbm, bias_hbm, pair_hbm, fi_hbm, ft_hbm, wi_hbm, wt_hbm, out_i, out_t,
    temp_ref, bias_ref,
    fi_ref, ft_ref, wi_ref, wt_ref,
    part_i, part_t, a_i_out, a_i_in, a_t_out, a_t_in,
    dir_i, dir_t, norm_i, norm_t, unit_0, unit_1, all_t, pair_out, pair_in, target_ref,
    w_ref, gi_0, gi_1, gt, gt_sib, ca_out_0, ca_in_0, ca_out_1, ca_in_1,
    half_0, half_1, cb_out_0, cb_in_0, cb_out_1, cb_in_1, c_t_out, c_t_in,
    grad_i, grad_t, g_i, g_t, sib_i, sib_t, e_i_out, e_i_in, e_t_out, e_t_in,
    load_s, a_i_ss, a_i_rs, a_t_ss, a_t_rs, ba_ss, ba_rs, bb_ss, bb_rs, b_t_ss, b_t_rs, relay_ss, relay_rs,
    ca_ss, ca_rs, cb_ss, cb_rs, gt_ss, gt_rs, c_t_ss, c_t_rs, d_i_ss, d_i_rs, d_t_ss, d_t_rs,
    e_i_ss, e_i_rs, e_t_ss, e_t_rs, one_ss, one_rs,
):
    loads = [
        pltpu.make_async_copy(src, dst, load_s.at[k])
        for k, (src, dst) in enumerate((
            (ft_hbm, ft_ref), (wt_hbm, wt_ref), (fi_hbm, fi_ref), (wi_hbm, wi_ref), (pair_hbm, pair_out.at[0:1]),
            (temp_hbm, temp_ref), (bias_hbm, bias_ref),
        ))
    ]
    for load in loads:
        load.start()

    dp = lax.axis_index("dp")
    t = lax.axis_index("tensor")
    ylo = lax.div(dp, 16)
    z = lax.rem(lax.div(dp, 2), 8)
    c = lax.rem(dp, 2)
    oc = 1 - c
    yhi = lax.div(t, XS)
    x = lax.rem(t, XS)
    y = yhi * 2 + ylo
    q = ylo * ZS + z

    def device(ylo_, z_, c_, t_):
        return ((ylo_ * ZS + z_) * 2 + c_, t_)

    sibling = device(ylo, z, oc, t)
    across = device(1 - ylo, z, c, t)
    beyond = device(1 - ylo, z, c, (1 - yhi) * XS + x)

    def at_x(xx):
        return (dp, yhi * XS + xx)

    def at_y(yy):
        return device(lax.rem(yy, 2), z, c, lax.div(yy, 2) * XS + x)

    def column(k):
        return device(lax.div(k, ZS), lax.rem(k, ZS), c, t)

    def tensor_peer(j):
        j = lax.rem(j * 5, TS)
        return lax.rem(yhi + lax.div(j, XS), 2) * XS + lax.rem(x + lax.rem(j, XS), XS)

    def z_peer(j):
        return lax.rem(z + j * 3, ZS)

    def column_peer(j):
        j = lax.rem(j * 7, PS)
        return lax.rem(ylo + lax.div(j, ZS), 2) * ZS + lax.rem(z + lax.rem(j, ZS), ZS)

    def copy(src, dst, ssem, rsem, dev):
        return pltpu.make_async_remote_copy(
            src_ref=src, dst_ref=dst, send_sem=ssem, recv_sem=rsem, device_id=dev, device_id_type=MESH
        )

    barrier = pltpu.get_barrier_semaphore()

    def greet(dev):
        pl.semaphore_signal(barrier, inc=1, device_id=dev, device_id_type=MESH)

    def greet_tensor(j, _):
        greet((dp, tensor_peer(j)))
        return 0

    def greet_column(j, _):
        greet(column(column_peer(j)))
        return 0

    lax.fori_loop(1, TS, greet_tensor, 0)
    lax.fori_loop(1, PS, greet_column, 0)
    greet(beyond)
    greet(sibling)

    def product(feat, weight):
        return lax.dot_general(
            feat[...], weight[...], (((0,), (0,)), ((), ())), preferred_element_type=f32
        ).reshape(TS, R, E)

    g_i[...] = jnp.zeros_like(g_i)
    g_t[...] = jnp.zeros_like(g_t)
    loads[0].wait()
    loads[1].wait()
    part_t[...] = product(ft_ref, wt_ref)
    loads[4].wait()
    pair_out[...] = jnp.broadcast_to(pair_out[0:1, :], (8, 256))
    pl.semaphore_wait(barrier, (TS - 1) + (PS - 1) + 2)

    def a_copy(wire_out, wire_in, ss, rs, k, slot):
        return copy(wire_out.at[k], wire_in.at[slot], ss.at[k], rs.at[slot], (dp, k))

    def a_send(part, wire_out, wire_in, ss, rs):
        def step(j, _):
            k = tensor_peer(j)
            put(wire_out, k, part[k])
            a_copy(wire_out, wire_in, ss, rs, k, t).start()
            return 0
        lax.fori_loop(1, TS, step, 0)

    def a_take(part, wire_out, wire_in, ss, rs):
        def step(j, total):
            k = tensor_peer(TS - j)
            a_copy(wire_out, wire_in, ss, rs, k, k).wait_recv()
            return total + take(wire_in, k, R)
        return lax.fori_loop(1, TS, step, part[t])

    a_send(part_t, a_t_out, a_t_in, a_t_ss, a_t_rs)
    pair_copy = copy(pair_out, pair_in, one_ss.at[0], one_rs.at[0], across)
    pair_copy.start()
    loads[2].wait()
    loads[3].wait()
    part_i[...] = product(fi_ref, wi_ref)
    a_send(part_i, a_i_out, a_i_in, a_i_ss, a_i_rs)

    def local_target(pair):
        r = pair & 31
        tt = (pair >> 5) & 7
        cc = (pair >> 8) & 1
        zz = (pair >> 9) & 7
        yy = (pair >> 12) & 1
        here = jnp.logical_and(tt == t, yy == ylo)
        return jnp.where(here, (cc * ZS + zz) * R + r, -1)

    pair_copy.wait_recv()
    own = local_target(pair_out[0:1, :])
    other = local_target(pair_in[0:1, :])
    by_ylo = (jnp.where(ylo == 0, own, other), jnp.where(ylo == 0, other, own))
    for yy in range(XS):
        for xx in range(XS):
            lane = ((yy // 2) * XS + xx) * R
            s0, s1 = (yy * XS + xx) * H, (xx * XS + yy) * H + PS * H
            target_ref[0:1, s0:s0 + H] = by_ylo[yy % 2][:, lane:lane + H]
            target_ref[0:1, s1:s1 + H] = by_ylo[yy % 2][:, lane + H:lane + R]

    def b_t_copy(zz, slot):
        s = c * ZS + slot
        return copy(all_t.at[s], all_t.at[s], b_t_ss.at[zz], b_t_rs.at[slot], device(ylo, zz, c, t))

    def relay(cc, zz):
        s = cc * ZS + zz
        return copy(all_t.at[s], all_t.at[s], relay_ss.at[zz], relay_rs.at[zz], sibling)

    norm, direct = unit_rows(a_take(part_t, a_t_out, a_t_in, a_t_ss, a_t_rs))
    norm_t[...] = norm
    dir_t[...] = direct
    all_t[c * ZS + z] = direct.astype(bf16)

    def b_t_send(j, _):
        b_t_copy(z_peer(j), z).start()
        return 0

    lax.fori_loop(1, ZS, b_t_send, 0)
    relay(c, z).start()

    halves = ((unit_0, at_x, x, at_y, y), (unit_1, at_y, y, at_x, x))

    def ba_copy(h, k, slot):
        unit, first, me, second, line = halves[h]
        s = line * XS + slot
        return copy(unit.at[s], unit.at[s], ba_ss.at[h * XS + k], ba_rs.at[h * XS + slot], first(k))

    def bb_copy(h, i, k, slot):
        unit, first, me, second, line = halves[h]
        s = slot * XS + i
        return copy(unit.at[s], unit.at[s], bb_ss.at[h * PS + k * XS + i], bb_rs.at[h * PS + s], second(k))

    norm, direct = unit_rows(a_take(part_i, a_i_out, a_i_in, a_i_ss, a_i_rs))
    norm_i[...] = norm
    dir_i[...] = direct
    unit = direct.astype(bf16)
    unit_0[y * XS + x] = unit[0:H]
    unit_1[x * XS + y] = unit[H:R]
    steps = [(d, h) for d in (2, 1, 3) for h in (0, 1)]
    for d, h in steps:
        me = halves[h][2]
        ba_copy(h, lax.rem(me + d, XS), me).start()

    def bb_send(h, i):
        line = halves[h][4]
        for d in (2, 1, 3):
            bb_copy(h, i, lax.rem(line + d, XS), line).start()

    for h in (0, 1):
        bb_send(h, halves[h][2])
    for d in (1, 3, 2):
        for h in (0, 1):
            k = lax.rem(halves[h][2] + d, XS)
            ba_copy(h, k, k).wait_recv()
            bb_send(h, k)

    def b_t_take(j, _):
        zz = z_peer(ZS - j)
        b_t_copy(zz, zz).wait_recv()
        relay(c, zz).start()
        return 0

    lax.fori_loop(1, ZS, b_t_take, 0)

    def relay_take(zz, _):
        relay(oc, zz).wait_recv()
        return 0

    lax.fori_loop(0, ZS, relay_take, 0)
    for d, h in steps:
        k = lax.rem(halves[h][4] + d, XS)
        for i in range(XS):
            bb_copy(h, i, k, k).wait_recv()

    loads[5].wait()
    loads[6].wait()
    scale = 4.0 + temp_ref[0].astype(f32)
    shift = -0.5 * bias_ref[0].astype(f32)
    half = PS * H

    def tile_weights(b, _):
        rows = all_t[pl.ds(b * 4, 4)].reshape(4 * R, E)
        for h, unit in ((0, unit_0), (1, unit_1)):
            logits = scale * lax.dot_general(
                rows, unit[...].reshape(half, E), (((1,), (1,)), ((), ())), preferred_element_type=f32
            ) + shift
            index = lax.broadcasted_iota(jnp.int32, (4 * R, half), 0) + b * (4 * R)
            sign = jnp.where(index == target_ref[0:1, h * half:(h + 1) * half], f32(1.0), f32(-1.0))
            w = (-scale * sign * jax.nn.sigmoid(-sign * logits)).astype(bf16)
            w_ref[pl.ds(pl.multiple_of(b * (4 * R), 4 * R), 4 * R), h * half:(h + 1) * half] = w
        return 0

    lax.fori_loop(0, 4, tile_weights, 0)

    back = ((gi_0, ca_out_0, ca_in_0, half_0, cb_out_0, cb_in_0), (gi_1, ca_out_1, ca_in_1, half_1, cb_out_1, cb_in_1))

    def ca_copy(h, i, k, slot):
        out, into = back[h][1], back[h][2]
        return copy(
            out.at[k * XS + i], into.at[slot * XS + i],
            ca_ss.at[h * PS + k * XS + i], ca_rs.at[h * PS + slot * XS + i], halves[h][3](k),
        )

    def cb_copy(h, k, slot):
        out, into = back[h][4], back[h][5]
        return copy(out.at[k], into.at[slot], cb_ss.at[h * XS + k], cb_rs.at[h * XS + slot], halves[h][1](k))

    for h in (0, 1):
        gi = back[h][0]
        for b in range(2):
            lane = h * half + b * 128
            gi[8 * b:8 * b + 8] = lax.dot_general(
                w_ref[:, lane:lane + 128], all_t[...].reshape(PS * R, E), (((0,), (0,)), ((), ())),
                preferred_element_type=f32,
            ).reshape(8, H, E)

        def ca_send(n, _, h=h):
            gi, out, me, line = back[h][0], back[h][1], halves[h][2], halves[h][4]
            i = lax.rem(me + 1 + lax.div(n, 3), XS)
            k = lax.rem(line + 1 + lax.rem(n, 3), XS)
            put(out, k * XS + i, gi[k * XS + i])
            ca_copy(h, i, k, line).start()
            return 0

        lax.fori_loop(0, 3 * XS, ca_send, 0)

    def tile_text(b):
        w = w_ref.at[pl.ds(pl.multiple_of(b * (4 * R), 4 * R), 4 * R)]
        total = jnp.dot(w[:, 0:half], unit_0[...].reshape(half, E), preferred_element_type=f32)
        total = total + jnp.dot(w[:, half:], unit_1[...].reshape(half, E), preferred_element_type=f32)
        gt[pl.ds(b * 4, 4)] = total.reshape(4, R, E)

    def gt_copy(b):
        return copy(
            gt.at[pl.ds(oc * ZS + b * 4, 4)], gt_sib.at[pl.ds(b * 4, 4)], gt_ss.at[b], gt_rs.at[b], sibling
        )

    def tile_other(b, _):
        tile_text(2 * oc + b)
        gt_copy(b).start()
        return 0

    def tile_own(b, _):
        tile_text(2 * c + b)
        return 0

    lax.fori_loop(0, 2, tile_other, 0)
    lax.fori_loop(0, 2, tile_own, 0)
    gt_copy(0).wait_recv()
    gt_copy(1).wait_recv()

    def c_t_copy(zz, slot):
        return copy(c_t_out.at[zz], c_t_in.at[slot], c_t_ss.at[zz], c_t_rs.at[slot], device(ylo, zz, c, t))

    def c_t_send(j, _):
        zz = z_peer(j)
        put(c_t_out, zz, gt[c * ZS + zz] + gt_sib[zz])
        c_t_copy(zz, z).start()
        return 0

    lax.fori_loop(1, ZS, c_t_send, 0)

    for h in (0, 1):
        gi, into, part, out = back[h][0], back[h][2], back[h][3], back[h][4]
        me, line = halves[h][2], halves[h][4]
        for e in (1, 2, 3, 0):
            i = lax.rem(me + e, XS)
            total = gi[line * XS + i]
            for d in (1, 3, 2):
                k = lax.rem(line + d, XS)
                ca_copy(h, i, k, k).wait_recv()
                total = total + take(into, k * XS + i, H)
            if e:
                put(out, i, total)
                cb_copy(h, i, me).start()
            else:
                part[...] = total

    def c_i_take(h):
        into, part, me = back[h][5], back[h][3], halves[h][2]
        total = part[...]
        for d in (1, 3, 2):
            k = lax.rem(me + d, XS)
            cb_copy(h, k, k).wait_recv()
            total = total + take(into, k, H)
        return total

    def c_t_take(j, total):
        zz = z_peer(ZS - j)
        c_t_copy(zz, zz).wait_recv()
        return total + take(c_t_in, zz, R)

    def d_copy(grad, ss, rs, k, slot):
        return copy(grad.at[slot], grad.at[slot], ss.at[k], rs.at[slot], (dp, k))

    def d_send(grad, ss, rs):
        def step(j, _):
            d_copy(grad, ss, rs, tensor_peer(j), t).start()
            return 0
        lax.fori_loop(1, TS, step, 0)

    def d_take(grad, ss, rs):
        def step(j, _):
            k = tensor_peer(TS - j)
            d_copy(grad, ss, rs, k, k).wait_recv()
            return 0
        lax.fori_loop(1, TS, step, 0)

    total = jnp.concatenate([c_i_take(0), c_i_take(1)], axis=0)
    grad_i[t] = back_rows(dir_i[...], norm_i[...], total)
    d_send(grad_i, d_i_ss, d_i_rs)
    total = lax.fori_loop(1, ZS, c_t_take, gt[c * ZS + z] + gt_sib[z])
    grad_t[t] = back_rows(dir_t[...], norm_t[...], total)
    d_send(grad_t, d_t_ss, d_t_rs)

    def weight_grad(grad, feat, packed, fold):
        g = lax.dot_general(
            grad[...].reshape(TS * R, E), feat[...], (((0,), (1,)), ((), ())), preferred_element_type=f32
        )
        rest, rows = g.shape[1] - 128, OUT // fold
        for k in range(2 * PS):
            packed[k % 2, k // 2, 0:OUT, :] = g[k * OUT:(k + 1) * OUT, 0:128]
            for n in range(fold):
                packed[k % 2, k // 2, OUT:OUT + rows, n * rest:(n + 1) * rest] = (
                    g[k * OUT + n * rows:k * OUT + (n + 1) * rows, 128:]
                )

    def e_copy(out, into, ss, rs, k, slot):
        return copy(out.at[k], into.at[slot], ss.at[k], rs.at[slot], column(k))

    def e_send(packed, sib, out, into, ss, rs):
        def step(j, _):
            k = column_peer(j)
            out[k] = (packed[c, k] + sib[k]).astype(bf16)
            e_copy(out, into, ss, rs, k, q).start()
            return 0
        lax.fori_loop(1, PS, step, 0)

    def e_take(packed, sib, out, into, ss, rs):
        def step(j, total):
            k = column_peer(PS - j)
            e_copy(out, into, ss, rs, k, k).wait_recv()
            return total + into[k].astype(f32)
        return lax.fori_loop(1, PS, step, packed[c, q] + sib[q])

    e_i = (g_i, sib_i, e_i_out, e_i_in, e_i_ss, e_i_rs)
    e_t = (g_t, sib_t, e_t_out, e_t_in, e_t_ss, e_t_rs)
    d_take(grad_i, d_i_ss, d_i_rs)
    weight_grad(grad_i, fi_ref, g_i, 2)
    g_i_copy = copy(g_i.at[oc], sib_i, one_ss.at[1], one_rs.at[1], sibling)
    g_i_copy.start()
    g_i_copy.wait_recv()
    e_send(*e_i)
    d_take(grad_t, d_t_ss, d_t_rs)
    weight_grad(grad_t, ft_ref, g_t, 3)
    g_t_copy = copy(g_t.at[oc], sib_t, one_ss.at[2], one_rs.at[2], sibling)
    g_t_copy.start()
    g_t_copy.wait_recv()
    e_send(*e_t)

    def unpack(total, out, width, fold):
        rest, rows = width - 128, OUT // fold
        out[:, 0:128] = total[0:OUT, :]
        for n in range(fold):
            out[n * rows:(n + 1) * rows, 128:width] = (
                total[OUT:OUT + rows, n * rest:(n + 1) * rest]
            )

    unpack(e_take(*e_i), out_i, DI, 2)
    unpack(e_take(*e_t), out_t, DT, 3)

    def sent_tensor(j, _):
        k = tensor_peer(j)
        a_copy(a_t_out, a_t_in, a_t_ss, a_t_rs, k, t).wait_send()
        a_copy(a_i_out, a_i_in, a_i_ss, a_i_rs, k, t).wait_send()
        d_copy(grad_t, d_t_ss, d_t_rs, k, t).wait_send()
        d_copy(grad_i, d_i_ss, d_i_rs, k, t).wait_send()
        return 0

    def sent_z(j, _):
        zz = z_peer(j)
        b_t_copy(zz, z).wait_send()
        c_t_copy(zz, z).wait_send()
        return 0

    def sent_column(j, _):
        k = column_peer(j)
        e_copy(e_i_out, e_i_in, e_i_ss, e_i_rs, k, q).wait_send()
        e_copy(e_t_out, e_t_in, e_t_ss, e_t_rs, k, q).wait_send()
        return 0

    def sent_relay(zz, _):
        relay(c, zz).wait_send()
        return 0

    lax.fori_loop(1, TS, sent_tensor, 0)
    lax.fori_loop(1, ZS, sent_z, 0)
    lax.fori_loop(1, PS, sent_column, 0)
    lax.fori_loop(0, ZS, sent_relay, 0)
    for d, h in steps:
        me, line = halves[h][2], halves[h][4]
        ba_copy(h, lax.rem(me + d, XS), me).wait_send()
        cb_copy(h, lax.rem(me + d, XS), me).wait_send()
        for i in range(XS):
            bb_copy(h, i, lax.rem(line + d, XS), line).wait_send()
            ca_copy(h, i, lax.rem(line + d, XS), line).wait_send()
    for b in (0, 1):
        gt_copy(b).wait_send()
    for sent in (pair_copy, g_i_copy, g_t_copy):
        sent.wait_send()


def on_device(image_features, text_features, image_weight, text_weight, image_pair, temp_index, bias_index):
    hbm = pl.BlockSpec(memory_space=pltpu.HBM)
    dma = pltpu.SemaphoreType.DMA
    V = pltpu.VMEM
    i16, i32 = jnp.int16, jnp.int32
    wire = lambda count, rows: V((count, G * rows + 16, 128), i16)
    scratch = (
        [pltpu.SMEM((1,), i32)] * 2
        + [V((DI, 256), bf16), V((DT, 256), bf16), V((DI, E), bf16), V((DT, E), bf16)]
        + [V((TS, R, E), f32)] * 2 + [wire(TS, R)] * 4
        + [V((R, E), f32)] * 2 + [V((R, 1), f32)] * 2
        + [V((PS, H, E), bf16)] * 2 + [V((PS, R, E), bf16)]
        + [V((8, 256), i32)] * 2 + [V((8, PS * R), i32)]
        + [V((PS * R, PS * R), bf16)] + [V((PS, H, E), f32)] * 2 + [V((PS, R, E), f32), V((ZS, R, E), f32)]
        + [wire(PS, H)] * 4 + [V((H, E), f32)] * 2 + [wire(XS, H)] * 4 + [wire(ZS, R)] * 2
        + [V((TS, R, E), bf16)] * 2
        + [V((2, PS, ROWS_I, 128), f32), V((2, PS, ROWS_T, 128), f32)]
        + [V((PS, ROWS_I, 128), f32), V((PS, ROWS_T, 128), f32)]
        + [V((PS, ROWS_I, 128), bf16)] * 2 + [V((PS, ROWS_T, 128), bf16)] * 2
        + [dma((7,))] + [dma((TS,))] * 4 + [dma((2 * XS,))] * 2 + [dma((2 * PS,))] * 2 + [dma((ZS,))] * 4
        + [dma((2 * PS,))] * 2 + [dma((2 * XS,))] * 2 + [dma((2,))] * 2 + [dma((ZS,))] * 2
        + [dma((TS,))] * 4 + [dma((PS,))] * 4 + [dma((3,))] * 2
    )
    grad_image, grad_text = pl.pallas_call(
        kernel,
        out_shape=[jax.ShapeDtypeStruct((OUT, DI), f32), jax.ShapeDtypeStruct((OUT, DT), f32)],
        in_specs=[hbm] * 7,
        out_specs=[pl.BlockSpec(memory_space=pltpu.VMEM)] * 2,
        scratch_shapes=scratch,
        compiler_params=pltpu.CompilerParams(
            collective_id=0, has_side_effects=True, vmem_limit_bytes=56 * 2**20
        ),
        name="pair_loss_grads",
    )(
        temp_index.reshape(1), bias_index.reshape(1), image_pair.reshape(1, 256),
        image_features.T, text_features.T, image_weight, text_weight,
    )
    return grad_image.T, grad_text.T


def solution(mesh):
    return jax.shard_map(
        on_device,
        mesh=mesh,
        in_specs=(P("dp", "tensor"), P("dp", "tensor"), P("tensor", None), P("tensor", None), P("dp"), P(), P()),
        out_specs=(P("tensor", "dp"), P("tensor", "dp")),
        check_vma=False,
    )
```

```python
import jax
import jax.numpy as jnp
from jax import lax
from jax.experimental import pallas as pl
from jax.experimental.pallas import tpu as pltpu
from jax.sharding import PartitionSpec as P

MESH = pl.DeviceIdType.MESH
E = 1152
DI = 176
DT = 144
R = 32
TS = 8
ZS = 8
PS = 16
OUT = 36
XS = 4
H = 16
ROWS_I = 64
ROWS_T = 48
LEVELS = 32000.0
G = E // 128
f32 = jnp.float32
bf16 = jnp.bfloat16


def put(wire, k, x, n):
    m = jnp.max(jnp.abs(x), axis=1, keepdims=True)
    hi = jnp.floor(m)
    lo = jnp.floor((m - hi) * LEVELS) + 1.0
    q = jnp.round(x * (LEVELS / (hi + lo * (1.0 / LEVELS)))).astype(jnp.int32).astype(jnp.int16)
    for i in range(x.shape[0] // n):
        rows = slice(i * n, (i + 1) * n)
        for g in range(G):
            wire[k + i, g * n:(g + 1) * n, :] = q[rows, g * 128:(g + 1) * 128]
        diagonal = lax.broadcasted_iota(jnp.int32, (n, 128), 0) == lax.broadcasted_iota(jnp.int32, (n, 128), 1)
        his = jnp.sum(jnp.where(diagonal, hi[rows], 0.0), axis=0, keepdims=True)
        los = jnp.sum(jnp.where(diagonal, lo[rows], 0.0), axis=0, keepdims=True)
        row = lax.broadcasted_iota(jnp.int32, (16, 128), 0)
        wire[k + i, G * n:G * n + 16, :] = (
            jnp.where(row == 0, his, jnp.where(row == 1, los, 0.0)).astype(jnp.int32).astype(jnp.int16)
        )


def take(wire, k, n):
    code = wire[k, G * n:G * n + 16, :].astype(jnp.int32).astype(f32)
    top = code[0:1, :] + code[1:2, :] * (1.0 / LEVELS)
    diagonal = lax.broadcasted_iota(jnp.int32, (n, 128), 0) == lax.broadcasted_iota(jnp.int32, (n, 128), 1)
    step = jnp.sum(jnp.where(diagonal, top, 0.0), axis=1, keepdims=True) * (1.0 / LEVELS)
    return jnp.concatenate(
        [wire[k, g * n:(g + 1) * n, :].astype(jnp.int32).astype(f32) * step for g in range(G)], axis=1
    )


def unit_rows(values):
    norm = jnp.sqrt(jnp.sum(values * values, axis=1, keepdims=True) + 1e-06)
    return norm, values / norm


def back_rows(direct, norm, grad):
    inner = jnp.sum(direct * grad, axis=1, keepdims=True)
    return ((grad - direct * inner) / norm).astype(bf16)


def kernel(
    temp_hbm, bias_hbm, pair_hbm, fi_hbm, ft_hbm, wi_hbm, wt_hbm, out_i, out_t,
    temp_ref, bias_ref,
    fi_ref, ft_ref, wi_ref, wt_ref,
    part_i, part_t, a_i_out, a_i_in, a_t_out, a_t_in,
    dir_i, dir_t, norm_i, norm_t, unit_0, unit_1, all_t, pair_out, pair_in, target_ref,
    w_ref, gi_0, gi_1, gt, gt_sib, ca_out_0, ca_in_0, ca_out_1, ca_in_1,
    half_0, half_1, cb_out_0, cb_in_0, cb_out_1, cb_in_1, c_t_out, c_t_in,
    grad_i, grad_t, g_i, g_t, sib_i, sib_t, e_i_out, e_i_in, e_t_out, e_t_in,
    load_s, a_i_ss, a_i_rs, a_t_ss, a_t_rs, ba_ss, ba_rs, bb_ss, bb_rs, b_t_ss, b_t_rs, relay_ss, relay_rs,
    ca_ss, ca_rs, cb_ss, cb_rs, gt_ss, gt_rs, c_t_ss, c_t_rs, d_i_ss, d_i_rs, d_t_ss, d_t_rs,
    e_i_ss, e_i_rs, e_t_ss, e_t_rs, one_ss, one_rs,
):
    loads = [
        pltpu.make_async_copy(src, dst, load_s.at[k])
        for k, (src, dst) in enumerate((
            (ft_hbm, ft_ref), (wt_hbm, wt_ref), (fi_hbm, fi_ref), (wi_hbm, wi_ref), (pair_hbm, pair_out.at[0:1]),
            (temp_hbm, temp_ref), (bias_hbm, bias_ref),
        ))
    ]
    for load in loads:
        load.start()

    dp = lax.axis_index("dp")
    t = lax.axis_index("tensor")
    ylo = lax.div(dp, 16)
    z = lax.rem(lax.div(dp, 2), 8)
    c = lax.rem(dp, 2)
    oc = 1 - c
    yhi = lax.div(t, XS)
    x = lax.rem(t, XS)
    y = yhi * 2 + ylo
    q = ylo * ZS + z

    def device(ylo_, z_, c_, t_):
        return ((ylo_ * ZS + z_) * 2 + c_, t_)

    sibling = device(ylo, z, oc, t)
    across = device(1 - ylo, z, c, t)
    beyond = device(1 - ylo, z, c, (1 - yhi) * XS + x)

    def at_x(xx):
        return (dp, yhi * XS + xx)

    def at_y(yy):
        return device(lax.rem(yy, 2), z, c, lax.div(yy, 2) * XS + x)

    def column(k):
        return device(lax.div(k, ZS), lax.rem(k, ZS), c, t)

    def tensor_peer(j):
        j = lax.rem(j * 5, TS)
        return lax.rem(yhi + lax.div(j, XS), 2) * XS + lax.rem(x + lax.rem(j, XS), XS)

    def z_step(n):
        m = lax.div(n + 1, 2)
        return lax.rem(4 + m * (1 - 2 * lax.rem(n, 2)) + ZS, ZS)

    def z_peer(j):
        return lax.rem(z + z_step(j - 1), ZS)

    def column_peer(j):
        n = j - 1
        return lax.rem(ylo + 1 - lax.rem(n, 2), 2) * ZS + lax.rem(z + z_step(lax.div(n, 2)), ZS)

    def copy(src, dst, ssem, rsem, dev):
        return pltpu.make_async_remote_copy(
            src_ref=src, dst_ref=dst, send_sem=ssem, recv_sem=rsem, device_id=dev, device_id_type=MESH
        )

    barrier = pltpu.get_barrier_semaphore()

    def greet(dev):
        pl.semaphore_signal(barrier, inc=1, device_id=dev, device_id_type=MESH)

    def greet_tensor(j, _):
        greet((dp, tensor_peer(j)))
        return 0

    def greet_column(j, _):
        greet(column(column_peer(j)))
        return 0

    lax.fori_loop(1, TS, greet_tensor, 0)
    lax.fori_loop(1, PS, greet_column, 0)
    greet(beyond)
    greet(sibling)

    def product(feat, weight):
        return lax.dot_general(
            feat[...], weight[...], (((0,), (0,)), ((), ())), preferred_element_type=f32
        ).reshape(TS, R, E)

    g_i[...] = jnp.zeros_like(g_i)
    g_t[...] = jnp.zeros_like(g_t)
    loads[0].wait()
    loads[1].wait()
    part_t[...] = product(ft_ref, wt_ref)
    loads[4].wait()
    pair_out[...] = jnp.broadcast_to(pair_out[0:1, :], (8, 256))
    pl.semaphore_wait(barrier, (TS - 1) + (PS - 1) + 2)

    def a_copy(wire_out, wire_in, ss, rs, k, slot):
        return copy(wire_out.at[k], wire_in.at[slot], ss.at[k], rs.at[slot], (dp, k))

    def a_send(part, wire_out, wire_in, ss, rs):
        for hi in (1 - yhi, yhi):
            put(wire_out, hi * XS, part[pl.ds(hi * XS, XS)].reshape(XS * R, E), R)
            for d in (2, 1, 3) if hi is yhi else (2, 1, 3, 0):
                a_copy(wire_out, wire_in, ss, rs, hi * XS + lax.rem(x + d, XS), t).start()

    def a_take(part, wire_out, wire_in, ss, rs):
        def step(j, total):
            k = tensor_peer(TS - j)
            a_copy(wire_out, wire_in, ss, rs, k, k).wait_recv()
            return total + take(wire_in, k, R)
        return lax.fori_loop(1, TS, step, part[t])

    a_send(part_t, a_t_out, a_t_in, a_t_ss, a_t_rs)
    pair_copy = copy(pair_out, pair_in, one_ss.at[0], one_rs.at[0], across)
    pair_copy.start()
    loads[2].wait()
    loads[3].wait()
    part_i[...] = product(fi_ref, wi_ref)
    a_send(part_i, a_i_out, a_i_in, a_i_ss, a_i_rs)

    def local_target(pair):
        r = pair & 31
        tt = (pair >> 5) & 7
        cc = (pair >> 8) & 1
        zz = (pair >> 9) & 7
        yy = (pair >> 12) & 1
        here = jnp.logical_and(tt == t, yy == ylo)
        return jnp.where(here, (cc * ZS + zz) * R + r, -1)

    pair_copy.wait_recv()
    own = local_target(pair_out[0:1, :])
    other = local_target(pair_in[0:1, :])
    by_ylo = (jnp.where(ylo == 0, own, other), jnp.where(ylo == 0, other, own))
    for yy in range(XS):
        for xx in range(XS):
            lane = ((yy // 2) * XS + xx) * R
            s0, s1 = (yy * XS + xx) * H, (xx * XS + yy) * H + PS * H
            target_ref[0:1, s0:s0 + H] = by_ylo[yy % 2][:, lane:lane + H]
            target_ref[0:1, s1:s1 + H] = by_ylo[yy % 2][:, lane + H:lane + R]

    def b_t_copy(zz, slot):
        s = c * ZS + slot
        return copy(all_t.at[s], all_t.at[s], b_t_ss.at[zz], b_t_rs.at[slot], device(ylo, zz, c, t))

    def relay(cc, zz):
        s = cc * ZS + zz
        return copy(all_t.at[s], all_t.at[s], relay_ss.at[zz], relay_rs.at[zz], sibling)

    norm, direct = unit_rows(a_take(part_t, a_t_out, a_t_in, a_t_ss, a_t_rs))
    norm_t[...] = norm
    dir_t[...] = direct
    all_t[c * ZS + z] = direct.astype(bf16)

    def b_t_send(j, _):
        b_t_copy(z_peer(j), z).start()
        return 0

    lax.fori_loop(1, ZS, b_t_send, 0)
    relay(c, z).start()

    halves = ((unit_0, at_x, x, at_y, y), (unit_1, at_y, y, at_x, x))

    def ba_copy(h, k, slot):
        unit, first, me, second, line = halves[h]
        s = line * XS + slot
        return copy(unit.at[s], unit.at[s], ba_ss.at[h * XS + k], ba_rs.at[h * XS + slot], first(k))

    def bb_copy(h, i, k, slot):
        unit, first, me, second, line = halves[h]
        s = slot * XS + i
        return copy(unit.at[s], unit.at[s], bb_ss.at[h * PS + k * XS + i], bb_rs.at[h * PS + s], second(k))

    norm, direct = unit_rows(a_take(part_i, a_i_out, a_i_in, a_i_ss, a_i_rs))
    norm_i[...] = norm
    dir_i[...] = direct
    unit = direct.astype(bf16)
    unit_0[y * XS + x] = unit[0:H]
    unit_1[x * XS + y] = unit[H:R]
    steps = [(d, h) for d in (2, 1, 3) for h in (0, 1)]
    for d, h in steps:
        me = halves[h][2]
        ba_copy(h, lax.rem(me + d, XS), me).start()

    def bb_send(h, i):
        line = halves[h][4]
        for d in (2, 1, 3):
            bb_copy(h, i, lax.rem(line + d, XS), line).start()

    for h in (0, 1):
        bb_send(h, halves[h][2])
    for d in (1, 3, 2):
        for h in (0, 1):
            k = lax.rem(halves[h][2] + d, XS)
            ba_copy(h, k, k).wait_recv()
            bb_send(h, k)

    def b_t_take(j, _):
        zz = z_peer(j)
        b_t_copy(zz, zz).wait_recv()
        relay(c, zz).start()
        return 0

    lax.fori_loop(1, ZS, b_t_take, 0)

    def relay_take(zz, _):
        relay(oc, zz).wait_recv()
        return 0

    lax.fori_loop(0, ZS, relay_take, 0)
    for d, h in steps:
        k = lax.rem(halves[h][4] + d, XS)
        for i in range(XS):
            bb_copy(h, i, k, k).wait_recv()

    loads[5].wait()
    loads[6].wait()
    scale = 4.0 + temp_ref[0].astype(f32)
    shift = -0.5 * bias_ref[0].astype(f32)
    half = PS * H

    def tile_weights(b, _):
        rows = all_t[pl.ds(b * 4, 4)].reshape(4 * R, E)
        for h, unit in ((0, unit_0), (1, unit_1)):
            logits = scale * lax.dot_general(
                rows, unit[...].reshape(half, E), (((1,), (1,)), ((), ())), preferred_element_type=f32
            ) + shift
            index = lax.broadcasted_iota(jnp.int32, (4 * R, half), 0) + b * (4 * R)
            sign = jnp.where(index == target_ref[0:1, h * half:(h + 1) * half], f32(1.0), f32(-1.0))
            w = (-scale * sign * jax.nn.sigmoid(-sign * logits)).astype(bf16)
            w_ref[pl.ds(pl.multiple_of(b * (4 * R), 4 * R), 4 * R), h * half:(h + 1) * half] = w
        return 0

    lax.fori_loop(0, 4, tile_weights, 0)

    back = ((gi_0, ca_out_0, ca_in_0, half_0, cb_out_0, cb_in_0), (gi_1, ca_out_1, ca_in_1, half_1, cb_out_1, cb_in_1))

    def ca_copy(h, i, k, slot):
        out, into = back[h][1], back[h][2]
        return copy(
            out.at[k * XS + i], into.at[slot * XS + i],
            ca_ss.at[h * PS + k * XS + i], ca_rs.at[h * PS + slot * XS + i], halves[h][3](k),
        )

    def cb_copy(h, k, slot):
        out, into = back[h][4], back[h][5]
        return copy(out.at[k], into.at[slot], cb_ss.at[h * XS + k], cb_rs.at[h * XS + slot], halves[h][1](k))

    for h in (0, 1):
        gi = back[h][0]
        for b in range(2):
            lane = h * half + b * 128
            gi[8 * b:8 * b + 8] = lax.dot_general(
                w_ref[:, lane:lane + 128], all_t[...].reshape(PS * R, E), (((0,), (0,)), ((), ())),
                preferred_element_type=f32,
            ).reshape(8, H, E)

        out, me, line = back[h][1], halves[h][2], halves[h][4]
        for d in (2, 1, 3):
            k = lax.rem(line + d, XS)
            put(out, k * XS, gi[pl.ds(k * XS, XS)].reshape(XS * H, E), H)
            for e in (2, 1, 3):
                ca_copy(h, lax.rem(me + e, XS), k, line).start()
    for d, h in steps:
        me, line = halves[h][2], halves[h][4]
        ca_copy(h, me, lax.rem(line + d, XS), line).start()

    def tile_text(b):
        w = w_ref.at[pl.ds(pl.multiple_of(b * (4 * R), 4 * R), 4 * R)]
        total = jnp.dot(w[:, 0:half], unit_0[...].reshape(half, E), preferred_element_type=f32)
        total = total + jnp.dot(w[:, half:], unit_1[...].reshape(half, E), preferred_element_type=f32)
        gt[pl.ds(b * 4, 4)] = total.reshape(4, R, E)

    def gt_copy(b):
        return copy(
            gt.at[pl.ds(oc * ZS + b * 4, 4)], gt_sib.at[pl.ds(b * 4, 4)], gt_ss.at[b], gt_rs.at[b], sibling
        )

    def tile_other(b, _):
        tile_text(2 * oc + b)
        gt_copy(b).start()
        return 0

    def c_t_copy(zz, slot):
        return copy(c_t_out.at[zz], c_t_in.at[slot], c_t_ss.at[zz], c_t_rs.at[slot], device(ylo, zz, c, t))

    def tile_own(b, _):
        tile_text(2 * c + b)
        gt_copy(b).wait_recv()
        rows = gt[pl.ds(c * ZS + b * 4, 4)] + gt_sib[pl.ds(b * 4, 4)]
        gt[pl.ds(c * ZS + b * 4, 4)] = rows
        put(c_t_out, b * 4, rows.reshape(4 * R, E), R)
        for n in range(4):
            zz = b * 4 + n

            @pl.when(zz != z)
            def _(zz=zz):
                c_t_copy(zz, z).start()
        return 0

    lax.fori_loop(0, 2, tile_other, 0)
    lax.fori_loop(0, 2, tile_own, 0)

    for h in (0, 1):
        gi, into, part, out = back[h][0], back[h][2], back[h][3], back[h][4]
        me, line = halves[h][2], halves[h][4]
        for e in (1, 2, 3, 0):
            i = lax.rem(me + e, XS)
            total = gi[line * XS + i]
            for d in (1, 3, 2):
                k = lax.rem(line + d, XS)
                ca_copy(h, i, k, k).wait_recv()
                total = total + take(into, k * XS + i, H)
            if e:
                put(out, i, total, H)
                cb_copy(h, i, me).start()
            else:
                part[...] = total

    def c_i_take(h):
        into, part, me = back[h][5], back[h][3], halves[h][2]
        total = part[...]
        for d in (1, 3, 2):
            k = lax.rem(me + d, XS)
            cb_copy(h, k, k).wait_recv()
            total = total + take(into, k, H)
        return total

    def c_t_take(j, total):
        zz = z_peer(j)
        c_t_copy(zz, zz).wait_recv()
        return total + take(c_t_in, zz, R)

    def d_copy(grad, ss, rs, k, slot):
        return copy(grad.at[slot], grad.at[slot], ss.at[k], rs.at[slot], (dp, k))

    def d_send(grad, ss, rs):
        def step(j, _):
            d_copy(grad, ss, rs, tensor_peer(j), t).start()
            return 0
        lax.fori_loop(1, TS, step, 0)

    def d_take(grad, ss, rs):
        def step(j, _):
            k = tensor_peer(TS - j)
            d_copy(grad, ss, rs, k, k).wait_recv()
            return 0
        lax.fori_loop(1, TS, step, 0)

    total = jnp.concatenate([c_i_take(0), c_i_take(1)], axis=0)
    grad_i[t] = back_rows(dir_i[...], norm_i[...], total)
    d_send(grad_i, d_i_ss, d_i_rs)
    total = lax.fori_loop(1, ZS, c_t_take, gt[c * ZS + z])
    grad_t[t] = back_rows(dir_t[...], norm_t[...], total)
    d_send(grad_t, d_t_ss, d_t_rs)

    def weight_grad(grad, feat, packed, fold):
        g = lax.dot_general(
            grad[...].reshape(TS * R, E), feat[...], (((0,), (1,)), ((), ())), preferred_element_type=f32
        )
        rest, rows = g.shape[1] - 128, OUT // fold
        for k in range(2 * PS):
            packed[k % 2, k // 2, 0:OUT, :] = g[k * OUT:(k + 1) * OUT, 0:128]
            for n in range(fold):
                packed[k % 2, k // 2, OUT:OUT + rows, n * rest:(n + 1) * rest] = (
                    g[k * OUT + n * rows:k * OUT + (n + 1) * rows, 128:]
                )

    def e_copy(out, into, ss, rs, k, slot):
        return copy(out.at[k], into.at[slot], ss.at[k], rs.at[slot], column(k))

    def e_send(packed, sib, out, into, ss, rs):
        def step(j, _):
            k = column_peer(j)
            out[k] = (packed[c, k] + sib[k]).astype(bf16)
            e_copy(out, into, ss, rs, k, q).start()
            return 0
        lax.fori_loop(1, PS, step, 0)

    def e_take(packed, sib, out, into, ss, rs):
        def step(j, total):
            k = column_peer(j)
            e_copy(out, into, ss, rs, k, k).wait_recv()
            return total + into[k].astype(f32)
        return lax.fori_loop(1, PS, step, packed[c, q] + sib[q])

    e_i = (g_i, sib_i, e_i_out, e_i_in, e_i_ss, e_i_rs)
    e_t = (g_t, sib_t, e_t_out, e_t_in, e_t_ss, e_t_rs)
    d_take(grad_i, d_i_ss, d_i_rs)
    weight_grad(grad_i, fi_ref, g_i, 2)
    g_i_copy = copy(g_i.at[oc], sib_i, one_ss.at[1], one_rs.at[1], sibling)
    g_i_copy.start()
    g_i_copy.wait_recv()
    e_send(*e_i)
    d_take(grad_t, d_t_ss, d_t_rs)
    weight_grad(grad_t, ft_ref, g_t, 3)
    g_t_copy = copy(g_t.at[oc], sib_t, one_ss.at[2], one_rs.at[2], sibling)
    g_t_copy.start()
    g_t_copy.wait_recv()
    e_send(*e_t)

    def unpack(total, out, width, fold):
        rest, rows = width - 128, OUT // fold
        out[:, 0:128] = total[0:OUT, :]
        for n in range(fold):
            out[n * rows:(n + 1) * rows, 128:width] = (
                total[OUT:OUT + rows, n * rest:(n + 1) * rest]
            )

    unpack(e_take(*e_i), out_i, DI, 2)
    unpack(e_take(*e_t), out_t, DT, 3)

    def sent_tensor(j, _):
        k = tensor_peer(j)
        a_copy(a_t_out, a_t_in, a_t_ss, a_t_rs, k, t).wait_send()
        a_copy(a_i_out, a_i_in, a_i_ss, a_i_rs, k, t).wait_send()
        d_copy(grad_t, d_t_ss, d_t_rs, k, t).wait_send()
        d_copy(grad_i, d_i_ss, d_i_rs, k, t).wait_send()
        return 0

    def sent_z(j, _):
        zz = z_peer(j)
        b_t_copy(zz, z).wait_send()
        c_t_copy(zz, z).wait_send()
        return 0

    def sent_column(j, _):
        k = column_peer(j)
        e_copy(e_i_out, e_i_in, e_i_ss, e_i_rs, k, q).wait_send()
        e_copy(e_t_out, e_t_in, e_t_ss, e_t_rs, k, q).wait_send()
        return 0

    def sent_relay(zz, _):
        relay(c, zz).wait_send()
        return 0

    lax.fori_loop(1, TS, sent_tensor, 0)
    lax.fori_loop(1, ZS, sent_z, 0)
    lax.fori_loop(1, PS, sent_column, 0)
    lax.fori_loop(0, ZS, sent_relay, 0)
    for d, h in steps:
        me, line = halves[h][2], halves[h][4]
        ba_copy(h, lax.rem(me + d, XS), me).wait_send()
        cb_copy(h, lax.rem(me + d, XS), me).wait_send()
        for i in range(XS):
            bb_copy(h, i, lax.rem(line + d, XS), line).wait_send()
            ca_copy(h, i, lax.rem(line + d, XS), line).wait_send()
    for b in (0, 1):
        gt_copy(b).wait_send()
    for sent in (pair_copy, g_i_copy, g_t_copy):
        sent.wait_send()


def on_device(image_features, text_features, image_weight, text_weight, image_pair, temp_index, bias_index):
    hbm = pl.BlockSpec(memory_space=pltpu.HBM)
    dma = pltpu.SemaphoreType.DMA
    V = pltpu.VMEM
    i16, i32 = jnp.int16, jnp.int32
    wire = lambda count, rows: V((count, G * rows + 16, 128), i16)
    scratch = (
        [pltpu.SMEM((1,), i32)] * 2
        + [V((DI, 256), bf16), V((DT, 256), bf16), V((DI, E), bf16), V((DT, E), bf16)]
        + [V((TS, R, E), f32)] * 2 + [wire(TS, R)] * 4
        + [V((R, E), f32)] * 2 + [V((R, 1), f32)] * 2
        + [V((PS, H, E), bf16)] * 2 + [V((PS, R, E), bf16)]
        + [V((8, 256), i32)] * 2 + [V((8, PS * R), i32)]
        + [V((PS * R, PS * R), bf16)] + [V((PS, H, E), f32)] * 2 + [V((PS, R, E), f32), V((ZS, R, E), f32)]
        + [wire(PS, H)] * 4 + [V((H, E), f32)] * 2 + [wire(XS, H)] * 4 + [wire(ZS, R)] * 2
        + [V((TS, R, E), bf16)] * 2
        + [V((2, PS, ROWS_I, 128), f32), V((2, PS, ROWS_T, 128), f32)]
        + [V((PS, ROWS_I, 128), f32), V((PS, ROWS_T, 128), f32)]
        + [V((PS, ROWS_I, 128), bf16)] * 2 + [V((PS, ROWS_T, 128), bf16)] * 2
        + [dma((7,))] + [dma((TS,))] * 4 + [dma((2 * XS,))] * 2 + [dma((2 * PS,))] * 2 + [dma((ZS,))] * 4
        + [dma((2 * PS,))] * 2 + [dma((2 * XS,))] * 2 + [dma((2,))] * 2 + [dma((ZS,))] * 2
        + [dma((TS,))] * 4 + [dma((PS,))] * 4 + [dma((3,))] * 2
    )
    grad_image, grad_text = pl.pallas_call(
        kernel,
        out_shape=[jax.ShapeDtypeStruct((OUT, DI), f32), jax.ShapeDtypeStruct((OUT, DT), f32)],
        in_specs=[hbm] * 7,
        out_specs=[pl.BlockSpec(memory_space=pltpu.VMEM)] * 2,
        scratch_shapes=scratch,
        compiler_params=pltpu.CompilerParams(
            collective_id=0, has_side_effects=True, vmem_limit_bytes=56430000
        ),
        name="pair_loss_grads",
    )(
        temp_index.reshape(1), bias_index.reshape(1), image_pair.reshape(1, 256),
        image_features.T, text_features.T, image_weight, text_weight,
    )
    return grad_image.T, grad_text.T


def solution(mesh):
    return jax.shard_map(
        on_device,
        mesh=mesh,
        in_specs=(P("dp", "tensor"), P("dp", "tensor"), P("tensor", None), P("tensor", None), P("dp"), P(), P()),
        out_specs=(P("tensor", "dp"), P("tensor", "dp")),
        check_vma=False,
    )
```

```python
import jax
import jax.numpy as jnp
from jax import lax
from jax.experimental import pallas as pl
from jax.experimental.pallas import tpu as pltpu
from jax.sharding import PartitionSpec as P

MESH = pl.DeviceIdType.MESH
E = 1152
DI = 176
DT = 144
R = 32
TS = 8
ZS = 8
PS = 16
OUT = 36
XS = 4
H = 16
ROWS_I = 64
ROWS_T = 48
LEVELS = 32000.0
G = E // 128
f32 = jnp.float32
bf16 = jnp.bfloat16


def put(wire, k, x, n):
    m = jnp.max(jnp.abs(x), axis=1, keepdims=True)
    hi = jnp.floor(m)
    lo = jnp.floor((m - hi) * LEVELS) + 1.0
    q = jnp.round(x * (LEVELS / (hi + lo * (1.0 / LEVELS)))).astype(jnp.int32).astype(jnp.int16)
    for i in range(x.shape[0] // n):
        rows = slice(i * n, (i + 1) * n)
        for g in range(G):
            wire[k + i, g * n:(g + 1) * n, :] = q[rows, g * 128:(g + 1) * 128]
        diagonal = lax.broadcasted_iota(jnp.int32, (n, 128), 0) == lax.broadcasted_iota(jnp.int32, (n, 128), 1)
        his = jnp.sum(jnp.where(diagonal, hi[rows], 0.0), axis=0, keepdims=True)
        los = jnp.sum(jnp.where(diagonal, lo[rows], 0.0), axis=0, keepdims=True)
        row = lax.broadcasted_iota(jnp.int32, (16, 128), 0)
        wire[k + i, G * n:G * n + 16, :] = (
            jnp.where(row == 0, his, jnp.where(row == 1, los, 0.0)).astype(jnp.int32).astype(jnp.int16)
        )


def take(wire, k, n):
    code = wire[k, G * n:G * n + 16, :].astype(jnp.int32).astype(f32)
    top = code[0:1, :] + code[1:2, :] * (1.0 / LEVELS)
    diagonal = lax.broadcasted_iota(jnp.int32, (n, 128), 0) == lax.broadcasted_iota(jnp.int32, (n, 128), 1)
    step = jnp.sum(jnp.where(diagonal, top, 0.0), axis=1, keepdims=True) * (1.0 / LEVELS)
    return jnp.concatenate(
        [wire[k, g * n:(g + 1) * n, :].astype(jnp.int32).astype(f32) * step for g in range(G)], axis=1
    )


def unit_rows(values):
    norm = jnp.sqrt(jnp.sum(values * values, axis=1, keepdims=True) + 1e-06)
    return norm, values / norm


def back_rows(direct, norm, grad):
    inner = jnp.sum(direct * grad, axis=1, keepdims=True)
    return ((grad - direct * inner) / norm).astype(bf16)


def kernel(
    temp_hbm, bias_hbm, pair_hbm, fi_hbm, ft_hbm, wi_hbm, wt_hbm, out_i, out_t,
    temp_ref, bias_ref,
    fi_ref, ft_ref, wi_ref, wt_ref,
    part_i, part_t, a_i_out, a_i_in, a_t_out, a_t_in,
    dir_i, dir_t, norm_i, norm_t, unit_0, unit_1, all_t, pair_out, pair_in, target_ref,
    w_ref, gi_0, gi_1, gt, gt_sib, ca_out_0, ca_in_0, ca_out_1, ca_in_1,
    half_0, half_1, cb_out_0, cb_in_0, cb_out_1, cb_in_1, co_out_0, co_in_0, co_out_1, co_in_1, c_t_out, c_t_in,
    grad_i, grad_t, g_i, g_t, sib_i, sib_t, e_i_out, e_i_in, e_t_out, e_t_in,
    load_s, a_i_ss, a_i_rs, a_t_ss, a_t_rs, ba_ss, ba_rs, bb_ss, bb_rs, b_t_ss, b_t_rs, relay_ss, relay_rs,
    ca_ss, ca_rs, co_ss, co_rs, cb_ss, cb_rs, gt_ss, gt_rs, c_t_ss, c_t_rs, d_i_ss, d_i_rs, d_t_ss, d_t_rs,
    e_i_ss, e_i_rs, e_t_ss, e_t_rs, one_ss, one_rs,
):
    loads = [
        pltpu.make_async_copy(src, dst, load_s.at[k])
        for k, (src, dst) in enumerate((
            (ft_hbm, ft_ref), (wt_hbm, wt_ref), (fi_hbm, fi_ref), (wi_hbm, wi_ref), (pair_hbm, pair_out.at[0:1]),
            (temp_hbm, temp_ref), (bias_hbm, bias_ref),
        ))
    ]
    for load in loads:
        load.start()

    dp = lax.axis_index("dp")
    t = lax.axis_index("tensor")
    ylo = lax.div(dp, 16)
    z = lax.rem(lax.div(dp, 2), 8)
    c = lax.rem(dp, 2)
    oc = 1 - c
    yhi = lax.div(t, XS)
    x = lax.rem(t, XS)
    y = yhi * 2 + ylo
    q = ylo * ZS + z

    def device(ylo_, z_, c_, t_):
        return ((ylo_ * ZS + z_) * 2 + c_, t_)

    sibling = device(ylo, z, oc, t)
    across = device(1 - ylo, z, c, t)
    beyond = device(1 - ylo, z, c, (1 - yhi) * XS + x)

    def at_x(xx):
        return (dp, yhi * XS + xx)

    def at_y(yy):
        return device(lax.rem(yy, 2), z, c, lax.div(yy, 2) * XS + x)

    def column(k):
        return device(lax.div(k, ZS), lax.rem(k, ZS), c, t)

    def tensor_peer(j):
        j = lax.rem(j * 5, TS)
        return lax.rem(yhi + lax.div(j, XS), 2) * XS + lax.rem(x + lax.rem(j, XS), XS)

    def z_step(n):
        m = lax.div(n + 1, 2)
        return lax.rem(4 + m * (1 - 2 * lax.rem(n, 2)) + ZS, ZS)

    def z_peer(j):
        return lax.rem(z + z_step(j - 1), ZS)

    def column_peer(j):
        n = j - 1
        return lax.rem(ylo + 1 - lax.rem(n, 2), 2) * ZS + lax.rem(z + z_step(lax.div(n, 2)), ZS)

    def copy(src, dst, ssem, rsem, dev):
        return pltpu.make_async_remote_copy(
            src_ref=src, dst_ref=dst, send_sem=ssem, recv_sem=rsem, device_id=dev, device_id_type=MESH
        )

    barrier = pltpu.get_barrier_semaphore()

    def greet(dev):
        pl.semaphore_signal(barrier, inc=1, device_id=dev, device_id_type=MESH)

    def greet_tensor(j, _):
        greet((dp, tensor_peer(j)))
        return 0

    def greet_column(j, _):
        greet(column(column_peer(j)))
        return 0

    lax.fori_loop(1, TS, greet_tensor, 0)
    lax.fori_loop(1, PS, greet_column, 0)
    greet(beyond)
    greet(sibling)

    def product(feat, weight):
        return lax.dot_general(
            feat[...], weight[...], (((0,), (0,)), ((), ())), preferred_element_type=f32
        ).reshape(TS, R, E)

    g_i[...] = jnp.zeros_like(g_i)
    g_t[...] = jnp.zeros_like(g_t)
    loads[0].wait()
    loads[1].wait()
    part_t[...] = product(ft_ref, wt_ref)
    loads[4].wait()
    pair_out[...] = jnp.broadcast_to(pair_out[0:1, :], (8, 256))
    pl.semaphore_wait(barrier, (TS - 1) + (PS - 1) + 2)

    def a_copy(wire_out, wire_in, ss, rs, k, slot):
        return copy(wire_out.at[k], wire_in.at[slot], ss.at[k], rs.at[slot], (dp, k))

    def a_send(part, wire_out, wire_in, ss, rs):
        for hi in (1 - yhi, yhi):
            put(wire_out, hi * XS, part[pl.ds(hi * XS, XS)].reshape(XS * R, E), R)
            for d in (2, 1, 3) if hi is yhi else (2, 1, 3, 0):
                a_copy(wire_out, wire_in, ss, rs, hi * XS + lax.rem(x + d, XS), t).start()

    def a_take(part, wire_out, wire_in, ss, rs):
        def step(j, total):
            k = tensor_peer(TS - j)
            a_copy(wire_out, wire_in, ss, rs, k, k).wait_recv()
            return total + take(wire_in, k, R)
        return lax.fori_loop(1, TS, step, part[t])

    a_send(part_t, a_t_out, a_t_in, a_t_ss, a_t_rs)
    pair_copy = copy(pair_out, pair_in, one_ss.at[0], one_rs.at[0], across)
    pair_copy.start()
    loads[2].wait()
    loads[3].wait()
    part_i[...] = product(fi_ref, wi_ref)
    a_send(part_i, a_i_out, a_i_in, a_i_ss, a_i_rs)

    def local_target(pair):
        r = pair & 31
        tt = (pair >> 5) & 7
        cc = (pair >> 8) & 1
        zz = (pair >> 9) & 7
        yy = (pair >> 12) & 1
        here = jnp.logical_and(tt == t, yy == ylo)
        return jnp.where(here, (cc * ZS + zz) * R + r, -1)

    pair_copy.wait_recv()
    own = local_target(pair_out[0:1, :])
    other = local_target(pair_in[0:1, :])
    by_ylo = (jnp.where(ylo == 0, own, other), jnp.where(ylo == 0, other, own))
    for yy in range(XS):
        for xx in range(XS):
            lane = ((yy // 2) * XS + xx) * R
            s0, s1 = (yy * XS + xx) * H, (xx * XS + yy) * H + PS * H
            target_ref[0:1, s0:s0 + H] = by_ylo[yy % 2][:, lane:lane + H]
            target_ref[0:1, s1:s1 + H] = by_ylo[yy % 2][:, lane + H:lane + R]

    def b_t_copy(zz, slot):
        s = c * ZS + slot
        return copy(all_t.at[s], all_t.at[s], b_t_ss.at[zz], b_t_rs.at[slot], device(ylo, zz, c, t))

    def relay(cc, zz):
        s = cc * ZS + zz
        return copy(all_t.at[s], all_t.at[s], relay_ss.at[zz], relay_rs.at[zz], sibling)

    norm, direct = unit_rows(a_take(part_t, a_t_out, a_t_in, a_t_ss, a_t_rs))
    norm_t[...] = norm
    dir_t[...] = direct
    all_t[c * ZS + z] = direct.astype(bf16)

    def b_t_send(j, _):
        b_t_copy(z_peer(j), z).start()
        return 0

    lax.fori_loop(1, ZS, b_t_send, 0)
    relay(c, z).start()

    halves = ((unit_0, at_x, x, at_y, y), (unit_1, at_y, y, at_x, x))

    def ba_copy(h, k, slot):
        unit, first, me, second, line = halves[h]
        s = line * XS + slot
        return copy(unit.at[s], unit.at[s], ba_ss.at[h * XS + k], ba_rs.at[h * XS + slot], first(k))

    def bb_copy(h, i, k, slot):
        unit, first, me, second, line = halves[h]
        s = slot * XS + i
        return copy(unit.at[s], unit.at[s], bb_ss.at[h * PS + k * XS + i], bb_rs.at[h * PS + s], second(k))

    norm, direct = unit_rows(a_take(part_i, a_i_out, a_i_in, a_i_ss, a_i_rs))
    norm_i[...] = norm
    dir_i[...] = direct
    unit = direct.astype(bf16)
    unit_0[y * XS + x] = unit[0:H]
    unit_1[x * XS + y] = unit[H:R]
    steps = [(d, h) for d in (2, 1, 3) for h in (0, 1)]
    for d, h in steps:
        me = halves[h][2]
        ba_copy(h, lax.rem(me + d, XS), me).start()

    def bb_send(h, i):
        line = halves[h][4]
        for d in (2, 1, 3):
            bb_copy(h, i, lax.rem(line + d, XS), line).start()

    for h in (0, 1):
        bb_send(h, halves[h][2])
    for d in (1, 3, 2):
        for h in (0, 1):
            k = lax.rem(halves[h][2] + d, XS)
            ba_copy(h, k, k).wait_recv()
            bb_send(h, k)

    def b_t_take(j, _):
        zz = z_peer(j)
        b_t_copy(zz, zz).wait_recv()
        relay(c, zz).start()
        return 0

    lax.fori_loop(1, ZS, b_t_take, 0)

    def relay_take(zz, _):
        relay(oc, zz).wait_recv()
        return 0

    lax.fori_loop(0, ZS, relay_take, 0)
    for d, h in steps:
        k = lax.rem(halves[h][4] + d, XS)
        for i in range(XS):
            bb_copy(h, i, k, k).wait_recv()

    loads[5].wait()
    loads[6].wait()
    scale = 4.0 + temp_ref[0].astype(f32)
    shift = -0.5 * bias_ref[0].astype(f32)
    half = PS * H

    for h, unit in ((0, unit_0), (1, unit_1)):
        logits = scale * lax.dot_general(
            all_t[...].reshape(PS * R, E), unit[...].reshape(half, E), (((1,), (1,)), ((), ())),
            preferred_element_type=f32,
        ) + shift
        index = lax.broadcasted_iota(jnp.int32, (PS * R, half), 0)
        sign = jnp.where(index == target_ref[0:1, h * half:(h + 1) * half], f32(1.0), f32(-1.0))
        w_ref[:, h * half:(h + 1) * half] = (-scale * sign * jax.nn.sigmoid(-sign * logits)).astype(bf16)

    back = ((gi_0, ca_out_0, ca_in_0, half_0, cb_out_0, cb_in_0, co_out_0, co_in_0), (gi_1, ca_out_1, ca_in_1, half_1, cb_out_1, cb_in_1, co_out_1, co_in_1))

    def ca_copy(h, k, slot):
        out, into = back[h][1], back[h][2]
        return copy(
            out.at[k], into.at[slot], ca_ss.at[h * XS + k], ca_rs.at[h * XS + slot], halves[h][3](k)
        )

    def co_copy(h, k, slot):
        out, into = back[h][6], back[h][7]
        return copy(
            out.at[k], into.at[slot], co_ss.at[h * XS + k], co_rs.at[h * XS + slot], halves[h][3](k)
        )

    def others(gi, h, k):
        return jnp.concatenate([gi[k * XS + lax.rem(halves[h][2] + e, XS)] for e in (2, 1, 3)], axis=0)

    def cb_copy(h, n, k, slot):
        out, into = back[h][4], back[h][5]
        return copy(out.at[n], into.at[slot], cb_ss.at[h * XS + n], cb_rs.at[h * XS + slot], halves[h][1](k))

    for h in (0, 1):
        gi = back[h][0]
        gi[...] = lax.dot_general(
            w_ref[:, h * half:(h + 1) * half], all_t[...].reshape(PS * R, E), (((0,), (0,)), ((), ())),
            preferred_element_type=f32,
        ).reshape(PS, H, E)
        out, me, line = back[h][1], halves[h][2], halves[h][4]
        for d in (2, 1, 3):
            k = lax.rem(line + d, XS)
            put(out, k, others(gi, h, k), 3 * H)
            ca_copy(h, k, line).start()
    for h in (0, 1):
        gi, own, me, line = back[h][0], back[h][6], halves[h][2], halves[h][4]
        for d in (2, 1, 3):
            k = lax.rem(line + d, XS)
            put(own, k, gi[k * XS + me], H)
            co_copy(h, k, line).start()

    def tile_text(cc):
        w = w_ref.at[pl.ds(pl.multiple_of(cc * (ZS * R), ZS * R), ZS * R)]
        total = jnp.dot(w[:, 0:half], unit_0[...].reshape(half, E), preferred_element_type=f32)
        total = total + jnp.dot(w[:, half:], unit_1[...].reshape(half, E), preferred_element_type=f32)
        gt[pl.ds(cc * ZS, ZS)] = total.reshape(ZS, R, E)

    def gt_copy(b):
        return copy(
            gt.at[pl.ds(oc * ZS + b * 4, 4)], gt_sib.at[pl.ds(b * 4, 4)], gt_ss.at[b], gt_rs.at[b], sibling
        )

    def c_t_copy(zz, slot):
        return copy(c_t_out.at[zz], c_t_in.at[slot], c_t_ss.at[zz], c_t_rs.at[slot], device(ylo, zz, c, t))

    def tile_own(b, _):
        gt_copy(b).wait_recv()
        rows = gt[pl.ds(c * ZS + b * 4, 4)] + gt_sib[pl.ds(b * 4, 4)]
        gt[pl.ds(c * ZS + b * 4, 4)] = rows
        put(c_t_out, b * 4, rows.reshape(4 * R, E), R)
        for n in range(4):
            zz = b * 4 + n

            @pl.when(zz != z)
            def _(zz=zz):
                c_t_copy(zz, z).start()
        return 0

    tile_text(oc)
    gt_copy(0).start()
    gt_copy(1).start()
    tile_text(c)
    lax.fori_loop(0, 2, tile_own, 0)

    for h in (0, 1):
        gi, into, part, out = back[h][0], back[h][2], back[h][3], back[h][4]
        me, line = halves[h][2], halves[h][4]
        total = others(gi, h, line)
        for d in (1, 3, 2):
            k = lax.rem(line + d, XS)
            ca_copy(h, k, k).wait_recv()
            total = total + take(into, k, 3 * H)
        put(out, 0, total, H)
        for n, e in enumerate((2, 1, 3)):
            cb_copy(h, n, lax.rem(me + e, XS), me).start()
    for h in (0, 1):
        gi, own, part = back[h][0], back[h][7], back[h][3]
        me, line = halves[h][2], halves[h][4]
        total = gi[line * XS + me]
        for d in (1, 3, 2):
            k = lax.rem(line + d, XS)
            co_copy(h, k, k).wait_recv()
            total = total + take(own, k, H)
        part[...] = total

    def c_i_take(h):
        into, part, me = back[h][5], back[h][3], halves[h][2]
        total = part[...]
        for d in (1, 3, 2):
            k = lax.rem(me + d, XS)
            cb_copy(h, 0, k, k).wait_recv()
            total = total + take(into, k, H)
        return total

    def c_t_take(j, total):
        zz = z_peer(j)
        c_t_copy(zz, zz).wait_recv()
        return total + take(c_t_in, zz, R)

    def d_copy(grad, ss, rs, k, slot):
        return copy(grad.at[slot], grad.at[slot], ss.at[k], rs.at[slot], (dp, k))

    def d_send(grad, ss, rs):
        def step(j, _):
            d_copy(grad, ss, rs, tensor_peer(j), t).start()
            return 0
        lax.fori_loop(1, TS, step, 0)

    def d_take(grad, ss, rs):
        def step(j, _):
            k = tensor_peer(TS - j)
            d_copy(grad, ss, rs, k, k).wait_recv()
            return 0
        lax.fori_loop(1, TS, step, 0)

    total = jnp.concatenate([c_i_take(0), c_i_take(1)], axis=0)
    grad_i[t] = back_rows(dir_i[...], norm_i[...], total)
    d_send(grad_i, d_i_ss, d_i_rs)
    total = lax.fori_loop(1, ZS, c_t_take, gt[c * ZS + z])
    grad_t[t] = back_rows(dir_t[...], norm_t[...], total)
    d_send(grad_t, d_t_ss, d_t_rs)

    def weight_grad(grad, feat, packed, fold):
        g = lax.dot_general(
            grad[...].reshape(TS * R, E), feat[...], (((0,), (1,)), ((), ())), preferred_element_type=f32
        )
        rest, rows = g.shape[1] - 128, OUT // fold
        for k in range(2 * PS):
            packed[k % 2, k // 2, 0:OUT, :] = g[k * OUT:(k + 1) * OUT, 0:128]
            for n in range(fold):
                packed[k % 2, k // 2, OUT:OUT + rows, n * rest:(n + 1) * rest] = (
                    g[k * OUT + n * rows:k * OUT + (n + 1) * rows, 128:]
                )

    def e_copy(out, into, ss, rs, k, slot):
        return copy(out.at[k], into.at[slot], ss.at[k], rs.at[slot], column(k))

    def e_send(packed, sib, out, into, ss, rs):
        def step(j, _):
            k = column_peer(j)
            out[k] = (packed[c, k] + sib[k]).astype(bf16)
            e_copy(out, into, ss, rs, k, q).start()
            return 0
        lax.fori_loop(1, PS, step, 0)

    def e_take(packed, sib, out, into, ss, rs):
        def step(j, total):
            k = column_peer(j)
            e_copy(out, into, ss, rs, k, k).wait_recv()
            return total + into[k].astype(f32)
        return lax.fori_loop(1, PS, step, packed[c, q] + sib[q])

    e_i = (g_i, sib_i, e_i_out, e_i_in, e_i_ss, e_i_rs)
    e_t = (g_t, sib_t, e_t_out, e_t_in, e_t_ss, e_t_rs)
    d_take(grad_i, d_i_ss, d_i_rs)
    weight_grad(grad_i, fi_ref, g_i, 2)
    g_i_copy = copy(g_i.at[oc], sib_i, one_ss.at[1], one_rs.at[1], sibling)
    g_i_copy.start()
    g_i_copy.wait_recv()
    e_send(*e_i)
    d_take(grad_t, d_t_ss, d_t_rs)
    weight_grad(grad_t, ft_ref, g_t, 3)
    g_t_copy = copy(g_t.at[oc], sib_t, one_ss.at[2], one_rs.at[2], sibling)
    g_t_copy.start()
    g_t_copy.wait_recv()
    e_send(*e_t)

    def unpack(total, out, width, fold):
        rest, rows = width - 128, OUT // fold
        out[:, 0:128] = total[0:OUT, :]
        for n in range(fold):
            out[n * rows:(n + 1) * rows, 128:width] = (
                total[OUT:OUT + rows, n * rest:(n + 1) * rest]
            )

    unpack(e_take(*e_i), out_i, DI, 2)
    unpack(e_take(*e_t), out_t, DT, 3)

    def sent_tensor(j, _):
        k = tensor_peer(j)
        a_copy(a_t_out, a_t_in, a_t_ss, a_t_rs, k, t).wait_send()
        a_copy(a_i_out, a_i_in, a_i_ss, a_i_rs, k, t).wait_send()
        d_copy(grad_t, d_t_ss, d_t_rs, k, t).wait_send()
        d_copy(grad_i, d_i_ss, d_i_rs, k, t).wait_send()
        return 0

    def sent_z(j, _):
        zz = z_peer(j)
        b_t_copy(zz, z).wait_send()
        c_t_copy(zz, z).wait_send()
        return 0

    def sent_column(j, _):
        k = column_peer(j)
        e_copy(e_i_out, e_i_in, e_i_ss, e_i_rs, k, q).wait_send()
        e_copy(e_t_out, e_t_in, e_t_ss, e_t_rs, k, q).wait_send()
        return 0

    def sent_relay(zz, _):
        relay(c, zz).wait_send()
        return 0

    lax.fori_loop(1, TS, sent_tensor, 0)
    lax.fori_loop(1, ZS, sent_z, 0)
    lax.fori_loop(1, PS, sent_column, 0)
    lax.fori_loop(0, ZS, sent_relay, 0)
    for d, h in steps:
        me, line = halves[h][2], halves[h][4]
        ba_copy(h, lax.rem(me + d, XS), me).wait_send()
        ca_copy(h, lax.rem(line + d, XS), line).wait_send()
        co_copy(h, lax.rem(line + d, XS), line).wait_send()
        for i in range(XS):
            bb_copy(h, i, lax.rem(line + d, XS), line).wait_send()
    for h in (0, 1):
        for n, e in enumerate((2, 1, 3)):
            cb_copy(h, n, lax.rem(halves[h][2] + e, XS), halves[h][2]).wait_send()
    for b in (0, 1):
        gt_copy(b).wait_send()
    for sent in (pair_copy, g_i_copy, g_t_copy):
        sent.wait_send()


def on_device(image_features, text_features, image_weight, text_weight, image_pair, temp_index, bias_index):
    hbm = pl.BlockSpec(memory_space=pltpu.HBM)
    dma = pltpu.SemaphoreType.DMA
    V = pltpu.VMEM
    i16, i32 = jnp.int16, jnp.int32
    wire = lambda count, rows: V((count, G * rows + 16, 128), i16)
    scratch = (
        [pltpu.SMEM((1,), i32)] * 2
        + [V((DI, 256), bf16), V((DT, 256), bf16), V((DI, E), bf16), V((DT, E), bf16)]
        + [V((TS, R, E), f32)] * 2 + [wire(TS, R)] * 4
        + [V((R, E), f32)] * 2 + [V((R, 1), f32)] * 2
        + [V((PS, H, E), bf16)] * 2 + [V((PS, R, E), bf16)]
        + [V((8, 256), i32)] * 2 + [V((8, PS * R), i32)]
        + [V((PS * R, PS * R), bf16)] + [V((PS, H, E), f32)] * 2 + [V((PS, R, E), f32), V((ZS, R, E), f32)]
        + [wire(XS, 3 * H)] * 4 + [V((H, E), f32)] * 2 + [wire(XS, H)] * 8 + [wire(ZS, R)] * 2
        + [V((TS, R, E), bf16)] * 2
        + [V((2, PS, ROWS_I, 128), f32), V((2, PS, ROWS_T, 128), f32)]
        + [V((PS, ROWS_I, 128), f32), V((PS, ROWS_T, 128), f32)]
        + [V((PS, ROWS_I, 128), bf16)] * 2 + [V((PS, ROWS_T, 128), bf16)] * 2
        + [dma((7,))] + [dma((TS,))] * 4 + [dma((2 * XS,))] * 2 + [dma((2 * PS,))] * 2 + [dma((ZS,))] * 4
        + [dma((2 * XS,))] * 6 + [dma((2,))] * 2 + [dma((ZS,))] * 2
        + [dma((TS,))] * 4 + [dma((PS,))] * 4 + [dma((3,))] * 2
    )
    grad_image, grad_text = pl.pallas_call(
        kernel,
        out_shape=[jax.ShapeDtypeStruct((OUT, DI), f32), jax.ShapeDtypeStruct((OUT, DT), f32)],
        in_specs=[hbm] * 7,
        out_specs=[pl.BlockSpec(memory_space=pltpu.VMEM)] * 2,
        scratch_shapes=scratch,
        compiler_params=pltpu.CompilerParams(
            collective_id=0, has_side_effects=True, vmem_limit_bytes=56430000
        ),
        name="pair_loss_grads",
    )(
        temp_index.reshape(1), bias_index.reshape(1), image_pair.reshape(1, 256),
        image_features.T, text_features.T, image_weight, text_weight,
    )
    return grad_image.T, grad_text.T


def solution(mesh):
    return jax.shard_map(
        on_device,
        mesh=mesh,
        in_specs=(P("dp", "tensor"), P("dp", "tensor"), P("tensor", None), P("tensor", None), P("dp"), P(), P()),
        out_specs=(P("tensor", "dp"), P("tensor", "dp")),
        check_vma=False,
    )
```

```python
import jax
import jax.numpy as jnp
from jax import lax
from jax.experimental import pallas as pl
from jax.experimental.pallas import tpu as pltpu
from jax.sharding import PartitionSpec as P

MESH = pl.DeviceIdType.MESH
E = 1152
DI = 176
DT = 144
R = 32
TS = 8
ZS = 8
PS = 16
OUT = 36
XS = 4
H = 16
ROWS_I = 64
ROWS_T = 48
LEVELS = 32000.0
G = E // 128
f32 = jnp.float32
bf16 = jnp.bfloat16


def put(wire, k, x, n):
    m = jnp.max(jnp.abs(x), axis=1, keepdims=True)
    hi = jnp.floor(m)
    lo = jnp.floor((m - hi) * LEVELS) + 1.0
    q = jnp.round(x * (LEVELS / (hi + lo * (1.0 / LEVELS)))).astype(jnp.int32).astype(jnp.int16)
    for i in range(x.shape[0] // n):
        rows = slice(i * n, (i + 1) * n)
        for g in range(G):
            wire[k + i, g * n:(g + 1) * n, :] = q[rows, g * 128:(g + 1) * 128]
        diagonal = lax.broadcasted_iota(jnp.int32, (n, 128), 0) == lax.broadcasted_iota(jnp.int32, (n, 128), 1)
        his = jnp.sum(jnp.where(diagonal, hi[rows], 0.0), axis=0, keepdims=True)
        los = jnp.sum(jnp.where(diagonal, lo[rows], 0.0), axis=0, keepdims=True)
        row = lax.broadcasted_iota(jnp.int32, (16, 128), 0)
        wire[k + i, G * n:G * n + 16, :] = (
            jnp.where(row == 0, his, jnp.where(row == 1, los, 0.0)).astype(jnp.int32).astype(jnp.int16)
        )


def take(wire, k, n):
    code = wire[k, G * n:G * n + 16, :].astype(jnp.int32).astype(f32)
    top = code[0:1, :] + code[1:2, :] * (1.0 / LEVELS)
    diagonal = lax.broadcasted_iota(jnp.int32, (n, 128), 0) == lax.broadcasted_iota(jnp.int32, (n, 128), 1)
    step = jnp.sum(jnp.where(diagonal, top, 0.0), axis=1, keepdims=True) * (1.0 / LEVELS)
    return jnp.concatenate(
        [wire[k, g * n:(g + 1) * n, :].astype(jnp.int32).astype(f32) * step for g in range(G)], axis=1
    )


def unit_rows(values):
    norm = jnp.sqrt(jnp.sum(values * values, axis=1, keepdims=True) + 1e-06)
    return norm, values / norm


def back_rows(direct, norm, grad):
    inner = jnp.sum(direct * grad, axis=1, keepdims=True)
    return ((grad - direct * inner) / norm).astype(bf16)


def kernel(
    temp_hbm, bias_hbm, pair_hbm, fi_hbm, ft_hbm, wi_hbm, wt_hbm, out_i, out_t,
    temp_ref, bias_ref,
    fi_ref, ft_ref, wi_ref, wt_ref,
    part_i, part_t, a_i_out, a_i_in, a_t_out, a_t_in,
    dir_i, dir_t, norm_i, norm_t, unit_0, unit_1, all_t, pair_out, pair_in, target_ref,
    w_ref, gi_0, gi_1, gt, gt_sib, ca_out_0, ca_in_0, ca_out_1, ca_in_1,
    half_0, half_1, cb_out_0, cb_in_0, cb_out_1, cb_in_1, co_out_0, co_in_0, co_out_1, co_in_1, c_t_out, c_t_in,
    grad_i, grad_t, g_i, g_t, sib_i, sib_t, e_i_out, e_i_in, e_t_out, e_t_in,
    load_s, a_i_ss, a_i_rs, a_t_ss, a_t_rs, ba_ss, ba_rs, bb_ss, bb_rs, b_t_ss, b_t_rs, relay_ss, relay_rs,
    ca_ss, ca_rs, co_ss, co_rs, cb_ss, cb_rs, gt_ss, gt_rs, c_t_ss, c_t_rs, d_i_ss, d_i_rs, d_t_ss, d_t_rs,
    e_i_ss, e_i_rs, e_t_ss, e_t_rs, one_ss, one_rs,
):
    loads = [
        pltpu.make_async_copy(src, dst, load_s.at[k])
        for k, (src, dst) in enumerate((
            (ft_hbm, ft_ref), (wt_hbm, wt_ref), (fi_hbm, fi_ref), (wi_hbm, wi_ref), (pair_hbm, pair_out.at[0:1]),
            (temp_hbm, temp_ref), (bias_hbm, bias_ref),
        ))
    ]
    for load in loads:
        load.start()

    dp = lax.axis_index("dp")
    t = lax.axis_index("tensor")
    ylo = lax.div(dp, 16)
    z = lax.rem(lax.div(dp, 2), 8)
    c = lax.rem(dp, 2)
    oc = 1 - c
    yhi = lax.div(t, XS)
    x = lax.rem(t, XS)
    y = yhi * 2 + ylo
    q = ylo * ZS + z

    def device(ylo_, z_, c_, t_):
        return ((ylo_ * ZS + z_) * 2 + c_, t_)

    sibling = device(ylo, z, oc, t)
    across = device(1 - ylo, z, c, t)
    beyond = device(1 - ylo, z, c, (1 - yhi) * XS + x)

    def at_x(xx):
        return (dp, yhi * XS + xx)

    def at_y(yy):
        return device(lax.rem(yy, 2), z, c, lax.div(yy, 2) * XS + x)

    def column(k):
        return device(lax.div(k, ZS), lax.rem(k, ZS), c, t)

    def tensor_peer(j):
        dy, dx = ((1, 2), (0, 2), (1, 1), (1, 3), (0, 1), (0, 3), (1, 0))[j - 1]
        return lax.rem(yhi + dy, 2) * XS + lax.rem(x + dx, XS)

    def tensor_steps(body, carry):
        for j in range(1, TS):
            carry = body(j, carry)
        return carry

    def z_step(n):
        m = lax.div(n + 1, 2)
        return lax.rem(4 + m * (1 - 2 * lax.rem(n, 2)) + ZS, ZS)

    def z_peer(j):
        return lax.rem(z + z_step(j - 1), ZS)

    def column_peer(j):
        n = j - 1
        return lax.rem(ylo + 1 - lax.rem(n, 2), 2) * ZS + lax.rem(z + z_step(lax.div(n, 2)), ZS)

    def copy(src, dst, ssem, rsem, dev):
        return pltpu.make_async_remote_copy(
            src_ref=src, dst_ref=dst, send_sem=ssem, recv_sem=rsem, device_id=dev, device_id_type=MESH
        )

    barrier = pltpu.get_barrier_semaphore()

    def greet(dev):
        pl.semaphore_signal(barrier, inc=1, device_id=dev, device_id_type=MESH)

    def greet_tensor(j, _):
        greet((dp, tensor_peer(j)))
        return 0

    def greet_column(j, _):
        greet(column(column_peer(j)))
        return 0

    tensor_steps(greet_tensor, 0)
    lax.fori_loop(1, PS, greet_column, 0)
    greet(beyond)
    greet(sibling)

    def product(feat, weight):
        return lax.dot_general(
            feat[...], weight[...], (((0,), (0,)), ((), ())), preferred_element_type=f32
        ).reshape(TS, R, E)

    g_i[...] = jnp.zeros_like(g_i)
    g_t[...] = jnp.zeros_like(g_t)
    loads[0].wait()
    loads[1].wait()
    part_t[...] = product(ft_ref, wt_ref)
    loads[4].wait()
    pair_out[...] = jnp.broadcast_to(pair_out[0:1, :], (8, 256))
    pl.semaphore_wait(barrier, (TS - 1) + (PS - 1) + 2)

    def a_copy(wire_out, wire_in, ss, rs, k, slot):
        return copy(wire_out.at[k], wire_in.at[slot], ss.at[k], rs.at[slot], (dp, k))

    def a_send(part, wire_out, wire_in, ss, rs):
        for hi in (1 - yhi, yhi):
            put(wire_out, hi * XS, part[pl.ds(hi * XS, XS)].reshape(XS * R, E), R)
            for d in (2, 1, 3) if hi is yhi else (2, 1, 3, 0):
                a_copy(wire_out, wire_in, ss, rs, hi * XS + lax.rem(x + d, XS), t).start()

    def a_take(part, wire_out, wire_in, ss, rs):
        def step(j, total):
            k = tensor_peer(TS - j)
            a_copy(wire_out, wire_in, ss, rs, k, k).wait_recv()
            return total + take(wire_in, k, R)
        return tensor_steps(step, part[t])

    a_send(part_t, a_t_out, a_t_in, a_t_ss, a_t_rs)
    pair_copy = copy(pair_out, pair_in, one_ss.at[0], one_rs.at[0], across)
    pair_copy.start()
    loads[2].wait()
    loads[3].wait()
    part_i[...] = product(fi_ref, wi_ref)
    a_send(part_i, a_i_out, a_i_in, a_i_ss, a_i_rs)

    def local_target(pair):
        r = pair & 31
        tt = (pair >> 5) & 7
        cc = (pair >> 8) & 1
        zz = (pair >> 9) & 7
        yy = (pair >> 12) & 1
        here = jnp.logical_and(tt == t, yy == ylo)
        return jnp.where(here, (cc * ZS + zz) * R + r, -1)

    pair_copy.wait_recv()
    own = local_target(pair_out[0:1, :])
    other = local_target(pair_in[0:1, :])
    by_ylo = (jnp.where(ylo == 0, own, other), jnp.where(ylo == 0, other, own))
    for yy in range(XS):
        for xx in range(XS):
            lane = ((yy // 2) * XS + xx) * R
            s0, s1 = (yy * XS + xx) * H, (xx * XS + yy) * H + PS * H
            target_ref[0:1, s0:s0 + H] = by_ylo[yy % 2][:, lane:lane + H]
            target_ref[0:1, s1:s1 + H] = by_ylo[yy % 2][:, lane + H:lane + R]

    def b_t_copy(zz, slot):
        s = c * ZS + slot
        return copy(all_t.at[s], all_t.at[s], b_t_ss.at[zz], b_t_rs.at[slot], device(ylo, zz, c, t))

    def relay(cc, zz):
        s = cc * ZS + zz
        return copy(all_t.at[s], all_t.at[s], relay_ss.at[zz], relay_rs.at[zz], sibling)

    norm, direct = unit_rows(a_take(part_t, a_t_out, a_t_in, a_t_ss, a_t_rs))
    norm_t[...] = norm
    dir_t[...] = direct
    all_t[c * ZS + z] = direct.astype(bf16)

    def b_t_send(j, _):
        b_t_copy(z_peer(j), z).start()
        return 0

    lax.fori_loop(1, ZS, b_t_send, 0)
    relay(c, z).start()

    halves = ((unit_0, at_x, x, at_y, y), (unit_1, at_y, y, at_x, x))

    def ba_copy(h, k, slot):
        unit, first, me, second, line = halves[h]
        s = line * XS + slot
        return copy(unit.at[s], unit.at[s], ba_ss.at[h * XS + k], ba_rs.at[h * XS + slot], first(k))

    def bb_copy(h, i, k, slot):
        unit, first, me, second, line = halves[h]
        s = slot * XS + i
        return copy(unit.at[s], unit.at[s], bb_ss.at[h * PS + k * XS + i], bb_rs.at[h * PS + s], second(k))

    norm, direct = unit_rows(a_take(part_i, a_i_out, a_i_in, a_i_ss, a_i_rs))
    norm_i[...] = norm
    dir_i[...] = direct
    unit = direct.astype(bf16)
    unit_0[y * XS + x] = unit[0:H]
    unit_1[x * XS + y] = unit[H:R]
    steps = [(d, h) for d in (2, 1, 3) for h in (0, 1)]
    for d, h in steps:
        me = halves[h][2]
        ba_copy(h, lax.rem(me + d, XS), me).start()

    def bb_send(h, i):
        line = halves[h][4]
        for d in (2, 1, 3):
            bb_copy(h, i, lax.rem(line + d, XS), line).start()

    for h in (0, 1):
        bb_send(h, halves[h][2])
    for d in (1, 3, 2):
        for h in (0, 1):
            k = lax.rem(halves[h][2] + d, XS)
            ba_copy(h, k, k).wait_recv()
            bb_send(h, k)

    def b_t_take(j, _):
        zz = z_peer(j)
        b_t_copy(zz, zz).wait_recv()
        relay(c, zz).start()
        return 0

    lax.fori_loop(1, ZS, b_t_take, 0)

    def relay_take(zz, _):
        relay(oc, zz).wait_recv()
        return 0

    lax.fori_loop(0, ZS, relay_take, 0)
    for d, h in steps:
        k = lax.rem(halves[h][4] + d, XS)
        for i in range(XS):
            bb_copy(h, i, k, k).wait_recv()

    loads[5].wait()
    loads[6].wait()
    scale = 4.0 + temp_ref[0].astype(f32)
    shift = -0.5 * bias_ref[0].astype(f32)
    half = PS * H

    for h, unit in ((0, unit_0), (1, unit_1)):
        logits = scale * lax.dot_general(
            all_t[...].reshape(PS * R, E), unit[...].reshape(half, E), (((1,), (1,)), ((), ())),
            preferred_element_type=f32,
        ) + shift
        index = lax.broadcasted_iota(jnp.int32, (PS * R, half), 0)
        sign = jnp.where(index == target_ref[0:1, h * half:(h + 1) * half], f32(1.0), f32(-1.0))
        w_ref[:, h * half:(h + 1) * half] = (-scale * sign * jax.nn.sigmoid(-sign * logits)).astype(bf16)

    back = ((gi_0, ca_out_0, ca_in_0, half_0, cb_out_0, cb_in_0, co_out_0, co_in_0), (gi_1, ca_out_1, ca_in_1, half_1, cb_out_1, cb_in_1, co_out_1, co_in_1))

    def ca_copy(h, k, slot):
        out, into = back[h][1], back[h][2]
        return copy(
            out.at[k], into.at[slot], ca_ss.at[h * XS + k], ca_rs.at[h * XS + slot], halves[h][3](k)
        )

    def co_copy(h, k, slot):
        out, into = back[h][6], back[h][7]
        return copy(
            out.at[k], into.at[slot], co_ss.at[h * XS + k], co_rs.at[h * XS + slot], halves[h][3](k)
        )

    def others(gi, h, k):
        return jnp.concatenate([gi[k * XS + lax.rem(halves[h][2] + e, XS)] for e in (2, 1, 3)], axis=0)

    def cb_copy(h, n, k, slot):
        out, into = back[h][4], back[h][5]
        return copy(out.at[n], into.at[slot], cb_ss.at[h * XS + n], cb_rs.at[h * XS + slot], halves[h][1](k))

    for h in (0, 1):
        gi = back[h][0]
        gi[...] = lax.dot_general(
            w_ref[:, h * half:(h + 1) * half], all_t[...].reshape(PS * R, E), (((0,), (0,)), ((), ())),
            preferred_element_type=f32,
        ).reshape(PS, H, E)
        out, me, line = back[h][1], halves[h][2], halves[h][4]
        for d in (2, 1, 3):
            k = lax.rem(line + d, XS)
            put(out, k, others(gi, h, k), 3 * H)
            ca_copy(h, k, line).start()
    for h in (0, 1):
        gi, own, me, line = back[h][0], back[h][6], halves[h][2], halves[h][4]
        for d in (2, 1, 3):
            k = lax.rem(line + d, XS)
            put(own, k, gi[k * XS + me], H)
            co_copy(h, k, line).start()

    def tile_text(cc):
        w = w_ref.at[pl.ds(pl.multiple_of(cc * (ZS * R), ZS * R), ZS * R)]
        total = jnp.dot(w[:, 0:half], unit_0[...].reshape(half, E), preferred_element_type=f32)
        total = total + jnp.dot(w[:, half:], unit_1[...].reshape(half, E), preferred_element_type=f32)
        gt[pl.ds(cc * ZS, ZS)] = total.reshape(ZS, R, E)

    def gt_copy(b):
        return copy(
            gt.at[pl.ds(oc * ZS + b * 4, 4)], gt_sib.at[pl.ds(b * 4, 4)], gt_ss.at[b], gt_rs.at[b], sibling
        )

    def c_t_copy(zz, slot):
        return copy(c_t_out.at[zz], c_t_in.at[slot], c_t_ss.at[zz], c_t_rs.at[slot], device(ylo, zz, c, t))

    def tile_own(b, _):
        gt_copy(b).wait_recv()
        rows = gt[pl.ds(c * ZS + b * 4, 4)] + gt_sib[pl.ds(b * 4, 4)]
        gt[pl.ds(c * ZS + b * 4, 4)] = rows
        put(c_t_out, b * 4, rows.reshape(4 * R, E), R)
        for n in range(4):
            zz = b * 4 + n

            @pl.when(zz != z)
            def _(zz=zz):
                c_t_copy(zz, z).start()
        return 0

    tile_text(oc)
    gt_copy(0).start()
    gt_copy(1).start()
    tile_text(c)
    lax.fori_loop(0, 2, tile_own, 0)

    for h in (0, 1):
        gi, into, part, out = back[h][0], back[h][2], back[h][3], back[h][4]
        me, line = halves[h][2], halves[h][4]
        total = others(gi, h, line)
        for d in (1, 3, 2):
            k = lax.rem(line + d, XS)
            ca_copy(h, k, k).wait_recv()
            total = total + take(into, k, 3 * H)
        put(out, 0, total, H)
        for n, e in enumerate((2, 1, 3)):
            cb_copy(h, n, lax.rem(me + e, XS), me).start()
    for h in (0, 1):
        gi, own, part = back[h][0], back[h][7], back[h][3]
        me, line = halves[h][2], halves[h][4]
        total = gi[line * XS + me]
        for d in (1, 3, 2):
            k = lax.rem(line + d, XS)
            co_copy(h, k, k).wait_recv()
            total = total + take(own, k, H)
        part[...] = total

    def c_i_take(h):
        into, part, me = back[h][5], back[h][3], halves[h][2]
        total = part[...]
        for d in (1, 3, 2):
            k = lax.rem(me + d, XS)
            cb_copy(h, 0, k, k).wait_recv()
            total = total + take(into, k, H)
        return total

    def c_t_take(j, total):
        zz = z_peer(j)
        c_t_copy(zz, zz).wait_recv()
        return total + take(c_t_in, zz, R)

    def d_copy(grad, ss, rs, k, slot):
        return copy(grad.at[slot], grad.at[slot], ss.at[k], rs.at[slot], (dp, k))

    def d_send(grad, ss, rs):
        def step(j, _):
            d_copy(grad, ss, rs, tensor_peer(j), t).start()
            return 0
        tensor_steps(step, 0)

    def d_take(grad, ss, rs):
        def step(j, _):
            k = tensor_peer(TS - j)
            d_copy(grad, ss, rs, k, k).wait_recv()
            return 0
        tensor_steps(step, 0)

    total = jnp.concatenate([c_i_take(0), c_i_take(1)], axis=0)
    grad_i[t] = back_rows(dir_i[...], norm_i[...], total)
    d_send(grad_i, d_i_ss, d_i_rs)
    total = lax.fori_loop(1, ZS, c_t_take, gt[c * ZS + z])
    grad_t[t] = back_rows(dir_t[...], norm_t[...], total)
    d_send(grad_t, d_t_ss, d_t_rs)

    def weight_grad(grad, feat, packed, fold):
        g = lax.dot_general(
            grad[...].reshape(TS * R, E), feat[...], (((0,), (1,)), ((), ())), preferred_element_type=f32
        )
        rest, rows = g.shape[1] - 128, OUT // fold
        for k in range(2 * PS):
            packed[k % 2, k // 2, 0:OUT, :] = g[k * OUT:(k + 1) * OUT, 0:128]
            for n in range(fold):
                packed[k % 2, k // 2, OUT:OUT + rows, n * rest:(n + 1) * rest] = (
                    g[k * OUT + n * rows:k * OUT + (n + 1) * rows, 128:]
                )

    def e_copy(out, into, ss, rs, k, slot):
        return copy(out.at[k], into.at[slot], ss.at[k], rs.at[slot], column(k))

    def e_send(packed, sib, out, into, ss, rs):
        def step(j, _):
            k = column_peer(j)
            out[k] = (packed[c, k] + sib[k]).astype(bf16)
            e_copy(out, into, ss, rs, k, q).start()
            return 0
        lax.fori_loop(1, PS, step, 0)

    def e_take(packed, sib, out, into, ss, rs):
        def step(j, total):
            k = column_peer(j)
            e_copy(out, into, ss, rs, k, k).wait_recv()
            return total + into[k].astype(f32)
        return lax.fori_loop(1, PS, step, packed[c, q] + sib[q])

    e_i = (g_i, sib_i, e_i_out, e_i_in, e_i_ss, e_i_rs)
    e_t = (g_t, sib_t, e_t_out, e_t_in, e_t_ss, e_t_rs)
    d_take(grad_i, d_i_ss, d_i_rs)
    weight_grad(grad_i, fi_ref, g_i, 2)
    g_i_copy = copy(g_i.at[oc], sib_i, one_ss.at[1], one_rs.at[1], sibling)
    g_i_copy.start()
    g_i_copy.wait_recv()
    e_send(*e_i)
    d_take(grad_t, d_t_ss, d_t_rs)
    weight_grad(grad_t, ft_ref, g_t, 3)
    g_t_copy = copy(g_t.at[oc], sib_t, one_ss.at[2], one_rs.at[2], sibling)
    g_t_copy.start()
    g_t_copy.wait_recv()
    e_send(*e_t)

    def unpack(total, out, width, fold):
        rest, rows = width - 128, OUT // fold
        out[:, 0:128] = total[0:OUT, :]
        for n in range(fold):
            out[n * rows:(n + 1) * rows, 128:width] = (
                total[OUT:OUT + rows, n * rest:(n + 1) * rest]
            )

    def sent_tensor(j, _):
        k = tensor_peer(j)
        a_copy(a_t_out, a_t_in, a_t_ss, a_t_rs, k, t).wait_send()
        a_copy(a_i_out, a_i_in, a_i_ss, a_i_rs, k, t).wait_send()
        d_copy(grad_t, d_t_ss, d_t_rs, k, t).wait_send()
        d_copy(grad_i, d_i_ss, d_i_rs, k, t).wait_send()
        return 0

    def sent_z(j, _):
        zz = z_peer(j)
        b_t_copy(zz, z).wait_send()
        c_t_copy(zz, z).wait_send()
        return 0

    def sent_relay(zz, _):
        relay(c, zz).wait_send()
        return 0

    tensor_steps(sent_tensor, 0)
    lax.fori_loop(1, ZS, sent_z, 0)
    lax.fori_loop(0, ZS, sent_relay, 0)
    for d, h in steps:
        me, line = halves[h][2], halves[h][4]
        ba_copy(h, lax.rem(me + d, XS), me).wait_send()
        ca_copy(h, lax.rem(line + d, XS), line).wait_send()
        co_copy(h, lax.rem(line + d, XS), line).wait_send()
        for i in range(XS):
            bb_copy(h, i, lax.rem(line + d, XS), line).wait_send()
    for h in (0, 1):
        for n, e in enumerate((2, 1, 3)):
            cb_copy(h, n, lax.rem(halves[h][2] + e, XS), halves[h][2]).wait_send()
    for b in (0, 1):
        gt_copy(b).wait_send()
    pair_copy.wait_send()

    unpack(e_take(*e_i), out_i, DI, 2)
    unpack(e_take(*e_t), out_t, DT, 3)

    def sent_column(j, _):
        k = column_peer(j)
        e_copy(e_i_out, e_i_in, e_i_ss, e_i_rs, k, q).wait_send()
        e_copy(e_t_out, e_t_in, e_t_ss, e_t_rs, k, q).wait_send()
        return 0

    lax.fori_loop(1, PS, sent_column, 0)
    for sent in (g_i_copy, g_t_copy):
        sent.wait_send()


def on_device(image_features, text_features, image_weight, text_weight, image_pair, temp_index, bias_index):
    hbm = pl.BlockSpec(memory_space=pltpu.HBM)
    dma = pltpu.SemaphoreType.DMA
    V = pltpu.VMEM
    i16, i32 = jnp.int16, jnp.int32
    wire = lambda count, rows: V((count, G * rows + 16, 128), i16)
    scratch = (
        [pltpu.SMEM((1,), i32)] * 2
        + [V((DI, 256), bf16), V((DT, 256), bf16), V((DI, E), bf16), V((DT, E), bf16)]
        + [V((TS, R, E), f32)] * 2 + [wire(TS, R)] * 4
        + [V((R, E), f32)] * 2 + [V((R, 1), f32)] * 2
        + [V((PS, H, E), bf16)] * 2 + [V((PS, R, E), bf16)]
        + [V((8, 256), i32)] * 2 + [V((8, PS * R), i32)]
        + [V((PS * R, PS * R), bf16)] + [V((PS, H, E), f32)] * 2 + [V((PS, R, E), f32), V((ZS, R, E), f32)]
        + [wire(XS, 3 * H)] * 4 + [V((H, E), f32)] * 2 + [wire(XS, H)] * 8 + [wire(ZS, R)] * 2
        + [V((TS, R, E), bf16)] * 2
        + [V((2, PS, ROWS_I, 128), f32), V((2, PS, ROWS_T, 128), f32)]
        + [V((PS, ROWS_I, 128), f32), V((PS, ROWS_T, 128), f32)]
        + [V((PS, ROWS_I, 128), bf16)] * 2 + [V((PS, ROWS_T, 128), bf16)] * 2
        + [dma((7,))] + [dma((TS,))] * 4 + [dma((2 * XS,))] * 2 + [dma((2 * PS,))] * 2 + [dma((ZS,))] * 4
        + [dma((2 * XS,))] * 6 + [dma((2,))] * 2 + [dma((ZS,))] * 2
        + [dma((TS,))] * 4 + [dma((PS,))] * 4 + [dma((3,))] * 2
    )
    grad_image, grad_text = pl.pallas_call(
        kernel,
        out_shape=[jax.ShapeDtypeStruct((OUT, DI), f32), jax.ShapeDtypeStruct((OUT, DT), f32)],
        in_specs=[hbm] * 7,
        out_specs=[pl.BlockSpec(memory_space=pltpu.VMEM)] * 2,
        scratch_shapes=scratch,
        compiler_params=pltpu.CompilerParams(
            collective_id=0, has_side_effects=True, vmem_limit_bytes=56430000
        ),
        name="pair_loss_grads",
    )(
        temp_index.reshape(1), bias_index.reshape(1), image_pair.reshape(1, 256),
        image_features.T, text_features.T, image_weight, text_weight,
    )
    return grad_image.T, grad_text.T


def solution(mesh):
    return jax.shard_map(
        on_device,
        mesh=mesh,
        in_specs=(P("dp", "tensor"), P("dp", "tensor"), P("tensor", None), P("tensor", None), P("dp"), P(), P()),
        out_specs=(P("tensor", "dp"), P("tensor", "dp")),
        check_vma=False,
    )
```

```python
import jax
import jax.numpy as jnp
from jax import lax
from jax.experimental import pallas as pl
from jax.experimental.pallas import tpu as pltpu
from jax.sharding import PartitionSpec as P

MESH = pl.DeviceIdType.MESH
E = 1152
DI = 176
DT = 144
R = 32
TS = 8
ZS = 8
PS = 16
OUT = 36
XS = 4
H = 16
ROWS_I = 64
ROWS_T = 48
LEVELS = 32000.0
G = E // 128
f32 = jnp.float32
bf16 = jnp.bfloat16


def put(wire, k, x, n):
    m = jnp.max(jnp.abs(x), axis=1, keepdims=True)
    hi = jnp.floor(m)
    lo = jnp.floor((m - hi) * LEVELS) + 1.0
    q = jnp.round(x * (LEVELS / (hi + lo * (1.0 / LEVELS)))).astype(jnp.int32).astype(jnp.int16)
    for i in range(x.shape[0] // n):
        rows = slice(i * n, (i + 1) * n)
        for g in range(G):
            wire[k + i, g * n:(g + 1) * n, :] = q[rows, g * 128:(g + 1) * 128]
        diagonal = lax.broadcasted_iota(jnp.int32, (n, 128), 0) == lax.broadcasted_iota(jnp.int32, (n, 128), 1)
        his = jnp.sum(jnp.where(diagonal, hi[rows], 0.0), axis=0, keepdims=True)
        los = jnp.sum(jnp.where(diagonal, lo[rows], 0.0), axis=0, keepdims=True)
        row = lax.broadcasted_iota(jnp.int32, (16, 128), 0)
        wire[k + i, G * n:G * n + 16, :] = (
            jnp.where(row == 0, his, jnp.where(row == 1, los, 0.0)).astype(jnp.int32).astype(jnp.int16)
        )


def take(wire, k, n):
    code = wire[k, G * n:G * n + 16, :].astype(jnp.int32).astype(f32)
    top = code[0:1, :] + code[1:2, :] * (1.0 / LEVELS)
    diagonal = lax.broadcasted_iota(jnp.int32, (n, 128), 0) == lax.broadcasted_iota(jnp.int32, (n, 128), 1)
    step = jnp.sum(jnp.where(diagonal, top, 0.0), axis=1, keepdims=True) * (1.0 / LEVELS)
    return jnp.concatenate(
        [wire[k, g * n:(g + 1) * n, :].astype(jnp.int32).astype(f32) * step for g in range(G)], axis=1
    )


def unit_rows(values):
    norm = jnp.sqrt(jnp.sum(values * values, axis=1, keepdims=True) + 1e-06)
    return norm, values / norm


def back_rows(direct, norm, grad):
    inner = jnp.sum(direct * grad, axis=1, keepdims=True)
    return ((grad - direct * inner) / norm).astype(bf16)


def kernel(
    temp_hbm, bias_hbm, pair_hbm, fi_hbm, ft_hbm, wi_hbm, wt_hbm, out_i, out_t,
    temp_ref, bias_ref,
    fi_ref, ft_ref, wi_ref, wt_ref,
    part_i, part_t, a_i_out, a_i_in, a_t_out, a_t_in,
    dir_i, dir_t, norm_i, norm_t, unit_0, unit_1, all_t, pair_out, pair_in, target_ref,
    w_ref, gi_0, gi_1, gt, gt_sib, ca_out_0, ca_in_0, ca_out_1, ca_in_1,
    half_0, half_1, cb_out_0, cb_in_0, cb_out_1, cb_in_1, co_out_0, co_in_0, co_out_1, co_in_1, c_t_out, c_t_in,
    grad_i, grad_t, g_i, g_t, sib_i, sib_t, e_i_out, e_i_in, e_t_out, e_t_in,
    load_s, a_i_ss, a_i_rs, a_t_ss, a_t_rs, ba_ss, ba_rs, bb_ss, bb_rs, b_t_ss, b_t_rs, relay_ss, relay_rs,
    ca_ss, ca_rs, co_ss, co_rs, cb_ss, cb_rs, gt_ss, gt_rs, c_t_ss, c_t_rs, d_i_ss, d_i_rs, d_t_ss, d_t_rs,
    e_i_ss, e_i_rs, e_t_ss, e_t_rs, one_ss, one_rs,
):
    loads = [
        pltpu.make_async_copy(src, dst, load_s.at[k])
        for k, (src, dst) in enumerate((
            (ft_hbm, ft_ref), (wt_hbm, wt_ref), (fi_hbm, fi_ref), (wi_hbm, wi_ref), (pair_hbm, pair_out.at[0:1]),
            (temp_hbm, temp_ref), (bias_hbm, bias_ref),
        ))
    ]
    for load in loads:
        load.start()

    dp = lax.axis_index("dp")
    t = lax.axis_index("tensor")
    ylo = lax.div(dp, 16)
    z = lax.rem(lax.div(dp, 2), 8)
    c = lax.rem(dp, 2)
    oc = 1 - c
    yhi = lax.div(t, XS)
    x = lax.rem(t, XS)
    y = yhi * 2 + ylo
    q = ylo * ZS + z

    def device(ylo_, z_, c_, t_):
        return ((ylo_ * ZS + z_) * 2 + c_, t_)

    sibling = device(ylo, z, oc, t)
    across = device(1 - ylo, z, c, t)
    beyond = device(1 - ylo, z, c, (1 - yhi) * XS + x)

    def at_x(xx):
        return (dp, yhi * XS + xx)

    def at_y(yy):
        return device(lax.rem(yy, 2), z, c, lax.div(yy, 2) * XS + x)

    def column(k):
        return device(lax.div(k, ZS), lax.rem(k, ZS), c, t)

    def tensor_peer(j):
        dy, dx = ((1, 2), (0, 2), (1, 0), (1, 1), (1, 3), (0, 1), (0, 3))[j - 1]
        return lax.rem(yhi + dy, 2) * XS + lax.rem(x + dx, XS)

    def tensor_steps(body, carry):
        for j in range(1, TS):
            carry = body(j, carry)
        return carry

    def z_step(n):
        m = lax.div(n + 1, 2)
        return lax.rem(4 + m * (1 - 2 * lax.rem(n, 2)) + ZS, ZS)

    def z_peer(j):
        return lax.rem(z + z_step(j - 1), ZS)

    def column_peer(j):
        n = j - 1
        return lax.rem(ylo + 1 - lax.rem(n, 2), 2) * ZS + lax.rem(z + z_step(lax.div(n, 2)), ZS)

    def copy(src, dst, ssem, rsem, dev):
        return pltpu.make_async_remote_copy(
            src_ref=src, dst_ref=dst, send_sem=ssem, recv_sem=rsem, device_id=dev, device_id_type=MESH
        )

    barrier = pltpu.get_barrier_semaphore()

    def greet(dev):
        pl.semaphore_signal(barrier, inc=1, device_id=dev, device_id_type=MESH)

    def greet_tensor(j, _):
        greet((dp, tensor_peer(j)))
        return 0

    def greet_column(j, _):
        greet(column(column_peer(j)))
        return 0

    tensor_steps(greet_tensor, 0)
    lax.fori_loop(1, PS, greet_column, 0)
    greet(beyond)
    greet(sibling)

    def product(feat, weight):
        return lax.dot_general(
            feat[...], weight[...], (((0,), (0,)), ((), ())), preferred_element_type=f32
        ).reshape(TS, R, E)

    def a_encode(part, wire_out):
        for b in range(2):
            put(wire_out, b * XS, part[b * XS:(b + 1) * XS].reshape(XS * R, E), R)

    g_i[...] = jnp.zeros_like(g_i)
    g_t[...] = jnp.zeros_like(g_t)
    loads[0].wait()
    loads[1].wait()
    part_t[...] = product(ft_ref, wt_ref)
    a_encode(part_t, a_t_out)
    loads[4].wait()
    pair_out[...] = jnp.broadcast_to(pair_out[0:1, :], (8, 256))
    pl.semaphore_wait(barrier, (TS - 1) + (PS - 1) + 2)

    def a_copy(wire_out, wire_in, ss, rs, k, slot):
        return copy(wire_out.at[k], wire_in.at[slot], ss.at[k], rs.at[slot], (dp, k))

    def a_send(wire_out, wire_in, ss, rs):
        def step(j, _):
            a_copy(wire_out, wire_in, ss, rs, tensor_peer(j), t).start()
            return 0
        tensor_steps(step, 0)

    def a_take(part, wire_out, wire_in, ss, rs):
        def step(j, total):
            k = tensor_peer(TS - j)
            a_copy(wire_out, wire_in, ss, rs, k, k).wait_recv()
            return total + take(wire_in, k, R)
        return tensor_steps(step, part[t])

    a_send(a_t_out, a_t_in, a_t_ss, a_t_rs)
    pair_copy = copy(pair_out, pair_in, one_ss.at[0], one_rs.at[0], across)
    pair_copy.start()
    loads[2].wait()
    loads[3].wait()
    part_i[...] = product(fi_ref, wi_ref)
    a_encode(part_i, a_i_out)
    a_send(a_i_out, a_i_in, a_i_ss, a_i_rs)

    def local_target(pair):
        r = pair & 31
        tt = (pair >> 5) & 7
        cc = (pair >> 8) & 1
        zz = (pair >> 9) & 7
        yy = (pair >> 12) & 1
        here = jnp.logical_and(tt == t, yy == ylo)
        return jnp.where(here, (cc * ZS + zz) * R + r, -1)

    pair_copy.wait_recv()
    own = local_target(pair_out[0:1, :])
    other = local_target(pair_in[0:1, :])
    by_ylo = (jnp.where(ylo == 0, own, other), jnp.where(ylo == 0, other, own))
    for yy in range(XS):
        for xx in range(XS):
            lane = ((yy // 2) * XS + xx) * R
            s0, s1 = (yy * XS + xx) * H, (xx * XS + yy) * H + PS * H
            target_ref[0:1, s0:s0 + H] = by_ylo[yy % 2][:, lane:lane + H]
            target_ref[0:1, s1:s1 + H] = by_ylo[yy % 2][:, lane + H:lane + R]

    def b_t_copy(zz, slot):
        s = c * ZS + slot
        return copy(all_t.at[s], all_t.at[s], b_t_ss.at[zz], b_t_rs.at[slot], device(ylo, zz, c, t))

    def relay(cc, zz):
        s = cc * ZS + zz
        return copy(all_t.at[s], all_t.at[s], relay_ss.at[zz], relay_rs.at[zz], sibling)

    norm, direct = unit_rows(a_take(part_t, a_t_out, a_t_in, a_t_ss, a_t_rs))
    norm_t[...] = norm
    dir_t[...] = direct
    all_t[c * ZS + z] = direct.astype(bf16)

    def b_t_send(j, _):
        b_t_copy(z_peer(j), z).start()
        return 0

    lax.fori_loop(1, ZS, b_t_send, 0)
    relay(c, z).start()

    halves = ((unit_0, at_x, x, at_y, y), (unit_1, at_y, y, at_x, x))

    def ba_copy(h, k, slot):
        unit, first, me, second, line = halves[h]
        s = line * XS + slot
        return copy(unit.at[s], unit.at[s], ba_ss.at[h * XS + k], ba_rs.at[h * XS + slot], first(k))

    def bb_copy(h, i, k, slot):
        unit, first, me, second, line = halves[h]
        s = slot * XS + i
        return copy(unit.at[s], unit.at[s], bb_ss.at[h * PS + k * XS + i], bb_rs.at[h * PS + s], second(k))

    norm, direct = unit_rows(a_take(part_i, a_i_out, a_i_in, a_i_ss, a_i_rs))
    norm_i[...] = norm
    dir_i[...] = direct
    unit = direct.astype(bf16)
    unit_0[y * XS + x] = unit[0:H]
    unit_1[x * XS + y] = unit[H:R]
    steps = [(d, h) for d in (2, 1, 3) for h in (0, 1)]
    for d, h in steps:
        me = halves[h][2]
        ba_copy(h, lax.rem(me + d, XS), me).start()

    def bb_send(h, i):
        line = halves[h][4]
        for d in (2, 1, 3):
            bb_copy(h, i, lax.rem(line + d, XS), line).start()

    for h in (0, 1):
        bb_send(h, halves[h][2])
    for d in (1, 3, 2):
        for h in (0, 1):
            k = lax.rem(halves[h][2] + d, XS)
            ba_copy(h, k, k).wait_recv()
            bb_send(h, k)

    def b_t_take(j, _):
        zz = z_peer(j)
        b_t_copy(zz, zz).wait_recv()
        relay(c, zz).start()
        return 0

    lax.fori_loop(1, ZS, b_t_take, 0)

    def relay_take(zz, _):
        relay(oc, zz).wait_recv()
        return 0

    lax.fori_loop(0, ZS, relay_take, 0)
    for d, h in steps:
        k = lax.rem(halves[h][4] + d, XS)
        for i in range(XS):
            bb_copy(h, i, k, k).wait_recv()

    loads[5].wait()
    loads[6].wait()
    scale = 4.0 + temp_ref[0].astype(f32)
    shift = -0.5 * bias_ref[0].astype(f32)
    half = PS * H

    for h, unit in ((0, unit_0), (1, unit_1)):
        logits = scale * lax.dot_general(
            all_t[...].reshape(PS * R, E), unit[...].reshape(half, E), (((1,), (1,)), ((), ())),
            preferred_element_type=f32,
        ) + shift
        index = lax.broadcasted_iota(jnp.int32, (PS * R, half), 0)
        sign = jnp.where(index == target_ref[0:1, h * half:(h + 1) * half], f32(1.0), f32(-1.0))
        w_ref[:, h * half:(h + 1) * half] = (-scale * sign * jax.nn.sigmoid(-sign * logits)).astype(bf16)

    back = ((gi_0, ca_out_0, ca_in_0, half_0, cb_out_0, cb_in_0, co_out_0, co_in_0), (gi_1, ca_out_1, ca_in_1, half_1, cb_out_1, cb_in_1, co_out_1, co_in_1))

    def ca_copy(h, k, slot):
        out, into = back[h][1], back[h][2]
        return copy(
            out.at[k], into.at[slot], ca_ss.at[h * XS + k], ca_rs.at[h * XS + slot], halves[h][3](k)
        )

    def co_copy(h, k, slot):
        out, into = back[h][6], back[h][7]
        return copy(
            out.at[k], into.at[slot], co_ss.at[h * XS + k], co_rs.at[h * XS + slot], halves[h][3](k)
        )

    def others(gi, h, k):
        return jnp.concatenate([gi[k * XS + lax.rem(halves[h][2] + e, XS)] for e in (2, 1, 3)], axis=0)

    def cb_copy(h, n, k, slot):
        out, into = back[h][4], back[h][5]
        return copy(out.at[n], into.at[slot], cb_ss.at[h * XS + n], cb_rs.at[h * XS + slot], halves[h][1](k))

    for h in (0, 1):
        gi = back[h][0]
        gi[...] = lax.dot_general(
            w_ref[:, h * half:(h + 1) * half], all_t[...].reshape(PS * R, E), (((0,), (0,)), ((), ())),
            preferred_element_type=f32,
        ).reshape(PS, H, E)
        out, me, line = back[h][1], halves[h][2], halves[h][4]
        for d in (2, 1, 3):
            k = lax.rem(line + d, XS)
            put(out, k, others(gi, h, k), 3 * H)
            ca_copy(h, k, line).start()
    for h in (0, 1):
        gi, own, me, line = back[h][0], back[h][6], halves[h][2], halves[h][4]
        for d in (2, 1, 3):
            k = lax.rem(line + d, XS)
            put(own, k, gi[k * XS + me], H)
            co_copy(h, k, line).start()

    def tile_text(cc):
        w = w_ref.at[pl.ds(pl.multiple_of(cc * (ZS * R), ZS * R), ZS * R)]
        total = jnp.dot(w[:, 0:half], unit_0[...].reshape(half, E), preferred_element_type=f32)
        total = total + jnp.dot(w[:, half:], unit_1[...].reshape(half, E), preferred_element_type=f32)
        gt[pl.ds(cc * ZS, ZS)] = total.reshape(ZS, R, E)

    def gt_copy(b):
        return copy(
            gt.at[pl.ds(oc * ZS + b * 4, 4)], gt_sib.at[pl.ds(b * 4, 4)], gt_ss.at[b], gt_rs.at[b], sibling
        )

    def c_t_copy(zz, slot):
        return copy(c_t_out.at[zz], c_t_in.at[slot], c_t_ss.at[zz], c_t_rs.at[slot], device(ylo, zz, c, t))

    def tile_own(b, _):
        gt_copy(b).wait_recv()
        rows = gt[pl.ds(c * ZS + b * 4, 4)] + gt_sib[pl.ds(b * 4, 4)]
        gt[pl.ds(c * ZS + b * 4, 4)] = rows
        put(c_t_out, b * 4, rows.reshape(4 * R, E), R)
        for n in range(4):
            zz = b * 4 + n

            @pl.when(zz != z)
            def _(zz=zz):
                c_t_copy(zz, z).start()
        return 0

    tile_text(oc)
    gt_copy(0).start()
    gt_copy(1).start()
    tile_text(c)
    lax.fori_loop(0, 2, tile_own, 0)

    for h in (0, 1):
        gi, into, part, out = back[h][0], back[h][2], back[h][3], back[h][4]
        me, line = halves[h][2], halves[h][4]
        total = others(gi, h, line)
        for d in (1, 3, 2):
            k = lax.rem(line + d, XS)
            ca_copy(h, k, k).wait_recv()
            total = total + take(into, k, 3 * H)
        put(out, 0, total, H)
        for n, e in enumerate((2, 1, 3)):
            cb_copy(h, n, lax.rem(me + e, XS), me).start()
    for h in (0, 1):
        gi, own, part = back[h][0], back[h][7], back[h][3]
        me, line = halves[h][2], halves[h][4]
        total = gi[line * XS + me]
        for d in (1, 3, 2):
            k = lax.rem(line + d, XS)
            co_copy(h, k, k).wait_recv()
            total = total + take(own, k, H)
        part[...] = total

    def c_i_take(h):
        into, part, me = back[h][5], back[h][3], halves[h][2]
        total = part[...]
        for d in (1, 3, 2):
            k = lax.rem(me + d, XS)
            cb_copy(h, 0, k, k).wait_recv()
            total = total + take(into, k, H)
        return total

    def c_t_take(j, total):
        zz = z_peer(j)
        c_t_copy(zz, zz).wait_recv()
        return total + take(c_t_in, zz, R)

    def d_copy(grad, ss, rs, k, slot):
        return copy(grad.at[slot], grad.at[slot], ss.at[k], rs.at[slot], (dp, k))

    def d_send(grad, ss, rs):
        def step(j, _):
            d_copy(grad, ss, rs, tensor_peer(j), t).start()
            return 0
        tensor_steps(step, 0)

    def d_take(grad, ss, rs):
        def step(j, _):
            k = tensor_peer(TS - j)
            d_copy(grad, ss, rs, k, k).wait_recv()
            return 0
        tensor_steps(step, 0)

    total = jnp.concatenate([c_i_take(0), c_i_take(1)], axis=0)
    grad_i[t] = back_rows(dir_i[...], norm_i[...], total)
    d_send(grad_i, d_i_ss, d_i_rs)
    total = lax.fori_loop(1, ZS, c_t_take, gt[c * ZS + z])
    grad_t[t] = back_rows(dir_t[...], norm_t[...], total)
    d_send(grad_t, d_t_ss, d_t_rs)

    def weight_grad(grad, feat, packed, fold):
        g = lax.dot_general(
            grad[...].reshape(TS * R, E), feat[...], (((0,), (1,)), ((), ())), preferred_element_type=f32
        )
        rest, rows = g.shape[1] - 128, OUT // fold
        for k in range(2 * PS):
            packed[k % 2, k // 2, 0:OUT, :] = g[k * OUT:(k + 1) * OUT, 0:128]
            for n in range(fold):
                packed[k % 2, k // 2, OUT:OUT + rows, n * rest:(n + 1) * rest] = (
                    g[k * OUT + n * rows:k * OUT + (n + 1) * rows, 128:]
                )

    def e_copy(out, into, ss, rs, k, slot):
        return copy(out.at[k], into.at[slot], ss.at[k], rs.at[slot], column(k))

    def e_send(packed, sib, out, into, ss, rs):
        def step(j, _):
            k = column_peer(j)
            out[k] = (packed[c, k] + sib[k]).astype(bf16)
            e_copy(out, into, ss, rs, k, q).start()
            return 0
        lax.fori_loop(1, PS, step, 0)

    def e_take(packed, sib, out, into, ss, rs):
        def step(j, total):
            k = column_peer(j)
            e_copy(out, into, ss, rs, k, k).wait_recv()
            return total + into[k].astype(f32)
        return lax.fori_loop(1, PS, step, packed[c, q] + sib[q])

    e_i = (g_i, sib_i, e_i_out, e_i_in, e_i_ss, e_i_rs)
    e_t = (g_t, sib_t, e_t_out, e_t_in, e_t_ss, e_t_rs)
    d_take(grad_i, d_i_ss, d_i_rs)
    weight_grad(grad_i, fi_ref, g_i, 2)
    g_i_copy = copy(g_i.at[oc], sib_i, one_ss.at[1], one_rs.at[1], sibling)
    g_i_copy.start()
    g_i_copy.wait_recv()
    e_send(*e_i)
    d_take(grad_t, d_t_ss, d_t_rs)
    weight_grad(grad_t, ft_ref, g_t, 3)
    g_t_copy = copy(g_t.at[oc], sib_t, one_ss.at[2], one_rs.at[2], sibling)
    g_t_copy.start()
    g_t_copy.wait_recv()
    e_send(*e_t)

    def unpack(total, out, width, fold):
        rest, rows = width - 128, OUT // fold
        out[:, 0:128] = total[0:OUT, :]
        for n in range(fold):
            out[n * rows:(n + 1) * rows, 128:width] = (
                total[OUT:OUT + rows, n * rest:(n + 1) * rest]
            )

    def sent_tensor(j, _):
        k = tensor_peer(j)
        a_copy(a_t_out, a_t_in, a_t_ss, a_t_rs, k, t).wait_send()
        a_copy(a_i_out, a_i_in, a_i_ss, a_i_rs, k, t).wait_send()
        d_copy(grad_t, d_t_ss, d_t_rs, k, t).wait_send()
        d_copy(grad_i, d_i_ss, d_i_rs, k, t).wait_send()
        return 0

    def sent_z(j, _):
        zz = z_peer(j)
        b_t_copy(zz, z).wait_send()
        c_t_copy(zz, z).wait_send()
        return 0

    def sent_relay(zz, _):
        relay(c, zz).wait_send()
        return 0

    tensor_steps(sent_tensor, 0)
    lax.fori_loop(1, ZS, sent_z, 0)
    lax.fori_loop(0, ZS, sent_relay, 0)
    for d, h in steps:
        me, line = halves[h][2], halves[h][4]
        ba_copy(h, lax.rem(me + d, XS), me).wait_send()
        ca_copy(h, lax.rem(line + d, XS), line).wait_send()
        co_copy(h, lax.rem(line + d, XS), line).wait_send()
        for i in range(XS):
            bb_copy(h, i, lax.rem(line + d, XS), line).wait_send()
    for h in (0, 1):
        for n, e in enumerate((2, 1, 3)):
            cb_copy(h, n, lax.rem(halves[h][2] + e, XS), halves[h][2]).wait_send()
    for b in (0, 1):
        gt_copy(b).wait_send()
    pair_copy.wait_send()

    unpack(e_take(*e_i), out_i, DI, 2)
    unpack(e_take(*e_t), out_t, DT, 3)

    def sent_column(j, _):
        k = column_peer(j)
        e_copy(e_i_out, e_i_in, e_i_ss, e_i_rs, k, q).wait_send()
        e_copy(e_t_out, e_t_in, e_t_ss, e_t_rs, k, q).wait_send()
        return 0

    lax.fori_loop(1, PS, sent_column, 0)
    for sent in (g_i_copy, g_t_copy):
        sent.wait_send()


def on_device(image_features, text_features, image_weight, text_weight, image_pair, temp_index, bias_index):
    hbm = pl.BlockSpec(memory_space=pltpu.HBM)
    dma = pltpu.SemaphoreType.DMA
    V = pltpu.VMEM
    i16, i32 = jnp.int16, jnp.int32
    wire = lambda count, rows: V((count, G * rows + 16, 128), i16)
    scratch = (
        [pltpu.SMEM((1,), i32)] * 2
        + [V((DI, 256), bf16), V((DT, 256), bf16), V((DI, E), bf16), V((DT, E), bf16)]
        + [V((TS, R, E), f32)] * 2 + [wire(TS, R)] * 4
        + [V((R, E), f32)] * 2 + [V((R, 1), f32)] * 2
        + [V((PS, H, E), bf16)] * 2 + [V((PS, R, E), bf16)]
        + [V((8, 256), i32)] * 2 + [V((8, PS * R), i32)]
        + [V((PS * R, PS * R), bf16)] + [V((PS, H, E), f32)] * 2 + [V((PS, R, E), f32), V((ZS, R, E), f32)]
        + [wire(XS, 3 * H)] * 4 + [V((H, E), f32)] * 2 + [wire(XS, H)] * 8 + [wire(ZS, R)] * 2
        + [V((TS, R, E), bf16)] * 2
        + [V((2, PS, ROWS_I, 128), f32), V((2, PS, ROWS_T, 128), f32)]
        + [V((PS, ROWS_I, 128), f32), V((PS, ROWS_T, 128), f32)]
        + [V((PS, ROWS_I, 128), bf16)] * 2 + [V((PS, ROWS_T, 128), bf16)] * 2
        + [dma((7,))] + [dma((TS,))] * 4 + [dma((2 * XS,))] * 2 + [dma((2 * PS,))] * 2 + [dma((ZS,))] * 4
        + [dma((2 * XS,))] * 6 + [dma((2,))] * 2 + [dma((ZS,))] * 2
        + [dma((TS,))] * 4 + [dma((PS,))] * 4 + [dma((3,))] * 2
    )
    grad_image, grad_text = pl.pallas_call(
        kernel,
        out_shape=[jax.ShapeDtypeStruct((OUT, DI), f32), jax.ShapeDtypeStruct((OUT, DT), f32)],
        in_specs=[hbm] * 7,
        out_specs=[pl.BlockSpec(memory_space=pltpu.VMEM)] * 2,
        scratch_shapes=scratch,
        compiler_params=pltpu.CompilerParams(
            collective_id=0, has_side_effects=True, vmem_limit_bytes=56430000
        ),
        name="pair_loss_grads",
    )(
        temp_index.reshape(1), bias_index.reshape(1), image_pair.reshape(1, 256),
        image_features.T, text_features.T, image_weight, text_weight,
    )
    return grad_image.T, grad_text.T


def solution(mesh):
    return jax.shard_map(
        on_device,
        mesh=mesh,
        in_specs=(P("dp", "tensor"), P("dp", "tensor"), P("tensor", None), P("tensor", None), P("dp"), P(), P()),
        out_specs=(P("tensor", "dp"), P("tensor", "dp")),
        check_vma=False,
    )
```

```python
import jax
import jax.numpy as jnp
from jax import lax
from jax.experimental import pallas as pl
from jax.experimental.pallas import tpu as pltpu
from jax.sharding import PartitionSpec as P

MESH = pl.DeviceIdType.MESH
E = 1152
DI = 176
DT = 144
R = 32
TS = 8
ZS = 8
PS = 16
OUT = 36
XS = 4
H = 16
ROWS_I = 64
ROWS_T = 48
LEVELS = 32000.0
G = E // 128
f32 = jnp.float32
bf16 = jnp.bfloat16


def put(wire, k, x, n):
    m = jnp.max(jnp.abs(x), axis=1, keepdims=True)
    hi = jnp.floor(m)
    lo = jnp.floor((m - hi) * LEVELS) + 1.0
    q = jnp.round(x * (LEVELS / (hi + lo * (1.0 / LEVELS)))).astype(jnp.int32).astype(jnp.int16)
    for i in range(x.shape[0] // n):
        rows = slice(i * n, (i + 1) * n)
        for g in range(G):
            wire[k + i, g * n:(g + 1) * n, :] = q[rows, g * 128:(g + 1) * 128]
        diagonal = lax.broadcasted_iota(jnp.int32, (n, 128), 0) == lax.broadcasted_iota(jnp.int32, (n, 128), 1)
        his = jnp.sum(jnp.where(diagonal, hi[rows], 0.0), axis=0, keepdims=True)
        los = jnp.sum(jnp.where(diagonal, lo[rows], 0.0), axis=0, keepdims=True)
        row = lax.broadcasted_iota(jnp.int32, (16, 128), 0)
        wire[k + i, G * n:G * n + 16, :] = (
            jnp.where(row == 0, his, jnp.where(row == 1, los, 0.0)).astype(jnp.int32).astype(jnp.int16)
        )


def take(wire, k, n):
    code = wire[k, G * n:G * n + 16, :].astype(jnp.int32).astype(f32)
    top = code[0:1, :] + code[1:2, :] * (1.0 / LEVELS)
    diagonal = lax.broadcasted_iota(jnp.int32, (n, 128), 0) == lax.broadcasted_iota(jnp.int32, (n, 128), 1)
    step = jnp.sum(jnp.where(diagonal, top, 0.0), axis=1, keepdims=True) * (1.0 / LEVELS)
    return jnp.concatenate(
        [wire[k, g * n:(g + 1) * n, :].astype(jnp.int32).astype(f32) * step for g in range(G)], axis=1
    )


def unit_rows(values):
    norm = jnp.sqrt(jnp.sum(values * values, axis=1, keepdims=True) + 1e-06)
    return norm, values / norm


def back_rows(direct, norm, grad):
    inner = jnp.sum(direct * grad, axis=1, keepdims=True)
    return ((grad - direct * inner) / norm).astype(bf16)


def kernel(
    temp_hbm, bias_hbm, pair_hbm, fi_hbm, ft_hbm, wi_hbm, wt_hbm, out_i, out_t,
    temp_ref, bias_ref,
    fi_ref, ft_ref, wi_ref, wt_ref,
    part_i, part_t, a_i_out, a_i_in, a_t_out, a_t_in,
    dir_i, dir_t, norm_i, norm_t, unit_0, unit_1, all_t, pair_out, pair_in, target_ref,
    w_ref, gi_0, gi_1, gt, gt_sib, ca_out_0, ca_in_0, ca_out_1, ca_in_1,
    half_0, half_1, cb_out_0, cb_in_0, cb_out_1, cb_in_1, co_out_0, co_in_0, co_out_1, co_in_1, c_t_out, c_t_in,
    grad_i, grad_t, g_i, g_t, sib_i, sib_t, e_i_out, e_i_in, e_t_out, e_t_in,
    load_s, a_i_ss, a_i_rs, a_t_ss, a_t_rs, ba_ss, ba_rs, bb_ss, bb_rs, b_t_ss, b_t_rs, relay_ss, relay_rs,
    ca_ss, ca_rs, co_ss, co_rs, cb_ss, cb_rs, gt_ss, gt_rs, c_t_ss, c_t_rs, d_i_ss, d_i_rs, d_t_ss, d_t_rs,
    e_i_ss, e_i_rs, e_t_ss, e_t_rs, one_ss, one_rs,
):
    loads = [
        pltpu.make_async_copy(src, dst, load_s.at[k])
        for k, (src, dst) in enumerate((
            (ft_hbm, ft_ref), (wt_hbm, wt_ref), (fi_hbm, fi_ref), (wi_hbm, wi_ref), (pair_hbm, pair_out.at[0:1]),
            (temp_hbm, temp_ref), (bias_hbm, bias_ref),
        ))
    ]
    for load in loads:
        load.start()

    dp = lax.axis_index("dp")
    t = lax.axis_index("tensor")
    ylo = lax.div(dp, 16)
    z = lax.rem(lax.div(dp, 2), 8)
    c = lax.rem(dp, 2)
    oc = 1 - c
    yhi = lax.div(t, XS)
    x = lax.rem(t, XS)
    y = yhi * 2 + ylo
    q = ylo * ZS + z

    def device(ylo_, z_, c_, t_):
        return ((ylo_ * ZS + z_) * 2 + c_, t_)

    sibling = device(ylo, z, oc, t)
    across = device(1 - ylo, z, c, t)
    beyond = device(1 - ylo, z, c, (1 - yhi) * XS + x)

    def at_x(xx):
        return (dp, yhi * XS + xx)

    def at_y(yy):
        return device(lax.rem(yy, 2), z, c, lax.div(yy, 2) * XS + x)

    def column(k):
        return device(lax.div(k, ZS), lax.rem(k, ZS), c, t)

    def tensor_peer(j):
        dy, dx = ((1, 2), (0, 2), (1, 0), (1, 1), (1, 3), (0, 1), (0, 3))[j - 1]
        return lax.rem(yhi + dy, 2) * XS + lax.rem(x + dx, XS)

    def tensor_steps(body, carry):
        for j in range(1, TS):
            carry = body(j, carry)
        return carry

    z_order = (4, 3, 5, 2, 6, 1, 7, 0)

    def z_peer(j):
        return lax.rem(z + z_order[j - 1], ZS)

    def column_peer(j):
        n = j - 1
        return lax.rem(ylo + 1 - n % 2, 2) * ZS + lax.rem(z + z_order[n // 2], ZS)

    def unrolled(count, body, carry):
        for j in range(1, count):
            carry = body(j, carry)
        return carry

    def copy(src, dst, ssem, rsem, dev):
        return pltpu.make_async_remote_copy(
            src_ref=src, dst_ref=dst, send_sem=ssem, recv_sem=rsem, device_id=dev, device_id_type=MESH
        )

    barrier = pltpu.get_barrier_semaphore()

    def greet(dev):
        pl.semaphore_signal(barrier, inc=1, device_id=dev, device_id_type=MESH)

    def greet_tensor(j, _):
        greet((dp, tensor_peer(j)))
        return 0

    def greet_column(j, _):
        greet(column(column_peer(j)))
        return 0

    tensor_steps(greet_tensor, 0)
    unrolled(PS, greet_column, 0)
    greet(beyond)
    greet(sibling)

    def product(feat, weight):
        return lax.dot_general(
            feat[...], weight[...], (((0,), (0,)), ((), ())), preferred_element_type=f32
        ).reshape(TS, R, E)

    def a_encode(part, wire_out):
        for b in range(2):
            put(wire_out, b * XS, part[b * XS:(b + 1) * XS].reshape(XS * R, E), R)

    g_i[...] = jnp.zeros_like(g_i)
    g_t[...] = jnp.zeros_like(g_t)
    loads[0].wait()
    loads[1].wait()
    part_t[...] = product(ft_ref, wt_ref)
    a_encode(part_t, a_t_out)
    loads[4].wait()
    pair_out[...] = jnp.broadcast_to(pair_out[0:1, :], (8, 256))
    pl.semaphore_wait(barrier, (TS - 1) + (PS - 1) + 2)

    def a_copy(wire_out, wire_in, ss, rs, k, slot):
        return copy(wire_out.at[k], wire_in.at[slot], ss.at[k], rs.at[slot], (dp, k))

    def a_send(wire_out, wire_in, ss, rs):
        def step(j, _):
            a_copy(wire_out, wire_in, ss, rs, tensor_peer(j), t).start()
            return 0
        tensor_steps(step, 0)

    def a_take(part, wire_out, wire_in, ss, rs):
        def step(j, total):
            k = tensor_peer(TS - j)
            a_copy(wire_out, wire_in, ss, rs, k, k).wait_recv()
            return total + take(wire_in, k, R)
        return tensor_steps(step, part[t])

    a_send(a_t_out, a_t_in, a_t_ss, a_t_rs)
    pair_copy = copy(pair_out, pair_in, one_ss.at[0], one_rs.at[0], across)
    pair_copy.start()
    loads[2].wait()
    loads[3].wait()
    part_i[...] = product(fi_ref, wi_ref)
    a_encode(part_i, a_i_out)
    a_send(a_i_out, a_i_in, a_i_ss, a_i_rs)

    def local_target(pair):
        r = pair & 31
        tt = (pair >> 5) & 7
        cc = (pair >> 8) & 1
        zz = (pair >> 9) & 7
        yy = (pair >> 12) & 1
        here = jnp.logical_and(tt == t, yy == ylo)
        return jnp.where(here, (cc * ZS + zz) * R + r, -1)

    pair_copy.wait_recv()
    own = local_target(pair_out[0:1, :])
    other = local_target(pair_in[0:1, :])
    by_ylo = (jnp.where(ylo == 0, own, other), jnp.where(ylo == 0, other, own))
    for yy in range(XS):
        for xx in range(XS):
            lane = ((yy // 2) * XS + xx) * R
            s0, s1 = (yy * XS + xx) * H, (xx * XS + yy) * H + PS * H
            target_ref[0:1, s0:s0 + H] = by_ylo[yy % 2][:, lane:lane + H]
            target_ref[0:1, s1:s1 + H] = by_ylo[yy % 2][:, lane + H:lane + R]

    def b_t_copy(zz, slot):
        s = c * ZS + slot
        return copy(all_t.at[s], all_t.at[s], b_t_ss.at[zz], b_t_rs.at[slot], device(ylo, zz, c, t))

    def relay(cc, zz):
        s = cc * ZS + zz
        return copy(all_t.at[s], all_t.at[s], relay_ss.at[zz], relay_rs.at[zz], sibling)

    norm, direct = unit_rows(a_take(part_t, a_t_out, a_t_in, a_t_ss, a_t_rs))
    norm_t[...] = norm
    dir_t[...] = direct
    all_t[c * ZS + z] = direct.astype(bf16)

    def b_t_send(j, _):
        b_t_copy(z_peer(j), z).start()
        return 0

    unrolled(ZS, b_t_send, 0)
    relay(c, z).start()

    halves = ((unit_0, at_x, x, at_y, y), (unit_1, at_y, y, at_x, x))

    def ba_copy(h, k, slot):
        unit, first, me, second, line = halves[h]
        s = line * XS + slot
        return copy(unit.at[s], unit.at[s], ba_ss.at[h * XS + k], ba_rs.at[h * XS + slot], first(k))

    def bb_copy(h, i, k, slot):
        unit, first, me, second, line = halves[h]
        s = slot * XS + i
        return copy(unit.at[s], unit.at[s], bb_ss.at[h * PS + k * XS + i], bb_rs.at[h * PS + s], second(k))

    norm, direct = unit_rows(a_take(part_i, a_i_out, a_i_in, a_i_ss, a_i_rs))
    norm_i[...] = norm
    dir_i[...] = direct
    unit = direct.astype(bf16)
    unit_0[y * XS + x] = unit[0:H]
    unit_1[x * XS + y] = unit[H:R]
    steps = [(d, h) for d in (2, 1, 3) for h in (0, 1)]
    for d, h in steps:
        me = halves[h][2]
        ba_copy(h, lax.rem(me + d, XS), me).start()

    def bb_send(h, i):
        line = halves[h][4]
        for d in (2, 1, 3):
            bb_copy(h, i, lax.rem(line + d, XS), line).start()

    for h in (0, 1):
        bb_send(h, halves[h][2])
    for d in (1, 3, 2):
        for h in (0, 1):
            k = lax.rem(halves[h][2] + d, XS)
            ba_copy(h, k, k).wait_recv()
            bb_send(h, k)

    def b_t_take(j, _):
        zz = z_peer(j)
        b_t_copy(zz, zz).wait_recv()
        relay(c, zz).start()
        return 0

    unrolled(ZS, b_t_take, 0)

    def relay_take(zz, _):
        relay(oc, zz).wait_recv()
        return 0

    lax.fori_loop(0, ZS, relay_take, 0)
    for d, h in steps:
        k = lax.rem(halves[h][4] + d, XS)
        for i in range(XS):
            bb_copy(h, i, k, k).wait_recv()

    loads[5].wait()
    loads[6].wait()
    scale = 4.0 + temp_ref[0].astype(f32)
    shift = -0.5 * bias_ref[0].astype(f32)
    half = PS * H

    for h, unit in ((0, unit_0), (1, unit_1)):
        logits = scale * lax.dot_general(
            all_t[...].reshape(PS * R, E), unit[...].reshape(half, E), (((1,), (1,)), ((), ())),
            preferred_element_type=f32,
        ) + shift
        index = lax.broadcasted_iota(jnp.int32, (PS * R, half), 0)
        sign = jnp.where(index == target_ref[0:1, h * half:(h + 1) * half], f32(1.0), f32(-1.0))
        w_ref[:, h * half:(h + 1) * half] = (-scale * sign * jax.nn.sigmoid(-sign * logits)).astype(bf16)

    back = ((gi_0, ca_out_0, ca_in_0, half_0, cb_out_0, cb_in_0, co_out_0, co_in_0), (gi_1, ca_out_1, ca_in_1, half_1, cb_out_1, cb_in_1, co_out_1, co_in_1))

    def ca_copy(h, k, slot):
        out, into = back[h][1], back[h][2]
        return copy(
            out.at[k], into.at[slot], ca_ss.at[h * XS + k], ca_rs.at[h * XS + slot], halves[h][3](k)
        )

    def co_copy(h, k, slot):
        out, into = back[h][6], back[h][7]
        return copy(
            out.at[k], into.at[slot], co_ss.at[h * XS + k], co_rs.at[h * XS + slot], halves[h][3](k)
        )

    def others(gi, h, k):
        return jnp.concatenate([gi[k * XS + lax.rem(halves[h][2] + e, XS)] for e in (2, 1, 3)], axis=0)

    def cb_copy(h, n, k, slot):
        out, into = back[h][4], back[h][5]
        return copy(out.at[n], into.at[slot], cb_ss.at[h * XS + n], cb_rs.at[h * XS + slot], halves[h][1](k))

    for h in (0, 1):
        gi = back[h][0]
        gi[...] = lax.dot_general(
            w_ref[:, h * half:(h + 1) * half], all_t[...].reshape(PS * R, E), (((0,), (0,)), ((), ())),
            preferred_element_type=f32,
        ).reshape(PS, H, E)
        out, me, line = back[h][1], halves[h][2], halves[h][4]
        for d in (2, 1, 3):
            k = lax.rem(line + d, XS)
            put(out, k, others(gi, h, k), 3 * H)
            ca_copy(h, k, line).start()
    for h in (0, 1):
        gi, own, me, line = back[h][0], back[h][6], halves[h][2], halves[h][4]
        for d in (2, 1, 3):
            k = lax.rem(line + d, XS)
            put(own, k, gi[k * XS + me], H)
            co_copy(h, k, line).start()

    def tile_text(cc):
        w = w_ref.at[pl.ds(pl.multiple_of(cc * (ZS * R), ZS * R), ZS * R)]
        total = jnp.dot(w[:, 0:half], unit_0[...].reshape(half, E), preferred_element_type=f32)
        total = total + jnp.dot(w[:, half:], unit_1[...].reshape(half, E), preferred_element_type=f32)
        gt[pl.ds(cc * ZS, ZS)] = total.reshape(ZS, R, E)

    def gt_copy(b):
        return copy(
            gt.at[pl.ds(oc * ZS + b * 4, 4)], gt_sib.at[pl.ds(b * 4, 4)], gt_ss.at[b], gt_rs.at[b], sibling
        )

    def c_t_copy(zz, slot):
        return copy(c_t_out.at[zz], c_t_in.at[slot], c_t_ss.at[zz], c_t_rs.at[slot], device(ylo, zz, c, t))

    def tile_own(b, _):
        gt_copy(b).wait_recv()
        rows = gt[pl.ds(c * ZS + b * 4, 4)] + gt_sib[pl.ds(b * 4, 4)]
        gt[pl.ds(c * ZS + b * 4, 4)] = rows
        put(c_t_out, b * 4, rows.reshape(4 * R, E), R)
        for n in range(4):
            zz = b * 4 + n

            @pl.when(zz != z)
            def _(zz=zz):
                c_t_copy(zz, z).start()
        return 0

    tile_text(oc)
    gt_copy(0).start()
    gt_copy(1).start()
    tile_text(c)
    lax.fori_loop(0, 2, tile_own, 0)

    for h in (0, 1):
        gi, into, part, out = back[h][0], back[h][2], back[h][3], back[h][4]
        me, line = halves[h][2], halves[h][4]
        total = others(gi, h, line)
        for d in (1, 3, 2):
            k = lax.rem(line + d, XS)
            ca_copy(h, k, k).wait_recv()
            total = total + take(into, k, 3 * H)
        put(out, 0, total, H)
        for n, e in enumerate((2, 1, 3)):
            cb_copy(h, n, lax.rem(me + e, XS), me).start()
    for h in (0, 1):
        gi, own, part = back[h][0], back[h][7], back[h][3]
        me, line = halves[h][2], halves[h][4]
        total = gi[line * XS + me]
        for d in (1, 3, 2):
            k = lax.rem(line + d, XS)
            co_copy(h, k, k).wait_recv()
            total = total + take(own, k, H)
        part[...] = total

    def c_i_take(h):
        into, part, me = back[h][5], back[h][3], halves[h][2]
        total = part[...]
        for d in (1, 3, 2):
            k = lax.rem(me + d, XS)
            cb_copy(h, 0, k, k).wait_recv()
            total = total + take(into, k, H)
        return total

    def c_t_take(j, total):
        zz = z_peer(j)
        c_t_copy(zz, zz).wait_recv()
        return total + take(c_t_in, zz, R)

    def d_copy(grad, ss, rs, k, slot):
        return copy(grad.at[slot], grad.at[slot], ss.at[k], rs.at[slot], (dp, k))

    def d_send(grad, ss, rs):
        def step(j, _):
            d_copy(grad, ss, rs, tensor_peer(j), t).start()
            return 0
        tensor_steps(step, 0)

    def d_take(grad, ss, rs):
        def step(j, _):
            k = tensor_peer(TS - j)
            d_copy(grad, ss, rs, k, k).wait_recv()
            return 0
        tensor_steps(step, 0)

    total = jnp.concatenate([c_i_take(0), c_i_take(1)], axis=0)
    grad_i[t] = back_rows(dir_i[...], norm_i[...], total)
    d_send(grad_i, d_i_ss, d_i_rs)
    total = unrolled(ZS, c_t_take, gt[c * ZS + z])
    grad_t[t] = back_rows(dir_t[...], norm_t[...], total)
    d_send(grad_t, d_t_ss, d_t_rs)

    def weight_grad(grad, feat, packed, fold):
        g = lax.dot_general(
            grad[...].reshape(TS * R, E), feat[...], (((0,), (1,)), ((), ())), preferred_element_type=f32
        )
        rest, rows = g.shape[1] - 128, OUT // fold
        for k in range(2 * PS):
            packed[k % 2, k // 2, 0:OUT, :] = g[k * OUT:(k + 1) * OUT, 0:128]
            for n in range(fold):
                packed[k % 2, k // 2, OUT:OUT + rows, n * rest:(n + 1) * rest] = (
                    g[k * OUT + n * rows:k * OUT + (n + 1) * rows, 128:]
                )

    def e_copy(out, into, ss, rs, k, slot):
        return copy(out.at[k], into.at[slot], ss.at[k], rs.at[slot], column(k))

    def e_send(packed, sib, out, into, ss, rs):
        def step(j, _):
            k = column_peer(j)
            out[k] = (packed[c, k] + sib[k]).astype(bf16)
            e_copy(out, into, ss, rs, k, q).start()
            return 0
        unrolled(PS, step, 0)

    def e_take(packed, sib, out, into, ss, rs):
        def step(j, total):
            k = column_peer(j)
            e_copy(out, into, ss, rs, k, k).wait_recv()
            return total + into[k].astype(f32)
        return unrolled(PS, step, packed[c, q] + sib[q])

    e_i = (g_i, sib_i, e_i_out, e_i_in, e_i_ss, e_i_rs)
    e_t = (g_t, sib_t, e_t_out, e_t_in, e_t_ss, e_t_rs)
    d_take(grad_i, d_i_ss, d_i_rs)
    weight_grad(grad_i, fi_ref, g_i, 2)
    g_i_copy = copy(g_i.at[oc], sib_i, one_ss.at[1], one_rs.at[1], sibling)
    g_i_copy.start()
    g_i_copy.wait_recv()
    e_send(*e_i)
    d_take(grad_t, d_t_ss, d_t_rs)
    weight_grad(grad_t, ft_ref, g_t, 3)
    g_t_copy = copy(g_t.at[oc], sib_t, one_ss.at[2], one_rs.at[2], sibling)
    g_t_copy.start()
    g_t_copy.wait_recv()
    e_send(*e_t)

    def unpack(total, out, width, fold):
        rest, rows = width - 128, OUT // fold
        out[:, 0:128] = total[0:OUT, :]
        for n in range(fold):
            out[n * rows:(n + 1) * rows, 128:width] = (
                total[OUT:OUT + rows, n * rest:(n + 1) * rest]
            )

    def sent_tensor(j, _):
        k = tensor_peer(j)
        a_copy(a_t_out, a_t_in, a_t_ss, a_t_rs, k, t).wait_send()
        a_copy(a_i_out, a_i_in, a_i_ss, a_i_rs, k, t).wait_send()
        d_copy(grad_t, d_t_ss, d_t_rs, k, t).wait_send()
        d_copy(grad_i, d_i_ss, d_i_rs, k, t).wait_send()
        return 0

    def sent_z(j, _):
        zz = z_peer(j)
        b_t_copy(zz, z).wait_send()
        c_t_copy(zz, z).wait_send()
        return 0

    def sent_relay(zz, _):
        relay(c, zz).wait_send()
        return 0

    tensor_steps(sent_tensor, 0)
    unrolled(ZS, sent_z, 0)
    lax.fori_loop(0, ZS, sent_relay, 0)
    for d, h in steps:
        me, line = halves[h][2], halves[h][4]
        ba_copy(h, lax.rem(me + d, XS), me).wait_send()
        ca_copy(h, lax.rem(line + d, XS), line).wait_send()
        co_copy(h, lax.rem(line + d, XS), line).wait_send()
        for i in range(XS):
            bb_copy(h, i, lax.rem(line + d, XS), line).wait_send()
    for h in (0, 1):
        for n, e in enumerate((2, 1, 3)):
            cb_copy(h, n, lax.rem(halves[h][2] + e, XS), halves[h][2]).wait_send()
    for b in (0, 1):
        gt_copy(b).wait_send()
    pair_copy.wait_send()

    unpack(e_take(*e_i), out_i, DI, 2)
    unpack(e_take(*e_t), out_t, DT, 3)

    def sent_column(j, _):
        k = column_peer(j)
        e_copy(e_i_out, e_i_in, e_i_ss, e_i_rs, k, q).wait_send()
        e_copy(e_t_out, e_t_in, e_t_ss, e_t_rs, k, q).wait_send()
        return 0

    unrolled(PS, sent_column, 0)
    for sent in (g_i_copy, g_t_copy):
        sent.wait_send()


def on_device(image_features, text_features, image_weight, text_weight, image_pair, temp_index, bias_index):
    hbm = pl.BlockSpec(memory_space=pltpu.HBM)
    dma = pltpu.SemaphoreType.DMA
    V = pltpu.VMEM
    i16, i32 = jnp.int16, jnp.int32
    wire = lambda count, rows: V((count, G * rows + 16, 128), i16)
    scratch = (
        [pltpu.SMEM((1,), i32)] * 2
        + [V((DI, 256), bf16), V((DT, 256), bf16), V((DI, E), bf16), V((DT, E), bf16)]
        + [V((TS, R, E), f32)] * 2 + [wire(TS, R)] * 4
        + [V((R, E), f32)] * 2 + [V((R, 1), f32)] * 2
        + [V((PS, H, E), bf16)] * 2 + [V((PS, R, E), bf16)]
        + [V((8, 256), i32)] * 2 + [V((8, PS * R), i32)]
        + [V((PS * R, PS * R), bf16)] + [V((PS, H, E), f32)] * 2 + [V((PS, R, E), f32), V((ZS, R, E), f32)]
        + [wire(XS, 3 * H)] * 4 + [V((H, E), f32)] * 2 + [wire(XS, H)] * 8 + [wire(ZS, R)] * 2
        + [V((TS, R, E), bf16)] * 2
        + [V((2, PS, ROWS_I, 128), f32), V((2, PS, ROWS_T, 128), f32)]
        + [V((PS, ROWS_I, 128), f32), V((PS, ROWS_T, 128), f32)]
        + [V((PS, ROWS_I, 128), bf16)] * 2 + [V((PS, ROWS_T, 128), bf16)] * 2
        + [dma((7,))] + [dma((TS,))] * 4 + [dma((2 * XS,))] * 2 + [dma((2 * PS,))] * 2 + [dma((ZS,))] * 4
        + [dma((2 * XS,))] * 6 + [dma((2,))] * 2 + [dma((ZS,))] * 2
        + [dma((TS,))] * 4 + [dma((PS,))] * 4 + [dma((3,))] * 2
    )
    grad_image, grad_text = pl.pallas_call(
        kernel,
        out_shape=[jax.ShapeDtypeStruct((OUT, DI), f32), jax.ShapeDtypeStruct((OUT, DT), f32)],
        in_specs=[hbm] * 7,
        out_specs=[pl.BlockSpec(memory_space=pltpu.VMEM)] * 2,
        scratch_shapes=scratch,
        compiler_params=pltpu.CompilerParams(
            collective_id=0, has_side_effects=True, vmem_limit_bytes=56430000
        ),
        name="pair_loss_grads",
    )(
        temp_index.reshape(1), bias_index.reshape(1), image_pair.reshape(1, 256),
        image_features.T, text_features.T, image_weight, text_weight,
    )
    return grad_image.T, grad_text.T


def solution(mesh):
    return jax.shard_map(
        on_device,
        mesh=mesh,
        in_specs=(P("dp", "tensor"), P("dp", "tensor"), P("tensor", None), P("tensor", None), P("dp"), P(), P()),
        out_specs=(P("tensor", "dp"), P("tensor", "dp")),
        check_vma=False,
    )
```
